512 devices in a mesh: tm: 16 (over y, core), grp: 32 (over z, x).
Axes of the slice: x: 4, y: 8, z: 8, core: 2. Of those that a mesh axis runs over, the one named last changes fastest.
Arguments:
- locations: float32 [16, 2, 65536], P(None, None, ('tm', 'grp')), may hold values from 0 to 32
- times: float32 [65536], P(('tm', 'grp')), may hold values from 0 to 65536, as said below
- background: float32 [65536], P(('tm', 'grp')), may hold values from 0.0005 to 0.005
- weights: float32 [16, 65536], P(None, ('tm', 'grp')), may hold values from -6 to 6
- window_start: int32 [1024], P(('tm', 'grp')), may hold values from 1 to 127, as said below
- live: int32 [512], P(('tm', 'grp')), may hold values from 1 to 128, 49152 in all
Outputs:
- grad: float32 [16, 2, 65536], P(None, None, ('tm', 'grp'))
- log_intensity: float32 [16, 65536], P(None, ('tm', 'grp'))
The draws below stay inside these ranges and needn't reach their ends.
Inputs may be any that keep to these rules, and one draw needn't show every extreme that they name: `window_start`: for block b of children, with k = b mod 64, the value lies in k + 1 to 64 + k; the first block of every shard has 1, the last 127. `times`: times_i - i lies in 0 to 1. Some device holds 128 live events in every draw.
All inputs are finite; a program needn't handle non-finite values.
Results may differ from the reference program's by a relative error of at most 0.0003.
Values sent between devices are 32-bit elements; how exact they have to be, the bound alone decides.
No kernel may reach another device: no remote copies, remote signals or barrier semaphores. Data moves between devices by JAX's collectives and lax.ppermute only.
A program may use at most 192 MiB of HBM per device.

```python
import math
import jax
import jax.numpy as jnp
import numpy as np
from jax import lax

CHAINS = 16
E_DEV = 128
BLK = 64
E_SHARD = 4096
EVENTS = 65536
NBS = 64
BLOCKS = 1024
N_TM = 16
N_GRP = 32


def draw_times(key, part):
    key = jax.random.fold_in(key, 5)
    jitter = jax.random.uniform(key, (EVENTS,), jnp.float32)
    return jnp.arange(EVENTS, dtype=jnp.int32).astype(jnp.float32) + jitter


def draw_window_start(key, part):
    key = jax.random.fold_in(key, 11)
    within = jnp.arange(BLOCKS, dtype=jnp.int32) % NBS
    reach = jax.random.randint(key, (BLOCKS,), 0, NBS, dtype=jnp.int32)
    reach = jnp.where(within == 0, NBS - 1, reach)
    reach = jnp.where(within == NBS - 1, 0, reach)
    return (NBS + within - reach).astype(jnp.int32)


def steps_of(key, extent, shards, low, high):
    level, own = 1.0, jax.random.fold_in(key, 6)
    for dim, parts in shards:
        heights = jnp.exp(jax.random.uniform(jax.random.fold_in(own, dim), (parts,), jnp.float32, low / len(shards), high / len(shards)))
        level = level * jnp.repeat(heights, extent[dim] // parts).reshape([-1 if axis == dim else 1 for axis in range(len(extent))])
    return level


def split_up(number_of, total, bound, lean):
    loads = [(1 << 20) // math.isqrt(grade ** lean) + 1 for grade in range(2, number_of + 1)]
    rest, holding = total - bound - (number_of - 1), [1] * (number_of - 1)
    while rest > 0:
        candidates = [i for i in range(number_of - 1) if holding[i] < bound]
        mass, left = sum([loads[i] for i in candidates]), rest
        for i in candidates:
            more = min(bound - holding[i], max(1, left * loads[i] // mass), rest)
            holding[i] = holding[i] + more
            rest = rest - more
    return np.array([bound] + holding)


def uneven(own_key, count, total, most, skew):
    if count == 2:
        one = jax.random.randint(own_key, (), max(1, total - most), min(most, total - 1) + 1)
        return jnp.stack([one, total - one])
    tallies = jnp.asarray(split_up(count, total, most, skew), jnp.int32)
    twos = (count - 1) // 2
    giver, receiver = tallies[1:1 + 2 * twos:2], tallies[2:2 + 2 * twos:2]
    room = jnp.minimum(giver - 1, most - receiver)
    moved = jax.random.randint(jax.random.fold_in(own_key, 1), (twos,), 0, 1 << 20) % (room + 1)
    tallies = tallies.at[1:1 + 2 * twos:2].set(giver - moved).at[2:2 + 2 * twos:2].set(receiver + moved)
    return tallies[jax.random.permutation(jax.random.fold_in(own_key, 2), count)]


def noise(rng, dims, deviation, most, pieces=(), held_as=jnp.bfloat16):
    values = jax.random.normal(rng, dims, jnp.float32) * deviation
    if len(pieces) > 0:
        values = steps_of(rng, dims, pieces, -0.22, 0.18) * values
    return jnp.clip(values, min=-most, max=most).astype(held_as)


def setup_inputs(seed: int = 0) -> dict:
    key_of = jax.random.split(jax.random.key(seed), 7)
    return {
        "locations": jnp.clip(32.0 * jax.random.uniform(key_of[0], (CHAINS, 2, EVENTS), jnp.float32) ** steps_of(key_of[0], (CHAINS, 2, EVENTS), ((2, 512),), -0.2, 0.2), 0.0, 32.0),
        "times": draw_times(jax.random.fold_in(key_of[6], 71), 0),
        "background": jnp.clip(jnp.exp(math.log(0.005) - 2.30258502 * jax.random.uniform(key_of[2], (EVENTS,), jnp.float32) ** steps_of(key_of[2], (EVENTS,), ((0, 512),), -0.2, 0.2)), 0.0005, 0.005),
        "weights": noise(key_of[3], (CHAINS, EVENTS), 1.0, 6.0, ((1, 512),), jnp.float32),
        "window_start": draw_window_start(jax.random.fold_in(key_of[6], 71), 0),
        "live": uneven(key_of[5], N_TM * N_GRP, N_TM * N_GRP * E_DEV * 3 // 4, E_DEV, 2).astype(jnp.int32),
    }


offspring = 0.8
fast_rate = 0.125
slow_rate = 0.0009765625

def time_kernel(delta, allowed):
    safe_delta = jnp.where(allowed, delta, 0.0)
    value = offspring * (0.5 * fast_rate * jnp.exp(-fast_rate * safe_delta) + 0.5 * slow_rate * jnp.exp(-slow_rate * safe_delta)) / (2.0 * math.pi)
    return jnp.where(allowed, value, 0.0)

def reference(locations, times, background, weights, window_start, live):
    slot_ids = jnp.arange(EVENTS, dtype=jnp.int32)
    alive_mask = (slot_ids % E_DEV < jnp.repeat(live, E_DEV)).astype(jnp.float32)
    window_len = E_SHARD + BLK
    times_pad = jnp.concatenate([jnp.zeros((E_SHARD,), times.dtype), times])
    alive_pad = jnp.concatenate([jnp.zeros((E_SHARD,), alive_mask.dtype), alive_mask])
    back_blocks = background.reshape(BLOCKS, BLK)
    alive_blocks = alive_mask.reshape(BLOCKS, BLK)
    weight_blocks = weights.reshape(CHAINS, BLOCKS, BLK).transpose(1, 0, 2)
    block_ids = jnp.arange(BLOCKS, dtype=jnp.int32)
    parent_idx = jnp.arange(window_len, dtype=jnp.int32)
    child_idx = jnp.arange(BLK, dtype=jnp.int32)

    def objective(locs_pad):

        @jax.checkpoint
        def block_term(inputs):
            block_id, start_blk, back_blk, alive_blk, weight_blk = inputs
            parent_locs = lax.dynamic_slice_in_dim(locs_pad, block_id * BLK, window_len, 2)
            child_locs = lax.dynamic_slice_in_dim(locs_pad, E_SHARD + block_id * BLK, BLK, 2)
            parent_times = lax.dynamic_slice_in_dim(times_pad, block_id * BLK, window_len, 0)
            child_times = lax.dynamic_slice_in_dim(times_pad, E_SHARD + block_id * BLK, BLK, 0)
            parent_alive = lax.dynamic_slice_in_dim(alive_pad, block_id * BLK, window_len, 0)
            allowed = (parent_idx[None, :] < E_SHARD + child_idx[:, None]) & (block_id % NBS * BLK + parent_idx[None, :] >= start_blk * BLK) & (parent_alive[None, :] > 0)
            temporal = time_kernel(child_times[:, None] - parent_times[None, :], allowed)
            diff_x = child_locs[:, 0, :, None] - parent_locs[:, 0, None, :]
            diff_y = child_locs[:, 1, :, None] - parent_locs[:, 1, None, :]
            kernel = temporal[None] * jnp.exp(-0.5 * (diff_x * diff_x + diff_y * diff_y))
            intensity = back_blk[None, :] + lax.optimization_barrier(jnp.sum(kernel, axis=2))
            logs_blk = alive_blk[None, :] * jnp.log(intensity)
            return (jnp.sum(weight_blk * logs_blk), logs_blk)
        terms, logs_all = lax.map(block_term, (block_ids, window_start, back_blocks, alive_blocks, weight_blocks))
        return (jnp.sum(terms), logs_all)
    locs_pad = jnp.concatenate([jnp.zeros((CHAINS, 2, E_SHARD), locations.dtype), locations], axis=2)
    grads, logs_all = jax.grad(objective, has_aux=True)(locs_pad)
    grad = grads[:, :, E_SHARD:]
    log_intensity = logs_all.transpose(1, 0, 2).reshape(CHAINS, EVENTS)
    return (grad, log_intensity)
```

```python
import math

import jax
import jax.numpy as jnp
from jax import lax
from jax.experimental import pallas as pl
from jax.experimental.pallas import tpu as pltpu
from jax.sharding import PartitionSpec as P

offspring = 0.8
fast_rate = 0.125
slow_rate = 0.0009765625

CH = 16
LANES = 128
TILES = 32
ROWS = 40
GROUP = 32
QUAD = 4
DEAD = -1e30

SCALE = math.sqrt(0.5 / math.log(2.0))
UNSCALE = 1.0 / SCALE
LOG2E = 1.0 / math.log(2.0)
LOG2_SLOW = math.log2(offspring * 0.5 * slow_rate / (2.0 * math.pi))


def from_behind(value, axis, by):
    count = lax.axis_size(axis)
    pairs = [(i, i + by) for i in range(count) if 0 <= i + by < count]
    return lax.ppermute(value, axis, pairs)


def log2_time_kernel(delta):
    fast = (fast_rate / slow_rate) * jnp.exp2(delta * (-(fast_rate - slow_rate) * LOG2E))
    return (LOG2_SLOW - delta * (slow_rate * LOG2E)) + jnp.log(1.0 + fast) * LOG2E


def pair_kernel(
    info, prev, own, weights, back, alive, child_side, logs, part_prev, part_own,
    log_t, child_b, kern, sums, ratio_b, total
):
    me = info[0]
    first_tile = (info[1] // LANES) // 2, (info[2] // LANES) // 2
    lane = lax.broadcasted_iota(jnp.int32, (CH, LANES), 1)
    mine = own[me]
    xs, ys = mine[0:CH], mine[CH : 2 * CH]
    pair_of_tiles = ((prev, 0), (own, TILES))

    for child in range(LANES):
        child_b[child] = jnp.broadcast_to(mine[0 : 2 * CH, child : child + 1], (2 * CH, LANES))

    row = lax.broadcasted_iota(jnp.int32, (LANES, LANES), 0)
    col = lax.broadcasted_iota(jnp.int32, (LANES, LANES), 1)
    child_time = jnp.transpose(jnp.broadcast_to(info_time(mine, alive), (LANES, LANES)))
    child_pos = (TILES + me) * LANES + row
    low = jnp.where(row < LANES // 2, info[1], info[2])
    span = child_pos - low

    def time_tiles(ref, offset):
        def body(step, carry):
            for u in range(2):
                q = 2 * step + u
                parent_time = ref[q, 2 * CH : 2 * CH + 1, :]
                value = log2_time_kernel(jnp.maximum(child_time - parent_time, 0.0))
                pos = (offset + q) * LANES + col
                ok = (pos >= low) & (pos < child_pos)
                log_t[offset + q] = jnp.where(ok, value, DEAD)
            return carry

        return body

    first = jnp.minimum(first_tile[0], first_tile[1])
    last_own = (me + 2) // 2
    lax.fori_loop(jnp.minimum(first, TILES // 2), TILES // 2, time_tiles(prev, 0), 0)
    lax.fori_loop(jnp.maximum(first - TILES // 2, 0), last_own, time_tiles(own, TILES), 0)

    def clear(q, carry):
        total[q] = jnp.zeros((3 * CH, LANES), jnp.float32)
        return carry

    lax.fori_loop(0, 2 * TILES, clear, 0)

    for group in range(LANES // GROUP):
        start = first_tile[group * GROUP // (LANES // 2)]
        prev_start = jnp.minimum(start, TILES // 2)
        own_start = jnp.maximum(start - TILES // 2, 0)

        def quad_sums(quad, carry):
            base = group * GROUP + quad * QUAD
            cx = [child_b[base + i, 0:CH] for i in range(QUAD)]
            cy = [child_b[base + i, CH : 2 * CH] for i in range(QUAD)]

            def tiles(ref, offset):
                def body(step, acc):
                    acc = list(acc)
                    for u in range(2):
                        q = 2 * step + u
                        px = ref[q, 0:CH]
                        py = ref[q, CH : 2 * CH]
                        for i in range(QUAD):
                            dx = px - cx[i]
                            dy = py - cy[i]
                            lt = log_t[offset + q, pl.ds(base + i, 1), :]
                            k = jnp.exp2((lt - dx * dx) - dy * dy)
                            kern[quad * QUAD + i, offset + q] = k
                            acc[3 * i] = acc[3 * i] + k
                            acc[3 * i + 1] = acc[3 * i + 1] + k * dx
                            acc[3 * i + 2] = acc[3 * i + 2] + k * dy
                    return tuple(acc)

                return body

            acc = tuple(jnp.zeros((CH, LANES), jnp.float32) for _ in range(3 * QUAD))
            acc = lax.fori_loop(prev_start, TILES // 2, tiles(prev, 0), acc)
            acc = lax.fori_loop(own_start, last_own, tiles(own, TILES), acc)
            for i in range(QUAD):
                for j in range(3):
                    sums[quad * QUAD + i, j * CH : (j + 1) * CH] = acc[3 * i + j]
            return carry

        lax.fori_loop(0, GROUP // QUAD, quad_sums, 0)

        collected = [jnp.zeros((CH, LANES), jnp.float32) for _ in range(3)]
        for i in range(GROUP):
            summed = jnp.sum(sums[i], axis=1, keepdims=True)
            for j in range(3):
                collected[j] = jnp.where(
                    lane == group * GROUP + i, summed[j * CH : (j + 1) * CH], collected[j]
                )
        intensity = back[...] + collected[0]
        ratio = weights[...] * alive[...] / intensity
        log_here = alive[...] * jnp.log(intensity)
        ratio_x, ratio_y = ratio * xs, ratio * ys
        side_x, side_y = ratio * collected[1] * UNSCALE, ratio * collected[2] * UNSCALE
        here = (lane >= group * GROUP) & (lane < (group + 1) * GROUP)
        logs[...] = jnp.where(here, log_here, logs[...])
        child_side[0:CH] = jnp.where(here, side_x, child_side[0:CH])
        child_side[CH : 2 * CH] = jnp.where(here, side_y, child_side[CH : 2 * CH])
        spread = jnp.concatenate([ratio, ratio_x, ratio_y], axis=0)
        for i in range(GROUP):
            at = group * GROUP + i
            ratio_b[i] = jnp.broadcast_to(spread[:, at : at + 1], (3 * CH, LANES))

        def quad_push(quad, carry):
            terms = [ratio_b[quad * QUAD + i] for i in range(QUAD)]

            def tiles(offset):
                def body(step, inner):
                    for u in range(2):
                        q = offset + 2 * step + u
                        ks = [kern[quad * QUAD + i, q] for i in range(QUAD)]
                        for j in range(3):
                            add = [ks[i] * terms[i][j * CH : (j + 1) * CH] for i in range(QUAD)]
                            at = slice(j * CH, (j + 1) * CH)
                            total[q, at] = total[q, at] + ((add[0] + add[1]) + (add[2] + add[3]))
                    return inner

                return body

            lax.fori_loop(prev_start, TILES // 2, tiles(0), 0)
            lax.fori_loop(own_start, last_own, tiles(TILES), 0)
            return carry

        lax.fori_loop(0, GROUP // QUAD, quad_push, 0)

    for ref, out, offset in ((prev, part_prev, 0), (own, part_own, TILES)):

        def finish(q, carry, ref=ref, out=out, offset=offset):
            weight = total[offset + q, 0:CH]
            for j in range(2):
                at = slice(j * CH, (j + 1) * CH)
                pulled = total[offset + q, (j + 1) * CH : (j + 2) * CH]
                out[q, at] = (pulled - ref[q, at] * weight) * UNSCALE
            return carry

        lax.fori_loop(0, TILES, finish, 0)


def info_time(mine, alive):
    return mine[2 * CH + 1 : 2 * CH + 2]


def pairs(info, prev, own, weights, back, alive):
    f32 = jnp.float32
    vmem = pl.BlockSpec(memory_space=pltpu.VMEM)
    return pl.pallas_call(
        pair_kernel,
        out_shape=(
            jax.ShapeDtypeStruct((2 * CH, LANES), f32),
            jax.ShapeDtypeStruct((CH, LANES), f32),
            jax.ShapeDtypeStruct((TILES, 2 * CH, LANES), f32),
            jax.ShapeDtypeStruct((TILES, 2 * CH, LANES), f32),
        ),
        in_specs=[pl.BlockSpec(memory_space=pltpu.SMEM)] + [vmem] * 5,
        out_specs=(vmem,) * 4,
        scratch_shapes=[
            pltpu.VMEM((2 * TILES, LANES, LANES), f32),
            pltpu.VMEM((LANES, 2 * CH, LANES), f32),
            pltpu.VMEM((GROUP, 2 * TILES, CH, LANES), f32),
            pltpu.VMEM((GROUP, 3 * CH, LANES), f32),
            pltpu.VMEM((GROUP, 3 * CH, LANES), f32),
            pltpu.VMEM((2 * TILES, 3 * CH, LANES), f32),
        ],
        compiler_params=pltpu.CompilerParams(vmem_limit_bytes=48 * 2**20),
    )(info, prev, own, weights, back, alive)


def per_device(locations, times, background, weights, window_start, live):
    slot_ids = jnp.arange(LANES, dtype=jnp.int32)
    alive = slot_ids < live[0]
    chunk = jnp.concatenate(
        [
            locations[:, 0, :] * SCALE,
            locations[:, 1, :] * SCALE,
            jnp.where(alive, times, DEAD)[None],
            times[None],
            jnp.zeros((ROWS - 2 * CH - 2, LANES), jnp.float32),
        ]
    )
    own = lax.all_to_all(jnp.broadcast_to(chunk[None], (TILES, ROWS, LANES)), "grp", 0, 0)
    prev = from_behind(own, "tm", 1)
    least = jnp.where(lax.axis_index("tm") == 0, TILES * LANES, 0)
    limit = jnp.maximum(window_start * (LANES // 2), least)
    info = jnp.concatenate([lax.axis_index("grp").astype(jnp.int32)[None], limit])
    child_side, log_intensity, part_prev, part_own = pairs(
        info, prev, own, weights, background[None], alive.astype(jnp.float32)[None]
    )
    part = part_own + from_behind(part_prev, "tm", -1)
    parent_side = jnp.sum(lax.all_to_all(part, "grp", 0, 0), axis=0)
    grad = (child_side + parent_side).reshape(2, CH, LANES).transpose(1, 0, 2)
    return (grad, log_intensity)


def solution(mesh):
    return jax.shard_map(
        per_device,
        mesh=mesh,
        in_specs=(
            P(None, None, ("tm", "grp")),
            P(("tm", "grp")),
            P(("tm", "grp")),
            P(None, ("tm", "grp")),
            P(("tm", "grp")),
            P(("tm", "grp")),
        ),
        out_specs=(P(None, None, ("tm", "grp")), P(None, ("tm", "grp"))),
        check_vma=False,
    )
```

```python
import math

import jax
import jax.numpy as jnp
from jax import lax
from jax.experimental import pallas as pl
from jax.experimental.pallas import tpu as pltpu
from jax.sharding import PartitionSpec as P

offspring = 0.8
fast_rate = 0.125
slow_rate = 0.0009765625

CH = 16
LANES = 128
TILES = 32
BLK = 64
QUAD = 4
SLOTS = 32
DEAD = -1e30

DEAD_ROW, TIME_ROW, BACK_ROW, ALIVE_ROW, META_ROW = range(2 * CH, 2 * CH + 5)
W_ROW = 40
ROWS = W_ROW + CH
TILE, LANE0, LOW = 1, 1 + SLOTS, 1 + 2 * SLOTS

SCALE = math.sqrt(0.5 / math.log(2.0))
UNSCALE = 1.0 / SCALE
LOG2E = 1.0 / math.log(2.0)
LOG2_SLOW = math.log2(offspring * 0.5 * slow_rate / (2.0 * math.pi))


def from_behind(value, axis, by):
    count = lax.axis_size(axis)
    pairs = [(i, i + by) for i in range(count) if 0 <= i + by < count]
    return lax.ppermute(value, axis, pairs)


def log2_time_kernel(delta):
    fast = (fast_rate / slow_rate) * jnp.exp2(delta * (-(fast_rate - slow_rate) * LOG2E))
    return (LOG2_SLOW - delta * (slow_rate * LOG2E)) + jnp.log(1.0 + fast) * LOG2E


def pair_kernel(
    info, prev, own, part_prev, part_own, log_t, child_b, kern, sums, ratio_b, total, times_q, child_t
):
    count = info[0]
    lane = lax.broadcasted_iota(jnp.int32, (1, LANES), 1)

    packed = jnp.zeros((ROWS, LANES), jnp.float32)
    for s in range(SLOTS):
        shift = lax.rem(QUAD * s + LANES - info[LANE0 + s], LANES)
        moved = pltpu.roll(own[info[TILE + s]], shift, 1)
        packed = jnp.where((lane >= QUAD * s) & (lane < QUAD * (s + 1)), moved, packed)
    xs, ys, weights = packed[0:CH], packed[CH : 2 * CH], packed[W_ROW : W_ROW + CH]
    back, alive = packed[BACK_ROW : BACK_ROW + 1], packed[ALIVE_ROW : ALIVE_ROW + 1]
    for child in range(LANES):
        child_b[child] = jnp.broadcast_to(packed[0 : 2 * CH, child : child + 1], (2 * CH, LANES))
    child_t[...] = jnp.transpose(jnp.broadcast_to(packed[TIME_ROW : TIME_ROW + 1], (LANES, LANES)))
    for q in range(TILES):
        times_q[q : q + 1] = prev[q, DEAD_ROW : DEAD_ROW + 1]
        times_q[TILES + q : TILES + q + 1] = own[q, DEAD_ROW : DEAD_ROW + 1]

    pos = lax.broadcasted_iota(jnp.int32, (2 * TILES, LANES), 0) * LANES
    pos = pos + lax.broadcasted_iota(jnp.int32, (2 * TILES, LANES), 1)

    def time_rows(s, carry):
        low = info[LOW + s]
        for i in range(QUAD):
            at = QUAD * s + i
            delta = jnp.maximum(child_t[pl.ds(at, 1)] - times_q[...], 0.0)
            child_pos = (TILES + info[TILE + s]) * LANES + info[LANE0 + s] + i
            ok = (pos >= low) & (pos < child_pos)
            log_t[at] = jnp.where(ok, log2_time_kernel(delta), DEAD)
        return carry

    lax.fori_loop(0, count, time_rows, 0)

    def clear(q, carry):
        total[q] = jnp.zeros((3 * CH, LANES), jnp.float32)
        return carry

    lax.fori_loop(0, 2 * TILES, clear, 0)

    half = TILES // 2

    def steps_of(s):
        start = info[LOW + s] // (2 * LANES)
        return start, half + (info[TILE + s] + 2) // 2

    def slot_sums(s, carry):
        start, end = steps_of(s)
        cx = [child_b[QUAD * s + i, 0:CH] for i in range(QUAD)]
        cy = [child_b[QUAD * s + i, CH : 2 * CH] for i in range(QUAD)]

        def tiles(ref, offset):
            def body(step, acc):
                acc = list(acc)
                for u in range(2):
                    q = 2 * step + u
                    px = ref[q - offset, 0:CH]
                    py = ref[q - offset, CH : 2 * CH]
                    for i in range(QUAD):
                        dx = px - cx[i]
                        dy = py - cy[i]
                        lt = log_t[QUAD * s + i, pl.ds(q, 1), :]
                        k = jnp.exp2((lt - dx * dx) - dy * dy)
                        kern[QUAD * s + i, q - 2 * start] = k
                        acc[3 * i] = acc[3 * i] + k
                        acc[3 * i + 1] = acc[3 * i + 1] + k * dx
                        acc[3 * i + 2] = acc[3 * i + 2] + k * dy
                return tuple(acc)

            return body

        acc = tuple(jnp.zeros((CH, LANES), jnp.float32) for _ in range(3 * QUAD))
        acc = lax.fori_loop(jnp.minimum(start, half), half, tiles(prev, 0), acc)
        acc = lax.fori_loop(jnp.maximum(start, half), end, tiles(own, TILES), acc)
        for i in range(QUAD):
            for j in range(3):
                sums[QUAD * s + i, j * CH : (j + 1) * CH] = acc[3 * i + j]
        return carry

    lax.fori_loop(0, count, slot_sums, 0)

    collected = [jnp.zeros((CH, LANES), jnp.float32) for _ in range(3)]
    for child in range(LANES):
        summed = jnp.sum(sums[child], axis=1, keepdims=True)
        for j in range(3):
            collected[j] = jnp.where(lane == child, summed[j * CH : (j + 1) * CH], collected[j])
    intensity = back + collected[0]
    ratio = weights / intensity
    spread = jnp.concatenate([ratio, ratio * xs, ratio * ys], axis=0)
    for child in range(LANES):
        ratio_b[child] = jnp.broadcast_to(spread[:, child : child + 1], (3 * CH, LANES))
    result = jnp.concatenate(
        [
            ratio * collected[1] * UNSCALE,
            ratio * collected[2] * UNSCALE,
            jnp.where(alive > 0.0, jnp.log(intensity), 0.0),
        ],
        axis=0,
    )

    def slot_push(s, carry):
        start, end = steps_of(s)
        terms = [ratio_b[QUAD * s + i] for i in range(QUAD)]

        def body(step, inner):
            for u in range(2):
                q = 2 * step + u
                ks = [kern[QUAD * s + i, q - 2 * start] for i in range(QUAD)]
                for j in range(3):
                    add = [ks[i] * terms[i][j * CH : (j + 1) * CH] for i in range(QUAD)]
                    at = slice(j * CH, (j + 1) * CH)
                    total[q, at] = total[q, at] + ((add[0] + add[1]) + (add[2] + add[3]))
            return inner

        lax.fori_loop(start, end, body, 0)
        return carry

    lax.fori_loop(0, count, slot_push, 0)

    for ref, out, offset in ((prev, part_prev, 0), (own, part_own, TILES)):

        def finish(q, carry, ref=ref, out=out, offset=offset):
            weight = total[offset + q, 0:CH]
            for j in range(2):
                at = slice(j * CH, (j + 1) * CH)
                pulled = total[offset + q, (j + 1) * CH : (j + 2) * CH]
                out[q, at] = (pulled - ref[q, at] * weight) * UNSCALE
            if out is part_own:
                out[q, 2 * CH : 3 * CH] = jnp.zeros((CH, LANES), jnp.float32)
            return carry

        lax.fori_loop(0, TILES, finish, 0)

    for s in range(SLOTS):
        tile, first = info[TILE + s], info[LANE0 + s]
        moved = pltpu.roll(result, lax.rem(first + LANES - QUAD * s, LANES), 1)
        here = (lane >= first) & (lane < jnp.where(s < count, first + QUAD, first))
        part_own[tile] = part_own[tile] + jnp.where(here, moved, 0.0)


def pairs(info, prev, own):
    f32 = jnp.float32
    vmem = pl.BlockSpec(memory_space=pltpu.VMEM)
    return pl.pallas_call(
        pair_kernel,
        out_shape=(
            jax.ShapeDtypeStruct((TILES, 2 * CH, LANES), f32),
            jax.ShapeDtypeStruct((TILES, 3 * CH, LANES), f32),
        ),
        in_specs=[pl.BlockSpec(memory_space=pltpu.SMEM)] + [vmem] * 2,
        out_specs=(vmem,) * 2,
        scratch_shapes=[
            pltpu.VMEM((LANES, 2 * TILES, LANES), f32),
            pltpu.VMEM((LANES, 2 * CH, LANES), f32),
            pltpu.VMEM((LANES, TILES + 4, CH, LANES), f32),
            pltpu.VMEM((LANES, 3 * CH, LANES), f32),
            pltpu.VMEM((LANES, 3 * CH, LANES), f32),
            pltpu.VMEM((2 * TILES, 3 * CH, LANES), f32),
            pltpu.VMEM((2 * TILES, LANES), f32),
            pltpu.VMEM((LANES, LANES), f32),
        ],
        compiler_params=pltpu.CompilerParams(vmem_limit_bytes=58 * 2**20),
    )(info, prev, own)


def plan(meta, me, no_prev):
    live = meta[:, 0].astype(jnp.int32)
    window = meta[:, 1:3].astype(jnp.int32).reshape(-1)
    blocks = 2 * TILES
    block = jnp.arange(blocks, dtype=jnp.int32)
    low = jnp.maximum(window * BLK, jnp.where(no_prev, TILES * LANES, 0))
    quads = jnp.clip((jnp.repeat(live, 2) - BLK * (block % 2) + QUAD - 1) // QUAD, 0, BLK // QUAD)
    cost = block * BLK - low
    order = (cost[:, None] > cost[None, :]) | ((cost[:, None] == cost[None, :]) & (block[:, None] < block[None, :]))
    before = jnp.sum(jnp.where(order, quads[:, None], 0), axis=0)
    rounds = jnp.arange(SLOTS, dtype=jnp.int32)
    number = rounds * TILES + (me + TILES // 2 * (rounds % 2)) % TILES
    mine = (before[None, :] <= number[:, None]) & (number[:, None] < (before + quads)[None, :])

    def pick(value):
        return jnp.sum(jnp.where(mine, value, 0), axis=1)

    count = jnp.sum((number < jnp.sum(quads)).astype(jnp.int32))
    which = pick(block[None, :])
    first = (which % 2) * BLK + QUAD * pick(number[:, None] - before[None, :])
    return jnp.concatenate([count[None], which // 2, first, pick(low[None, :])])


def per_device(locations, times, background, weights, window_start, live):
    slot_ids = jnp.arange(LANES, dtype=jnp.int32)
    alive = slot_ids < live[0]
    alive_mask = alive.astype(jnp.float32)
    meta = jnp.pad(jnp.concatenate([live, window_start]).astype(jnp.float32), (0, LANES - 3))
    chunk = jnp.concatenate(
        [
            locations[:, 0, :] * SCALE,
            locations[:, 1, :] * SCALE,
            jnp.stack([jnp.where(alive, times, DEAD), times, background, alive_mask, meta]),
            jnp.zeros((W_ROW - META_ROW - 1, LANES), jnp.float32),
            weights * alive_mask,
        ]
    )
    own = lax.all_to_all(jnp.broadcast_to(chunk[None], (TILES, ROWS, LANES)), "grp", 0, 0)
    prev = from_behind(own[:, 0:W_ROW], "tm", 1)
    info = plan(own[:, META_ROW, 0:3], lax.axis_index("grp").astype(jnp.int32), lax.axis_index("tm") == 0)
    part_prev, part_own = pairs(info, prev, own)
    back = from_behind(part_prev, "tm", -1)
    part = jnp.concatenate([part_own[:, 0 : 2 * CH] + back, part_own[:, 2 * CH :]], axis=1)
    result = jnp.sum(lax.all_to_all(part, "grp", 0, 0), axis=0)
    grad = result[0 : 2 * CH].reshape(2, CH, LANES).transpose(1, 0, 2)
    return (grad, result[2 * CH :])


def solution(mesh):
    return jax.shard_map(
        per_device,
        mesh=mesh,
        in_specs=(
            P(None, None, ("tm", "grp")),
            P(("tm", "grp")),
            P(("tm", "grp")),
            P(None, ("tm", "grp")),
            P(("tm", "grp")),
            P(("tm", "grp")),
        ),
        out_specs=(P(None, None, ("tm", "grp")), P(None, ("tm", "grp"))),
        check_vma=False,
    )
```

```python
import math

import jax
import jax.numpy as jnp
from jax import lax
from jax.experimental import pallas as pl
from jax.experimental.pallas import tpu as pltpu
from jax.sharding import PartitionSpec as P

offspring = 0.8
fast_rate = 0.125
slow_rate = 0.0009765625

CH = 16
LANES = 128
TILES = 32
BLK = 64
QUAD = 4
SLOTS = 32
DEAD = -1e30

HALF = TILES // 2

TIME_ROW, BACK_ROW, META_ROW = range(2 * CH, 2 * CH + 3)
W_ROW = 40
ROWS = W_ROW + CH
COUNT, FIRST, LOW = range(3)

SCALE = math.sqrt(0.5 / math.log(2.0))
UNSCALE = 1.0 / SCALE
LOG2E = 1.0 / math.log(2.0)
LOG2_SLOW = math.log2(offspring * 0.5 * slow_rate / (2.0 * math.pi))


def from_behind(value, axis, by):
    count = lax.axis_size(axis)
    pairs = [(i, i + by) for i in range(count) if 0 <= i + by < count]
    return lax.ppermute(value, axis, pairs)


def log2_time_kernel(delta):
    fast = (fast_rate / slow_rate) * jnp.exp2(delta * (-(fast_rate - slow_rate) * LOG2E))
    return (LOG2_SLOW - delta * (slow_rate * LOG2E)) + jnp.log(1.0 + fast) * LOG2E


def slot_lanes(lane, s):
    return (lane >= QUAD * s) & (lane < QUAD * (s + 1))


def lane_ids():
    return lax.broadcasted_iota(jnp.int32, (1, LANES), 1)


def spread_lanes(out, values):
    rows = values.shape[0]
    for child in range(LANES):
        out[child] = jnp.broadcast_to(values[:, child : child + 1], (rows, LANES))


def gather_lanes(sums):
    lane = lane_ids()
    collected = jnp.zeros(sums.shape[1:], jnp.float32)
    for child in range(LANES):
        collected = jnp.where(lane == child, jnp.sum(sums[child], axis=1, keepdims=True), collected)
    return collected


def set_times(out, packed, times_q, tiles):
    out[...] = jnp.transpose(jnp.broadcast_to(packed[TIME_ROW : TIME_ROW + 1], (LANES, LANES)))
    for q in range(TILES):
        times_q[q : q + 1] = tiles[q, TIME_ROW : TIME_ROW + 1]


def time_rows(info, s, log_t, child_t, times_q, offset):
    pos = lax.broadcasted_iota(jnp.int32, (TILES, LANES), 0) * LANES + offset
    pos = pos + lax.broadcasted_iota(jnp.int32, (TILES, LANES), 1)
    low = info[LOW, s]
    for i in range(QUAD):
        at = QUAD * s + i
        delta = jnp.maximum(child_t[pl.ds(at, 1)] - times_q[...], 0.0)
        ok = (pos >= low) & (pos < info[FIRST, s] + i)
        log_t[at] = jnp.where(ok, log2_time_kernel(delta), DEAD)


def kernel_of(tiles, q, child_b, log_t, at):
    dx = tiles[q, 0:CH] - child_b[at, 0:CH]
    dy = tiles[q, CH : 2 * CH] - child_b[at, CH : 2 * CH]
    lt = log_t[at, pl.ds(q, 1), :]
    return jnp.exp2((lt - dx * dx) - dy * dy), dx, dy


def slot_sums(tiles, s, start, end, child_b, log_t, sums, kern=None):
    for i in range(QUAD):
        sums[QUAD * s + i] = jnp.zeros((3 * CH, LANES), jnp.float32)

    def body(step, carry):
        for i in range(QUAD):
            at = QUAD * s + i
            k0, dx0, dy0 = kernel_of(tiles, 2 * step, child_b, log_t, at)
            k1, dx1, dy1 = kernel_of(tiles, 2 * step + 1, child_b, log_t, at)
            if kern is not None:
                kern[at, 2 * step] = k0
                kern[at, 2 * step + 1] = k1
            sums[at, 0:CH] = (sums[at, 0:CH] + k0) + k1
            sums[at, CH : 2 * CH] = (sums[at, CH : 2 * CH] + k0 * dx0) + k1 * dx1
            sums[at, 2 * CH :] = (sums[at, 2 * CH :] + k0 * dy0) + k1 * dy1
        return carry

    lax.fori_loop(start, end, body, 0)


def own_steps(info, s):
    return jnp.maximum(info[LOW, s] // (2 * LANES) - HALF, 0), info[FIRST, s] // (2 * LANES) - HALF + 1


def prev_start(info, s):
    return jnp.minimum(info[LOW, s] // (2 * LANES), HALF)


def own_sums_kernel(info, own, packed, collected, log_t, child_b, sums, times_q, child_t):
    count = info[COUNT, 0]
    lane = lane_ids()
    mine = jnp.zeros((ROWS, LANES), jnp.float32)
    for s in range(SLOTS):
        first = info[FIRST, s]
        moved = pltpu.roll(own[first // LANES - TILES], lax.rem(QUAD * s + LANES - lax.rem(first, LANES), LANES), 1)
        mine = jnp.where(slot_lanes(lane, s), moved, mine)
    packed[...] = mine
    spread_lanes(child_b, mine[0 : 2 * CH])
    set_times(child_t, mine, times_q, own)

    def times(s, carry):
        time_rows(info, s, log_t, child_t, times_q, TILES * LANES)
        return carry

    lax.fori_loop(0, count, times, 0)

    def slot(s, carry):
        start, end = own_steps(info, s)
        slot_sums(own, s, start, end, child_b, log_t, sums)
        return carry

    lax.fori_loop(0, count, slot, 0)
    collected[...] = gather_lanes(sums)


def prev_kernel(
    info, prev, packed, own_sums, part, result, ratio_out,
    log_t, child_b, kern, sums, total, times_q, child_t
):
    count = info[COUNT, 0]
    spread_lanes(child_b, packed[0 : 2 * CH])
    set_times(child_t, packed, times_q, prev)

    def times(s, carry):
        @pl.when(info[LOW, s] < TILES * LANES)
        def _():
            time_rows(info, s, log_t, child_t, times_q, 0)

        return carry

    lax.fori_loop(0, count, times, 0)

    def slot(s, carry):
        slot_sums(prev, s, prev_start(info, s), HALF, child_b, log_t, sums, kern)
        return carry

    lax.fori_loop(0, count, slot, 0)

    collected = own_sums[...] + gather_lanes(sums)
    xs, ys, weights = packed[0:CH], packed[CH : 2 * CH], packed[W_ROW : W_ROW + CH]
    intensity = packed[BACK_ROW : BACK_ROW + 1] + collected[0:CH]
    alive = packed[TIME_ROW : TIME_ROW + 1] >= 0.0
    ratio = weights / intensity
    ratio_out[...] = ratio
    result[0:CH] = ratio * collected[CH : 2 * CH] * UNSCALE
    result[CH : 2 * CH] = ratio * collected[2 * CH :] * UNSCALE
    result[2 * CH :] = jnp.where(alive, jnp.log(intensity), 0.0)
    spread_lanes(sums, jnp.concatenate([ratio, ratio * xs, ratio * ys], axis=0))

    def clear(q, carry):
        total[q] = jnp.zeros((3 * CH, LANES), jnp.float32)
        return carry

    lax.fori_loop(0, TILES, clear, 0)

    def push(s, carry):
        def body(step, inner):
            for u in range(2):
                q = 2 * step + u
                ks = [kern[QUAD * s + i, q] for i in range(QUAD)]
                for j in range(3):
                    at = slice(j * CH, (j + 1) * CH)
                    add = [ks[i] * sums[QUAD * s + i, at] for i in range(QUAD)]
                    total[q, at] = total[q, at] + ((add[0] + add[1]) + (add[2] + add[3]))
            return inner

        lax.fori_loop(prev_start(info, s), HALF, body, 0)
        return carry

    lax.fori_loop(0, count, push, 0)

    def finish(q, carry):
        weight = total[q, 0:CH]
        for j in range(2):
            at = slice(j * CH, (j + 1) * CH)
            part[q, at] = (total[q, (j + 1) * CH : (j + 2) * CH] - prev[q, at] * weight) * UNSCALE
        return carry

    lax.fori_loop(0, TILES, finish, 0)


def own_push_kernel(info, own, packed, result, ratio, part, log_t, child_b, ratio_b, times_q, child_t):
    count = info[COUNT, 0]
    lane = lane_ids()
    spread_lanes(child_b, packed[0 : 2 * CH])
    spread_lanes(ratio_b, ratio[...] * -UNSCALE)
    set_times(child_t, packed, times_q, own)

    def times(s, carry):
        time_rows(info, s, log_t, child_t, times_q, TILES * LANES)
        return carry

    lax.fori_loop(0, count, times, 0)

    def clear(q, carry):
        part[q] = jnp.zeros((3 * CH, LANES), jnp.float32)
        return carry

    lax.fori_loop(0, TILES, clear, 0)

    def slot(s, carry):
        start, end = own_steps(info, s)

        def body(step, inner):
            for u in range(2):
                q = 2 * step + u
                xs, ys = [], []
                for i in range(QUAD):
                    k, dx, dy = kernel_of(own, q, child_b, log_t, QUAD * s + i)
                    weighted = k * ratio_b[QUAD * s + i]
                    xs.append(weighted * dx)
                    ys.append(weighted * dy)
                part[q, 0:CH] = part[q, 0:CH] + ((xs[0] + xs[1]) + (xs[2] + xs[3]))
                part[q, CH : 2 * CH] = part[q, CH : 2 * CH] + ((ys[0] + ys[1]) + (ys[2] + ys[3]))
            return inner

        lax.fori_loop(start, end, body, 0)
        return carry

    lax.fori_loop(0, count, slot, 0)

    for s in range(SLOTS):
        first = info[FIRST, s]
        tile, at = first // LANES - TILES, lax.rem(first, LANES)
        moved = pltpu.roll(result[...], lax.rem(at + LANES - QUAD * s, LANES), 1)
        here = (lane >= at) & (lane < jnp.where(s < count, at + QUAD, at))
        part[tile] = part[tile] + jnp.where(here, moved, 0.0)


def call(kernel, out_rows, scratch, *operands):
    vmem = pl.BlockSpec(memory_space=pltpu.VMEM)
    return pl.pallas_call(
        kernel,
        out_shape=[jax.ShapeDtypeStruct(shape, jnp.float32) for shape in out_rows],
        in_specs=[pl.BlockSpec(memory_space=pltpu.SMEM)] + [vmem] * (len(operands) - 1),
        out_specs=[vmem] * len(out_rows),
        scratch_shapes=[pltpu.VMEM(shape, jnp.float32) for shape in scratch],
        compiler_params=pltpu.CompilerParams(vmem_limit_bytes=50 * 2**20),
    )(*operands)


TIMES = [(TILES, LANES), (LANES, LANES)]
LOG_T = (LANES, TILES, LANES)
CHILD_B = (LANES, 2 * CH, LANES)
SUMS = (LANES, 3 * CH, LANES)


def own_sums(info, own):
    return call(own_sums_kernel, [(ROWS, LANES), (3 * CH, LANES)], [LOG_T, CHILD_B, SUMS] + TIMES, info, own)


def prev_pairs(info, prev, packed, collected):
    return call(
        prev_kernel,
        [(TILES, 2 * CH, LANES), (3 * CH, LANES), (CH, LANES)],
        [LOG_T, CHILD_B, (LANES, TILES, CH, LANES), SUMS, (TILES, 3 * CH, LANES)] + TIMES,
        info, prev, packed, collected,
    )


def own_push(info, own, packed, result, ratio):
    return call(
        own_push_kernel,
        [(TILES, 3 * CH, LANES)],
        [LOG_T, CHILD_B, (LANES, CH, LANES)] + TIMES,
        info, own, packed, result, ratio,
    )[0]


def plan(meta, me, no_prev):
    blocks = 2 * TILES
    block = jnp.arange(blocks, dtype=jnp.int32)
    rounds = jnp.arange(SLOTS, dtype=jnp.int32)
    live = jnp.repeat(meta[:, 0], 2).astype(jnp.int32)
    window = meta[:, 1:3].reshape(-1).astype(jnp.int32)
    low = jnp.maximum(window * BLK, jnp.where(no_prev, TILES * LANES, 0))
    quads = jnp.clip((live - BLK * (block % 2) + QUAD - 1) // QUAD, 0, BLK // QUAD)
    key = (low - block * BLK) * blocks + block
    before = jnp.sum(jnp.where(key[:, None] < key[None, :], quads[:, None], 0), axis=0)
    number = rounds * TILES + (me + TILES // 2 * (rounds % 2)) % TILES
    offset = number[:, None] - before[None, :]
    mine = (offset >= 0) & (offset < quads[None, :])
    first = TILES * LANES + block[None, :] * BLK + QUAD * offset
    values = jnp.stack([jnp.ones_like(first), first, jnp.broadcast_to(low[None, :], first.shape)])
    info = jnp.sum(jnp.where(mine[None], values, 0), axis=2)
    count = jnp.sum(info[0])
    return jnp.stack([jnp.full((SLOTS,), count), jnp.maximum(info[1], TILES * LANES), info[2]])


def per_device(locations, times, background, weights, window_start, live):
    slot_ids = jnp.arange(LANES, dtype=jnp.int32)
    alive = slot_ids < live[0]
    meta = jnp.pad(jnp.concatenate([live, window_start]).astype(jnp.float32), (0, LANES - 3))
    chunk = jnp.concatenate(
        [
            locations[:, 0, :] * SCALE,
            locations[:, 1, :] * SCALE,
            jnp.stack([jnp.where(alive, times, DEAD), background, meta]),
            jnp.zeros((W_ROW - META_ROW - 1, LANES), jnp.float32),
            jnp.where(alive, weights, 0.0),
        ]
    )
    own = lax.all_to_all(jnp.broadcast_to(chunk[None], (TILES, ROWS, LANES)), "grp", 0, 0)
    prev = from_behind(own[:, 0:W_ROW], "tm", 1)
    info = plan(own[:, META_ROW, 0:3], lax.axis_index("grp").astype(jnp.int32), lax.axis_index("tm") == 0)
    packed, collected = own_sums(info, own)
    part_prev, result, ratio = prev_pairs(info, prev, packed, collected)
    back = from_behind(part_prev, "tm", -1)
    part_own = own_push(info, own, packed, result, ratio)
    part = jnp.concatenate([part_own[:, 0 : 2 * CH] + back, part_own[:, 2 * CH :]], axis=1)
    total = jnp.sum(lax.all_to_all(part, "grp", 0, 0), axis=0)
    grad = total[0 : 2 * CH].reshape(2, CH, LANES).transpose(1, 0, 2)
    return (grad, total[2 * CH :])


def solution(mesh):
    return jax.shard_map(
        per_device,
        mesh=mesh,
        in_specs=(
            P(None, None, ("tm", "grp")),
            P(("tm", "grp")),
            P(("tm", "grp")),
            P(None, ("tm", "grp")),
            P(("tm", "grp")),
            P(("tm", "grp")),
        ),
        out_specs=(P(None, None, ("tm", "grp")), P(None, ("tm", "grp"))),
        check_vma=False,
    )
```

```python
import math

import jax
import jax.numpy as jnp
from jax import lax
from jax.experimental import pallas as pl
from jax.experimental.pallas import tpu as pltpu
from jax.sharding import PartitionSpec as P

offspring = 0.8
fast_rate = 0.125
slow_rate = 0.0009765625

CH = 16
LANES = 128
TILES = 32
BLK = 64
QUAD = 4
SLOTS = 32
DEAD = -1e30

HALF = TILES // 2

TIME_ROW, BACK_ROW, META_ROW = range(2 * CH, 2 * CH + 3)
W_ROW = 40
ROWS = W_ROW + CH
VALID, FIRST, LOW = range(3)

SCALE = math.sqrt(0.5 / math.log(2.0))
UNSCALE = 1.0 / SCALE
LOG2E = 1.0 / math.log(2.0)
LOG2_SLOW = math.log2(offspring * 0.5 * slow_rate / (2.0 * math.pi))


def from_behind(value, axis, by):
    count = lax.axis_size(axis)
    pairs = [(i, i + by) for i in range(count) if 0 <= i + by < count]
    return lax.ppermute(value, axis, pairs)


def log2_time_kernel(delta):
    fast = (fast_rate / slow_rate) * jnp.exp2(delta * (-(fast_rate - slow_rate) * LOG2E))
    return (LOG2_SLOW - delta * (slow_rate * LOG2E)) + jnp.log(1.0 + fast) * LOG2E


def slot_lanes(lane, s):
    return (lane >= QUAD * s) & (lane < QUAD * (s + 1))


def lane_ids():
    return lax.broadcasted_iota(jnp.int32, (1, LANES), 1)


def spread_lanes(out, values):
    rows = values.shape[0]
    for child in range(LANES):
        out[child] = jnp.broadcast_to(values[:, child : child + 1], (rows, LANES))


def gather_lanes(sums):
    lane = lane_ids()
    collected = jnp.zeros(sums.shape[1:], jnp.float32)
    for child in range(LANES):
        collected = jnp.where(lane == child, jnp.sum(sums[child], axis=1, keepdims=True), collected)
    return [collected[j * CH : (j + 1) * CH] for j in range(3)]


def slots_of(info):
    count = info[VALID, 0]
    for s in range(1, SLOTS):
        count = count + info[VALID, s]
    return count


def first_of(info, s):
    return jnp.maximum(info[FIRST, s], TILES * LANES)


def set_times(times_q, tiles):
    for q in range(TILES):
        times_q[q : q + 1] = tiles[q, TIME_ROW : TIME_ROW + 1]


def time_rows(info, s, log_t, child_t, times_q, own):
    pos = lax.broadcasted_iota(jnp.int32, (TILES, LANES), 0) * LANES + (TILES * LANES if own else 0)
    pos = pos + lax.broadcasted_iota(jnp.int32, (TILES, LANES), 1)
    ok = pos >= info[LOW, s]
    for i in range(QUAD):
        at = QUAD * s + i
        delta = jnp.maximum(child_t[pl.ds(at, 1)] - times_q[...], 0.0)
        allowed = ok & (pos < info[FIRST, s] + i) if own else ok
        log_t[at] = jnp.where(allowed, log2_time_kernel(delta), DEAD)


def kernel_of(tiles, q, child_b, log_t, at):
    dx = tiles[q, 0:CH] - child_b[at, 0:CH]
    dy = tiles[q, CH : 2 * CH] - child_b[at, CH : 2 * CH]
    lt = log_t[at, pl.ds(q, 1), :]
    return jnp.exp2((lt - dx * dx) - dy * dy), dx, dy


def slot_sums(tiles, s, start, end, child_b, log_t, sums, kern=None):
    for i in range(QUAD):
        sums[QUAD * s + i] = jnp.zeros((3 * CH, LANES), jnp.float32)

    def body(step, carry):
        for i in range(QUAD):
            at = QUAD * s + i
            k0, dx0, dy0 = kernel_of(tiles, 2 * step, child_b, log_t, at)
            k1, dx1, dy1 = kernel_of(tiles, 2 * step + 1, child_b, log_t, at)
            if kern is not None:
                kern[at, 2 * step] = k0
                kern[at, 2 * step + 1] = k1
            sums[at, 0:CH] = (sums[at, 0:CH] + k0) + k1
            sums[at, CH : 2 * CH] = (sums[at, CH : 2 * CH] + k0 * dx0) + k1 * dx1
            sums[at, 2 * CH :] = (sums[at, 2 * CH :] + k0 * dy0) + k1 * dy1
        return carry

    lax.fori_loop(start, end, body, 0)


def own_steps(info, s):
    return jnp.maximum(info[LOW, s] // (2 * LANES) - HALF, 0), info[FIRST, s] // (2 * LANES) - HALF + 1


def prev_start(info, s):
    return jnp.minimum(info[LOW, s] // (2 * LANES), HALF)


def own_sums_kernel(info, own, packed, collected, child_b, child_t, log_t, sums, times_q):
    count = slots_of(info)
    lane = lane_ids()
    mine = jnp.zeros((ROWS, LANES), jnp.float32)
    for s in range(SLOTS):
        first = first_of(info, s)
        moved = pltpu.roll(own[first // LANES - TILES], lax.rem(QUAD * s + LANES - lax.rem(first, LANES), LANES), 1)
        mine = jnp.where(slot_lanes(lane, s), moved, mine)
    packed[...] = mine
    spread_lanes(child_b, mine[0 : 2 * CH])
    child_t[...] = jnp.transpose(jnp.broadcast_to(mine[TIME_ROW : TIME_ROW + 1], (LANES, LANES)))
    set_times(times_q, own)

    def times(s, carry):
        time_rows(info, s, log_t, child_t, times_q, True)
        return carry

    lax.fori_loop(0, count, times, 0)

    def slot(s, carry):
        start, end = own_steps(info, s)
        slot_sums(own, s, start, end, child_b, log_t, sums)
        return carry

    lax.fori_loop(0, count, slot, 0)
    for j, part in enumerate(gather_lanes(sums)):
        collected[j * CH : (j + 1) * CH] = part


def prev_kernel(
    info, prev, packed, own_sums, child_b, child_t, part, result, ratio_out,
    log_t, kern, sums, total, times_q
):
    count = slots_of(info)
    set_times(times_q, prev)

    def times(s, carry):
        @pl.when(info[LOW, s] < TILES * LANES)
        def _():
            time_rows(info, s, log_t, child_t, times_q, False)

        return carry

    lax.fori_loop(0, count, times, 0)

    def slot(s, carry):
        slot_sums(prev, s, prev_start(info, s), HALF, child_b, log_t, sums, kern)
        return carry

    lax.fori_loop(0, count, slot, 0)

    here = gather_lanes(sums)
    summed, pull_x, pull_y = [own_sums[j * CH : (j + 1) * CH] + here[j] for j in range(3)]
    xs, ys, weights = packed[0:CH], packed[CH : 2 * CH], packed[W_ROW : W_ROW + CH]
    intensity = packed[BACK_ROW : BACK_ROW + 1] + summed
    alive = packed[TIME_ROW : TIME_ROW + 1] >= 0.0
    ratio = weights / intensity
    ratio_out[...] = ratio
    result[0:CH] = ratio * pull_x * UNSCALE
    result[CH : 2 * CH] = ratio * pull_y * UNSCALE
    result[2 * CH :] = jnp.where(alive, jnp.log(intensity), 0.0)
    spread_lanes(sums, jnp.concatenate([ratio, ratio * xs, ratio * ys], axis=0))

    def clear(q, carry):
        total[q] = jnp.zeros((3 * CH, LANES), jnp.float32)
        return carry

    lax.fori_loop(0, TILES, clear, 0)

    def push(s, carry):
        def body(step, inner):
            for u in range(2):
                q = 2 * step + u
                ks = [kern[QUAD * s + i, q] for i in range(QUAD)]
                for j in range(3):
                    at = slice(j * CH, (j + 1) * CH)
                    add = [ks[i] * sums[QUAD * s + i, at] for i in range(QUAD)]
                    total[q, at] = total[q, at] + ((add[0] + add[1]) + (add[2] + add[3]))
            return inner

        lax.fori_loop(prev_start(info, s), HALF, body, 0)
        return carry

    lax.fori_loop(0, count, push, 0)

    def finish(q, carry):
        weight = total[q, 0:CH]
        for j in range(2):
            at = slice(j * CH, (j + 1) * CH)
            part[q, at] = (total[q, (j + 1) * CH : (j + 2) * CH] - prev[q, at] * weight) * UNSCALE
        return carry

    lax.fori_loop(0, TILES, finish, 0)


def own_push_kernel(info, own, result, ratio, child_b, child_t, part, log_t, ratio_b, times_q):
    count = slots_of(info)
    lane = lane_ids()
    spread_lanes(ratio_b, ratio[...] * -UNSCALE)
    set_times(times_q, own)

    def times(s, carry):
        time_rows(info, s, log_t, child_t, times_q, True)
        return carry

    lax.fori_loop(0, count, times, 0)

    def clear(q, carry):
        part[q] = jnp.zeros((3 * CH, LANES), jnp.float32)
        return carry

    lax.fori_loop(0, TILES, clear, 0)

    def slot(s, carry):
        start, end = own_steps(info, s)

        def body(step, inner):
            for u in range(2):
                q = 2 * step + u
                xs, ys = [], []
                for i in range(QUAD):
                    k, dx, dy = kernel_of(own, q, child_b, log_t, QUAD * s + i)
                    weighted = k * ratio_b[QUAD * s + i]
                    xs.append(weighted * dx)
                    ys.append(weighted * dy)
                part[q, 0:CH] = part[q, 0:CH] + ((xs[0] + xs[1]) + (xs[2] + xs[3]))
                part[q, CH : 2 * CH] = part[q, CH : 2 * CH] + ((ys[0] + ys[1]) + (ys[2] + ys[3]))
            return inner

        lax.fori_loop(start, end, body, 0)
        return carry

    lax.fori_loop(0, count, slot, 0)

    for s in range(SLOTS):
        first = first_of(info, s)
        tile, at = first // LANES - TILES, lax.rem(first, LANES)
        moved = pltpu.roll(result[...], lax.rem(at + LANES - QUAD * s, LANES), 1)
        here = (lane >= at) & (lane < jnp.where(s < count, at + QUAD, at))
        part[tile] = part[tile] + jnp.where(here, moved, 0.0)


def call(kernel, out_rows, scratch, scalars, *operands, mib=24):
    vmem = pl.BlockSpec(memory_space=pltpu.VMEM)
    return pl.pallas_call(
        kernel,
        out_shape=[jax.ShapeDtypeStruct(shape, jnp.float32) for shape in out_rows],
        in_specs=[pl.BlockSpec(memory_space=pltpu.SMEM)] * len(scalars) + [vmem] * len(operands),
        out_specs=[vmem] * len(out_rows),
        scratch_shapes=[pltpu.VMEM(shape, jnp.float32) for shape in scratch],
        compiler_params=pltpu.CompilerParams(vmem_limit_bytes=mib * 2**20),
    )(*scalars, *operands)


TIMES = (TILES, LANES)
LOG_T = (LANES, TILES, LANES)
CHILD_B = (LANES, 2 * CH, LANES)
SUMS = (LANES, 3 * CH, LANES)


def pack_kernel(window, live, locations, times, background, weights, out):
    lane = lane_ids()
    alive = lane < live[0]
    numbers = (live[0], window[0], window[1])
    meta = jnp.zeros((1, LANES), jnp.float32)
    for i, number in enumerate(numbers):
        meta = jnp.where(lane == i, number.astype(jnp.float32), meta)
    rows = jnp.concatenate([jnp.where(alive, times[...], DEAD), background[...], meta], axis=0)
    rest = jnp.zeros((W_ROW - META_ROW - 1, LANES), jnp.float32)
    chunk = jnp.concatenate(
        [locations[:, 0, :] * SCALE, locations[:, 1, :] * SCALE, rows, rest, jnp.where(alive, weights[...], 0.0)],
        axis=0,
    )
    for to in range(TILES):
        out[to] = chunk


def pack(window, live, *operands):
    return call(pack_kernel, [(TILES, ROWS, LANES)], [], (window, live), *operands)[0]


def own_sums(info, own):
    return call(
        own_sums_kernel, [(ROWS, LANES), (3 * CH, LANES), CHILD_B, (LANES, LANES)], [LOG_T, SUMS, TIMES], (info,), own
    )


def prev_pairs(info, *operands):
    return call(
        prev_kernel,
        [(TILES, 2 * CH, LANES), (3 * CH, LANES), (CH, LANES)],
        [LOG_T, (LANES, TILES, CH, LANES), SUMS, (TILES, 3 * CH, LANES), TIMES],
        (info,), *operands, mib=48,
    )


def own_push(info, *operands):
    return call(own_push_kernel, [(TILES, 3 * CH, LANES)], [LOG_T, (LANES, CH, LANES), TIMES], (info,), *operands)[0]


def plan(meta, me, no_prev):
    blocks = 2 * TILES
    block = jnp.arange(blocks, dtype=jnp.int32)
    rounds = jnp.arange(SLOTS, dtype=jnp.int32)
    live = jnp.repeat(meta[:, 0], 2).astype(jnp.int32)
    window = meta[:, 1:3].reshape(-1).astype(jnp.int32)
    low = jnp.maximum(window * BLK, jnp.where(no_prev, TILES * LANES, 0))
    quads = jnp.clip((live - BLK * (block % 2) + QUAD - 1) // QUAD, 0, BLK // QUAD)
    key = (low - block * BLK) * blocks + block
    before = jnp.sum(jnp.where(key[:, None] < key[None, :], quads[:, None], 0), axis=0)
    number = rounds * TILES + (me + TILES // 2 * (rounds % 2)) % TILES
    offset = number[:, None] - before[None, :]
    mine = (offset >= 0) & (offset < quads[None, :])
    first = TILES * LANES + block[None, :] * BLK + QUAD * offset
    values = jnp.stack([jnp.ones_like(first), first, jnp.broadcast_to(low[None, :], first.shape)])
    return jnp.sum(jnp.where(mine[None], values, 0), axis=2)


def per_device(locations, times, background, weights, window_start, live):
    sent = pack(window_start, live, locations, times[None], background[None], weights)
    own = lax.all_to_all(sent, "grp", 0, 0)
    prev = from_behind(own[:, 0:W_ROW], "tm", 1)
    info = plan(own[:, META_ROW, 0:3], lax.axis_index("grp").astype(jnp.int32), lax.axis_index("tm") == 0)
    packed, collected, child_b, child_t = own_sums(info, own)
    part_prev, result, ratio = prev_pairs(info, prev, packed, collected, child_b, child_t)
    back = from_behind(part_prev, "tm", -1)
    part_own = own_push(info, own, result, ratio, child_b, child_t)
    part = jnp.concatenate([part_own[:, 0 : 2 * CH] + back, part_own[:, 2 * CH :]], axis=1)
    total = jnp.sum(lax.all_to_all(part, "grp", 0, 0), axis=0)
    grad = total[0 : 2 * CH].reshape(2, CH, LANES).transpose(1, 0, 2)
    return (grad, total[2 * CH :])


def solution(mesh):
    return jax.shard_map(
        per_device,
        mesh=mesh,
        in_specs=(
            P(None, None, ("tm", "grp")),
            P(("tm", "grp")),
            P(("tm", "grp")),
            P(None, ("tm", "grp")),
            P(("tm", "grp")),
            P(("tm", "grp")),
        ),
        out_specs=(P(None, None, ("tm", "grp")), P(None, ("tm", "grp"))),
        check_vma=False,
    )
```

```python
import math

import jax
import jax.numpy as jnp
from jax import lax
from jax.experimental import pallas as pl
from jax.experimental.pallas import tpu as pltpu
from jax.sharding import PartitionSpec as P

offspring = 0.8
fast_rate = 0.125
slow_rate = 0.0009765625

CH = 16
LANES = 128
TILES = 32
BLK = 64
QUAD = 4
SLOTS = 32
DEAD = -1e30

HALF = TILES // 2

TIME_ROW, BACK_ROW, META_ROW = range(2 * CH, 2 * CH + 3)
W_ROW = 40
ROWS = W_ROW + CH
VALID, FIRST, LOW, BEFORE = range(4)
LOG_ROW = 2 * CH
BACK_ROWS = LOG_ROW + 8

SCALE = math.sqrt(0.5 / math.log(2.0))
UNSCALE = 1.0 / SCALE
LOG2E = 1.0 / math.log(2.0)
LOG2_SLOW = math.log2(offspring * 0.5 * slow_rate / (2.0 * math.pi))


def from_behind(value, axis, by):
    count = lax.axis_size(axis)
    pairs = [(i, i + by) for i in range(count) if 0 <= i + by < count]
    return lax.ppermute(value, axis, pairs)


def log2_time_kernel(delta):
    fast = (fast_rate / slow_rate) * jnp.exp2(delta * (-(fast_rate - slow_rate) * LOG2E))
    return (LOG2_SLOW - delta * (slow_rate * LOG2E)) + jnp.log(1.0 + fast) * LOG2E


def slot_lanes(lane, s):
    return (lane >= QUAD * s) & (lane < QUAD * (s + 1))


def lane_ids():
    return lax.broadcasted_iota(jnp.int32, (1, LANES), 1)


def spread_lanes(out, values):
    rows = values.shape[0]
    for child in range(LANES):
        out[child] = jnp.broadcast_to(values[:, child : child + 1], (rows, LANES))


def gather_lanes(sums):
    lane = lane_ids()
    collected = jnp.zeros(sums.shape[1:], jnp.float32)
    for child in range(LANES):
        collected = jnp.where(lane == child, jnp.sum(sums[child], axis=1, keepdims=True), collected)
    return [collected[j * CH : (j + 1) * CH] for j in range(3)]


def slots_of(info):
    count = info[VALID, 0]
    for s in range(1, SLOTS):
        count = count + info[VALID, s]
    return count


def first_of(info, s):
    return jnp.maximum(info[FIRST, s], TILES * LANES)


def set_times(times_q, tiles):
    for q in range(TILES):
        times_q[q : q + 1] = tiles[q, TIME_ROW : TIME_ROW + 1]


def time_rows(info, s, log_t, child_t, times_q, own):
    pos = lax.broadcasted_iota(jnp.int32, (TILES, LANES), 0) * LANES + (TILES * LANES if own else 0)
    pos = pos + lax.broadcasted_iota(jnp.int32, (TILES, LANES), 1)
    ok = pos >= info[LOW, s]
    for i in range(QUAD):
        at = QUAD * s + i
        delta = jnp.maximum(child_t[pl.ds(at, 1)] - times_q[...], 0.0)
        allowed = ok & (pos < info[FIRST, s] + i) if own else ok
        log_t[at] = jnp.where(allowed, log2_time_kernel(delta), DEAD)


def kernel_of(tiles, q, child_b, log_t, at):
    dx = tiles[q, 0:CH] - child_b[at, 0:CH]
    dy = tiles[q, CH : 2 * CH] - child_b[at, CH : 2 * CH]
    lt = log_t[at, pl.ds(q, 1), :]
    return jnp.exp2((lt - dx * dx) - dy * dy), dx, dy


def slot_sums(tiles, s, start, end, child_b, log_t, sums, kern=None):
    for i in range(QUAD):
        sums[QUAD * s + i] = jnp.zeros((3 * CH, LANES), jnp.float32)

    def body(step, carry):
        for i in range(QUAD):
            at = QUAD * s + i
            k0, dx0, dy0 = kernel_of(tiles, 2 * step, child_b, log_t, at)
            k1, dx1, dy1 = kernel_of(tiles, 2 * step + 1, child_b, log_t, at)
            if kern is not None:
                kern[at, 2 * step] = k0
                kern[at, 2 * step + 1] = k1
            sums[at, 0:CH] = (sums[at, 0:CH] + k0) + k1
            sums[at, CH : 2 * CH] = (sums[at, CH : 2 * CH] + k0 * dx0) + k1 * dx1
            sums[at, 2 * CH :] = (sums[at, 2 * CH :] + k0 * dy0) + k1 * dy1
        return carry

    lax.fori_loop(start, end, body, 0)


def own_steps(info, s):
    return jnp.maximum(info[LOW, s] // (2 * LANES) - HALF, 0), info[FIRST, s] // (2 * LANES) - HALF + 1


def prev_start(info, s):
    return jnp.minimum(info[LOW, s] // (2 * LANES), HALF)


def own_sums_kernel(info, own, packed, collected, child_b, child_t, log_t, sums, times_q):
    count = slots_of(info)
    lane = lane_ids()
    mine = jnp.zeros((ROWS, LANES), jnp.float32)
    for s in range(SLOTS):
        first = first_of(info, s)
        moved = pltpu.roll(own[first // LANES - TILES], lax.rem(QUAD * s + LANES - lax.rem(first, LANES), LANES), 1)
        mine = jnp.where(slot_lanes(lane, s), moved, mine)
    packed[...] = mine
    spread_lanes(child_b, mine[0 : 2 * CH])
    child_t[...] = jnp.transpose(jnp.broadcast_to(mine[TIME_ROW : TIME_ROW + 1], (LANES, LANES)))
    set_times(times_q, own)

    def times(s, carry):
        time_rows(info, s, log_t, child_t, times_q, True)
        return carry

    lax.fori_loop(0, count, times, 0)

    def slot(s, carry):
        start, end = own_steps(info, s)
        slot_sums(own, s, start, end, child_b, log_t, sums)
        return carry

    lax.fori_loop(0, count, slot, 0)
    for j, part in enumerate(gather_lanes(sums)):
        collected[j * CH : (j + 1) * CH] = part


def prev_kernel(
    info, prev, packed, own_sums, child_b, child_t, part, result, ratio_out,
    log_t, kern, sums, total, times_q
):
    count = slots_of(info)
    set_times(times_q, prev)

    def times(s, carry):
        @pl.when(info[LOW, s] < TILES * LANES)
        def _():
            time_rows(info, s, log_t, child_t, times_q, False)

        return carry

    lax.fori_loop(0, count, times, 0)

    def slot(s, carry):
        slot_sums(prev, s, prev_start(info, s), HALF, child_b, log_t, sums, kern)
        return carry

    lax.fori_loop(0, count, slot, 0)

    here = gather_lanes(sums)
    summed, pull_x, pull_y = [own_sums[j * CH : (j + 1) * CH] + here[j] for j in range(3)]
    xs, ys, weights = packed[0:CH], packed[CH : 2 * CH], packed[W_ROW : W_ROW + CH]
    intensity = packed[BACK_ROW : BACK_ROW + 1] + summed
    alive = (packed[TIME_ROW : TIME_ROW + 1] >= 0.0) & (lane_ids() < QUAD * count)
    ratio = weights / intensity
    ratio_out[...] = ratio
    result[0:CH] = ratio * pull_x * UNSCALE
    result[CH : 2 * CH] = ratio * pull_y * UNSCALE
    result[2 * CH :] = jnp.where(alive, jnp.log(intensity), 0.0)
    spread_lanes(sums, jnp.concatenate([ratio, ratio * xs, ratio * ys], axis=0))

    def clear(q, carry):
        total[q] = jnp.zeros((3 * CH, LANES), jnp.float32)
        return carry

    lax.fori_loop(0, TILES, clear, 0)

    def push(s, carry):
        def body(step, inner):
            for u in range(2):
                q = 2 * step + u
                ks = [kern[QUAD * s + i, q] for i in range(QUAD)]
                for j in range(3):
                    at = slice(j * CH, (j + 1) * CH)
                    add = [ks[i] * sums[QUAD * s + i, at] for i in range(QUAD)]
                    total[q, at] = total[q, at] + ((add[0] + add[1]) + (add[2] + add[3]))
            return inner

        lax.fori_loop(prev_start(info, s), HALF, body, 0)
        return carry

    lax.fori_loop(0, count, push, 0)

    def finish(q, carry):
        weight = total[q, 0:CH]
        for j in range(2):
            at = slice(j * CH, (j + 1) * CH)
            part[q, at] = (total[q, (j + 1) * CH : (j + 2) * CH] - prev[q, at] * weight) * UNSCALE
        return carry

    lax.fori_loop(0, TILES, finish, 0)


def exact_dot(a, b):
    return jnp.dot(a, b, precision=lax.Precision.HIGHEST, preferred_element_type=jnp.float32)


def logs_by_slot(logs):
    wide = jnp.concatenate([logs, jnp.zeros((LANES - CH, LANES), jnp.float32)], axis=0)
    row = lax.broadcasted_iota(jnp.int32, (LANES, LANES), 0)
    lane = lax.broadcasted_iota(jnp.int32, (LANES, LANES), 1)
    by_child = exact_dot(jnp.transpose(wide), ((lane % BLK) // QUAD == row).astype(jnp.float32))
    by_child = jnp.where(lane % QUAD == row % QUAD, by_child, 0.0)
    slot = lax.broadcasted_iota(jnp.int32, (SLOTS, LANES), 0)
    child = lax.broadcasted_iota(jnp.int32, (SLOTS, LANES), 1)
    return exact_dot((child // QUAD == slot).astype(jnp.float32), by_child)


def own_push_kernel(info, own, result, ratio, child_b, child_t, part, log_t, ratio_b, times_q, slot_logs):
    count = slots_of(info)
    lane = lane_ids()
    spread_lanes(ratio_b, ratio[...] * -UNSCALE)
    set_times(times_q, own)

    def times(s, carry):
        time_rows(info, s, log_t, child_t, times_q, True)
        return carry

    lax.fori_loop(0, count, times, 0)

    def clear(q, carry):
        part[q] = jnp.zeros((BACK_ROWS, LANES), jnp.float32)
        return carry

    lax.fori_loop(0, TILES, clear, 0)

    def slot(s, carry):
        start, end = own_steps(info, s)

        def body(step, inner):
            for u in range(2):
                q = 2 * step + u
                xs, ys = [], []
                for i in range(QUAD):
                    k, dx, dy = kernel_of(own, q, child_b, log_t, QUAD * s + i)
                    weighted = k * ratio_b[QUAD * s + i]
                    xs.append(weighted * dx)
                    ys.append(weighted * dy)
                part[q, 0:CH] = part[q, 0:CH] + ((xs[0] + xs[1]) + (xs[2] + xs[3]))
                part[q, CH : 2 * CH] = part[q, CH : 2 * CH] + ((ys[0] + ys[1]) + (ys[2] + ys[3]))
            return inner

        lax.fori_loop(start, end, body, 0)
        return carry

    lax.fori_loop(0, count, slot, 0)

    slot_logs[...] = logs_by_slot(result[2 * CH :])
    for s in range(SLOTS):
        first = first_of(info, s)
        tile, at = first // LANES - TILES, lax.rem(first, LANES)
        moved = pltpu.roll(result[0 : 2 * CH], lax.rem(at + LANES - QUAD * s, LANES), 1)
        here = (lane >= at) & (lane < jnp.where(s < count, at + QUAD, at))
        part[tile, 0 : 2 * CH] = part[tile, 0 : 2 * CH] + jnp.where(here, moved, 0.0)
        half = jnp.where(s < count, at // BLK, 2)
        row = part[tile, LOG_ROW : LOG_ROW + 1]
        part[tile, LOG_ROW : LOG_ROW + 1] = row + jnp.where(lane // BLK == half, slot_logs[s : s + 1], 0.0)


def call(kernel, out_rows, scratch, scalars, *operands, mib=24):
    vmem = pl.BlockSpec(memory_space=pltpu.VMEM)
    return pl.pallas_call(
        kernel,
        out_shape=[jax.ShapeDtypeStruct(shape, jnp.float32) for shape in out_rows],
        in_specs=[pl.BlockSpec(memory_space=pltpu.SMEM)] * len(scalars) + [vmem] * len(operands),
        out_specs=[vmem] * len(out_rows),
        scratch_shapes=[pltpu.VMEM(shape, jnp.float32) for shape in scratch],
        compiler_params=pltpu.CompilerParams(vmem_limit_bytes=mib * 2**20),
    )(*scalars, *operands)


TIMES = (TILES, LANES)
LOG_T = (LANES, TILES, LANES)
CHILD_B = (LANES, 2 * CH, LANES)
SUMS = (LANES, 3 * CH, LANES)


def pack_kernel(*refs):
    operands, out, scratch, arrived = refs[:6], refs[6], refs[7:13], refs[13]
    copies = [pltpu.make_async_copy(operands[i], scratch[i], arrived.at[i]) for i in range(6)]
    for copy in copies:
        copy.start()
    for copy in copies:
        copy.wait()
    window, live, locations, times, background, weights = scratch
    lane = lane_ids()
    alive = lane < live[0]
    numbers = (live[0], window[0], window[1])
    meta = jnp.zeros((1, LANES), jnp.float32)
    for i, number in enumerate(numbers):
        meta = jnp.where(lane == i, number.astype(jnp.float32), meta)
    rows = jnp.concatenate([jnp.where(alive, times[...], DEAD), background[...], meta], axis=0)
    rest = jnp.zeros((W_ROW - META_ROW - 1, LANES), jnp.float32)
    chunk = jnp.concatenate(
        [locations[:, 0, :] * SCALE, locations[:, 1, :] * SCALE, rows, rest, jnp.where(alive, weights[...], 0.0)],
        axis=0,
    )
    for to in range(TILES):
        out[to] = chunk


def pack(*operands):
    spaces = [pltpu.SMEM] * 2 + [pltpu.VMEM] * 4
    return pl.pallas_call(
        pack_kernel,
        out_shape=jax.ShapeDtypeStruct((TILES, ROWS, LANES), jnp.float32),
        in_specs=[pl.BlockSpec(memory_space=pltpu.HBM)] * 6,
        out_specs=pl.BlockSpec(memory_space=pltpu.VMEM),
        scratch_shapes=[space(x.shape, x.dtype) for space, x in zip(spaces, operands)]
        + [pltpu.SemaphoreType.DMA((6,))],
        compiler_params=pltpu.CompilerParams(vmem_limit_bytes=24 * 2**20),
    )(*operands)


def collect_kernel(info, received, grad, logs, log_rows):
    log_rows[...] = jnp.zeros((LANES, LANES), jnp.float32)
    total = received[0, 0 : 2 * CH]
    log_rows[0:1] = received[0, LOG_ROW : LOG_ROW + 1]
    for source in range(1, TILES):
        total = total + received[source, 0 : 2 * CH]
        log_rows[source : source + 1] = received[source, LOG_ROW : LOG_ROW + 1]
    grad[:, 0, :] = total[0:CH]
    grad[:, 1, :] = total[CH:]
    row = lax.broadcasted_iota(jnp.int32, (LANES, LANES), 0)
    lane = lax.broadcasted_iota(jnp.int32, (LANES, LANES), 1)
    number = jnp.where(lane < BLK, info[BEFORE, 0], info[BEFORE, 1]) + (lane % BLK) // QUAD
    source = (number - HALF * ((number // TILES) % 2)) % TILES
    chosen = exact_dot(jnp.transpose(log_rows[...]), (row == source).astype(jnp.float32))
    chosen = jnp.where((row // BLK == lane // BLK) & (row % QUAD == lane % QUAD), chosen, 0.0)
    chain = lax.broadcasted_iota(jnp.int32, (CH, LANES), 0)
    place = lax.broadcasted_iota(jnp.int32, (CH, LANES), 1)
    logs[...] = exact_dot(((place % BLK) // QUAD == chain).astype(jnp.float32), chosen)


def collect(info, received):
    vmem = pl.BlockSpec(memory_space=pltpu.VMEM)
    return pl.pallas_call(
        collect_kernel,
        out_shape=[
            jax.ShapeDtypeStruct((CH, 2, LANES), jnp.float32),
            jax.ShapeDtypeStruct((CH, LANES), jnp.float32),
        ],
        in_specs=[pl.BlockSpec(memory_space=pltpu.SMEM), vmem],
        out_specs=[vmem] * 2,
        scratch_shapes=[pltpu.VMEM((LANES, LANES), jnp.float32)],
        compiler_params=pltpu.CompilerParams(vmem_limit_bytes=24 * 2**20),
    )(info, received)


def own_sums(info, own):
    return call(
        own_sums_kernel, [(ROWS, LANES), (3 * CH, LANES), CHILD_B, (LANES, LANES)], [LOG_T, SUMS, TIMES], (info,), own
    )


def prev_pairs(info, *operands):
    return call(
        prev_kernel,
        [(TILES, 2 * CH, LANES), (3 * CH, LANES), (CH, LANES)],
        [LOG_T, (LANES, TILES, CH, LANES), SUMS, (TILES, 3 * CH, LANES), TIMES],
        (info,), *operands, mib=48,
    )


def own_push(info, *operands):
    return call(
        own_push_kernel,
        [(TILES, BACK_ROWS, LANES)],
        [LOG_T, (LANES, CH, LANES), TIMES, (SLOTS, LANES)],
        (info,), *operands,
    )[0]


def plan(meta, me, no_prev):
    blocks = 2 * TILES
    block = jnp.arange(blocks, dtype=jnp.int32)
    rounds = jnp.arange(SLOTS, dtype=jnp.int32)
    live = jnp.repeat(meta[:, 0], 2).astype(jnp.int32)
    window = meta[:, 1:3].reshape(-1).astype(jnp.int32)
    low = jnp.maximum(window * BLK, jnp.where(no_prev, TILES * LANES, 0))
    quads = jnp.clip((live - BLK * (block % 2) + QUAD - 1) // QUAD, 0, BLK // QUAD)
    key = (low - block * BLK) * blocks + block
    before = jnp.sum(jnp.where(key[:, None] < key[None, :], quads[:, None], 0), axis=0)
    number = rounds * TILES + (me + TILES // 2 * (rounds % 2)) % TILES
    offset = number[:, None] - before[None, :]
    mine = (offset >= 0) & (offset < quads[None, :])
    first = TILES * LANES + block[None, :] * BLK + QUAD * offset
    own_block = block[None, :] == 2 * me + rounds[:, None] % 2
    every = [jnp.broadcast_to(value[None, :], first.shape) for value in (low, before)]
    values = jnp.stack([jnp.ones_like(first), first, *every])
    mine = jnp.stack([mine, mine, mine, own_block])
    return jnp.sum(jnp.where(mine, values, 0), axis=2)


def per_device(locations, times, background, weights, window_start, live):
    sent = pack(window_start, live, locations, times[None], background[None], weights)
    own = lax.all_to_all(sent, "grp", 0, 0)
    prev = from_behind(own[:, 0:W_ROW], "tm", 1)
    info = plan(own[:, META_ROW, 0:3], lax.axis_index("grp").astype(jnp.int32), lax.axis_index("tm") == 0)
    packed, collected, child_b, child_t = own_sums(info, own)
    part_prev, result, ratio = prev_pairs(info, prev, packed, collected, child_b, child_t)
    back = from_behind(part_prev, "tm", -1)
    part_own = own_push(info, own, result, ratio, child_b, child_t)
    part = jnp.concatenate([part_own[:, 0 : 2 * CH] + back, part_own[:, 2 * CH :]], axis=1)
    grad, log_intensity = collect(info, lax.all_to_all(part, "grp", 0, 0))
    return (grad, log_intensity)


def solution(mesh):
    return jax.shard_map(
        per_device,
        mesh=mesh,
        in_specs=(
            P(None, None, ("tm", "grp")),
            P(("tm", "grp")),
            P(("tm", "grp")),
            P(None, ("tm", "grp")),
            P(("tm", "grp")),
            P(("tm", "grp")),
        ),
        out_specs=(P(None, None, ("tm", "grp")), P(None, ("tm", "grp"))),
        check_vma=False,
    )
```

```python
import math

import jax
import jax.numpy as jnp
from jax import lax
from jax.experimental import pallas as pl
from jax.experimental.pallas import tpu as pltpu
from jax.sharding import PartitionSpec as P

offspring = 0.8
fast_rate = 0.125
slow_rate = 0.0009765625

CH = 16
LANES = 128
TILES = 32
BLK = 64
QUAD = 4
SLOTS = 32
DEAD = -1e30

HALF = TILES // 2

TIME_ROW, BACK_ROW, META_ROW, QUAD_ROW = range(2 * CH, 2 * CH + 4)
ROWS = 40
W_ROW = ROWS
VALID, FIRST, LOW = range(3)
LOG_ROW = 2 * CH
BACK_ROWS = LOG_ROW + 8

SCALE = math.sqrt(0.5 / math.log(2.0))
UNSCALE = 1.0 / SCALE
LOG2E = 1.0 / math.log(2.0)
LOG2_SLOW = math.log2(offspring * 0.5 * slow_rate / (2.0 * math.pi))


def from_behind(value, axis, by):
    count = lax.axis_size(axis)
    pairs = [(i, i + by) for i in range(count) if 0 <= i + by < count]
    return lax.ppermute(value, axis, pairs)


def log2_time_kernel(delta):
    fast = (fast_rate / slow_rate) * jnp.exp2(delta * (-(fast_rate - slow_rate) * LOG2E))
    return (LOG2_SLOW - delta * (slow_rate * LOG2E)) + jnp.log(1.0 + fast) * LOG2E


def slot_lanes(lane, s):
    return (lane >= QUAD * s) & (lane < QUAD * (s + 1))


def lane_ids():
    return lax.broadcasted_iota(jnp.int32, (1, LANES), 1)


def spread_lanes(out, values):
    rows = values.shape[0]
    for child in range(LANES):
        out[child] = jnp.broadcast_to(values[:, child : child + 1], (rows, LANES))


def gather_lanes(sums):
    lane = lane_ids()
    collected = jnp.zeros(sums.shape[1:], jnp.float32)
    for child in range(LANES):
        collected = jnp.where(lane == child, jnp.sum(sums[child], axis=1, keepdims=True), collected)
    return [collected[j * CH : (j + 1) * CH] for j in range(3)]


def mirrored(tile):
    return ((tile & 1) << 4) | ((tile & 2) << 2) | (tile & 4) | ((tile & 8) >> 2) | ((tile & 16) >> 4)


def deal(live, first_window, second_window):
    quads = [jnp.clip((live - BLK * i + QUAD - 1) // QUAD, 0, BLK // QUAD) for i in range(2)]
    second = (first_window >= second_window).astype(jnp.int32)
    swap = second * (quads[1] - quads[0])
    return second, quads[0] + swap, quads[1] - swap


def quad_at(place, live, first_window, second_window):
    first, ahead, behind = deal(live, first_window, second_window)
    later = (place >= ahead).astype(jnp.int32)
    block = first + later * (1 - 2 * first)
    valid = place < ahead + behind
    return jnp.where(valid, block * (BLK // QUAD) + place - later * ahead, 0), valid


def set_times(times_q, tiles):
    for q in range(TILES):
        times_q[q : q + 1] = tiles[q, TIME_ROW : TIME_ROW + 1]


def time_rows(info, s, log_t, child_t, times_q, own):
    pos = lax.broadcasted_iota(jnp.int32, (TILES, LANES), 0) * LANES + (TILES * LANES if own else 0)
    pos = pos + lax.broadcasted_iota(jnp.int32, (TILES, LANES), 1)
    ok = pos >= info[LOW, s]
    for i in range(QUAD):
        at = QUAD * s + i
        delta = jnp.maximum(child_t[pl.ds(at, 1)] - times_q[...], 0.0)
        allowed = ok & (pos < info[FIRST, s] + i) if own else ok
        log_t[at] = jnp.where(allowed, log2_time_kernel(delta), DEAD)


def kernel_of(tiles, q, child_b, log_t, at):
    dx = tiles[q, 0:CH] - child_b[at, 0:CH]
    dy = tiles[q, CH : 2 * CH] - child_b[at, CH : 2 * CH]
    lt = log_t[at, pl.ds(q, 1), :]
    return jnp.exp2((lt - dx * dx) - dy * dy), dx, dy


def slot_sums(tiles, s, start, end, child_b, log_t, sums, kern=None):
    for i in range(QUAD):
        sums[QUAD * s + i] = jnp.zeros((3 * CH, LANES), jnp.float32)

    def body(step, carry):
        for i in range(QUAD):
            at = QUAD * s + i
            k0, dx0, dy0 = kernel_of(tiles, 2 * step, child_b, log_t, at)
            k1, dx1, dy1 = kernel_of(tiles, 2 * step + 1, child_b, log_t, at)
            if kern is not None:
                kern[at, 2 * step] = k0
                kern[at, 2 * step + 1] = k1
            sums[at, 0:CH] = (sums[at, 0:CH] + k0) + k1
            sums[at, CH : 2 * CH] = (sums[at, CH : 2 * CH] + k0 * dx0) + k1 * dx1
            sums[at, 2 * CH :] = (sums[at, 2 * CH :] + k0 * dy0) + k1 * dy1
        return carry

    lax.fori_loop(start, end, body, 0)


def own_steps(info, s):
    return jnp.maximum(info[LOW, s] // (2 * LANES) - HALF, 0), info[FIRST, s] // (2 * LANES) - HALF + 1


def prev_start(info, s):
    return jnp.minimum(info[LOW, s] // (2 * LANES), HALF)


def exact_dot(a, b):
    return jnp.dot(a, b, precision=lax.Precision.HIGHEST, preferred_element_type=jnp.float32)


def square():
    return lax.broadcasted_iota(jnp.int32, (LANES, LANES), 0), lax.broadcasted_iota(jnp.int32, (LANES, LANES), 1)


def rows_of_quads(values):
    wide = jnp.concatenate([values, jnp.zeros((LANES - CH, LANES), jnp.float32)], axis=0)
    row, lane = square()
    by_lane = exact_dot(jnp.transpose(wide), (lane // QUAD == row).astype(jnp.float32))
    by_lane = jnp.where(lane % QUAD == row % QUAD, by_lane, 0.0)
    slot = lax.broadcasted_iota(jnp.int32, (SLOTS, LANES), 0)
    child = lax.broadcasted_iota(jnp.int32, (SLOTS, LANES), 1)
    return exact_dot((child // QUAD == slot).astype(jnp.float32), by_lane)


def place_quads(rows, source):
    row, lane = square()
    chosen = exact_dot(jnp.transpose(rows), (row == source).astype(jnp.float32))
    chosen = jnp.where(row % QUAD == lane % QUAD, chosen, 0.0)
    chain = lax.broadcasted_iota(jnp.int32, (CH, LANES), 0)
    place = lax.broadcasted_iota(jnp.int32, (CH, LANES), 1)
    return exact_dot((place // QUAD == chain).astype(jnp.float32), chosen)


def own_sums_kernel(info, own, packed, collected, child_b, child_t, log_t, sums, times_q, quad_rows):
    lane = lane_ids()
    mine = jnp.zeros((ROWS, LANES), jnp.float32)
    quad_rows[...] = jnp.zeros((LANES, LANES), jnp.float32)
    for s in range(SLOTS):
        shift = lax.rem(QUAD * s + LANES - lax.rem(info[FIRST, s], LANES), LANES)
        mine = jnp.where(slot_lanes(lane, s), pltpu.roll(own[s], shift, 1), mine)
        quad_rows[s : s + 1] = own[s, QUAD_ROW : QUAD_ROW + 1]
    packed[0:ROWS] = mine
    packed[W_ROW:] = place_quads(quad_rows[...], lane // QUAD)
    spread_lanes(child_b, mine[0 : 2 * CH])
    child_t[...] = jnp.transpose(jnp.broadcast_to(mine[TIME_ROW : TIME_ROW + 1], (LANES, LANES)))
    set_times(times_q, own)

    def times(s, carry):
        @pl.when(info[VALID, s] > 0)
        def _():
            time_rows(info, s, log_t, child_t, times_q, True)

        return carry

    lax.fori_loop(0, SLOTS, times, 0)

    def slot(s, carry):
        start, end = own_steps(info, s)
        slot_sums(own, s, start, end, child_b, log_t, sums)
        return carry

    lax.fori_loop(0, SLOTS, slot, 0)
    for j, part in enumerate(gather_lanes(sums)):
        collected[j * CH : (j + 1) * CH] = part


def prev_kernel(
    info, prev, packed, own_sums, child_b, child_t, part, result, ratio_out,
    log_t, kern, sums, total, times_q
):
    set_times(times_q, prev)

    def times(s, carry):
        @pl.when(info[LOW, s] < TILES * LANES)
        def _():
            time_rows(info, s, log_t, child_t, times_q, False)

        return carry

    lax.fori_loop(0, SLOTS, times, 0)

    def slot(s, carry):
        slot_sums(prev, s, prev_start(info, s), HALF, child_b, log_t, sums, kern)
        return carry

    lax.fori_loop(0, SLOTS, slot, 0)

    here = gather_lanes(sums)
    summed, pull_x, pull_y = [own_sums[j * CH : (j + 1) * CH] + here[j] for j in range(3)]
    xs, ys, weights = packed[0:CH], packed[CH : 2 * CH], packed[W_ROW : W_ROW + CH]
    intensity = packed[BACK_ROW : BACK_ROW + 1] + summed
    alive = packed[TIME_ROW : TIME_ROW + 1] >= 0.0
    ratio = weights / intensity
    ratio_out[...] = ratio
    result[0:CH] = ratio * pull_x * UNSCALE
    result[CH : 2 * CH] = ratio * pull_y * UNSCALE
    result[2 * CH :] = jnp.where(alive, jnp.log(intensity), 0.0)
    spread_lanes(sums, jnp.concatenate([ratio, ratio * xs, ratio * ys], axis=0))

    def clear(q, carry):
        total[q] = jnp.zeros((3 * CH, LANES), jnp.float32)
        return carry

    lax.fori_loop(0, TILES, clear, 0)

    def push(s, carry):
        def body(step, inner):
            for u in range(2):
                q = 2 * step + u
                ks = [kern[QUAD * s + i, q] for i in range(QUAD)]
                for j in range(3):
                    at = slice(j * CH, (j + 1) * CH)
                    add = [ks[i] * sums[QUAD * s + i, at] for i in range(QUAD)]
                    total[q, at] = total[q, at] + ((add[0] + add[1]) + (add[2] + add[3]))
            return inner

        lax.fori_loop(prev_start(info, s), HALF, body, 0)
        return carry

    lax.fori_loop(0, SLOTS, push, 0)

    def finish(q, carry):
        weight = total[q, 0:CH]
        for j in range(2):
            at = slice(j * CH, (j + 1) * CH)
            part[q, at] = (total[q, (j + 1) * CH : (j + 2) * CH] - prev[q, at] * weight) * UNSCALE
        return carry

    lax.fori_loop(0, TILES, finish, 0)


def own_push_kernel(info, own, result, ratio, child_b, child_t, part, log_t, ratio_b, times_q, slot_logs):
    lane = lane_ids()
    spread_lanes(ratio_b, ratio[...] * -UNSCALE)
    set_times(times_q, own)

    def times(s, carry):
        @pl.when(info[VALID, s] > 0)
        def _():
            time_rows(info, s, log_t, child_t, times_q, True)

        return carry

    lax.fori_loop(0, SLOTS, times, 0)

    def clear(q, carry):
        part[q] = jnp.zeros((BACK_ROWS, LANES), jnp.float32)
        return carry

    lax.fori_loop(0, TILES, clear, 0)

    def slot(s, carry):
        start, end = own_steps(info, s)

        def body(step, inner):
            for u in range(2):
                q = 2 * step + u
                xs, ys = [], []
                for i in range(QUAD):
                    k, dx, dy = kernel_of(own, q, child_b, log_t, QUAD * s + i)
                    weighted = k * ratio_b[QUAD * s + i]
                    xs.append(weighted * dx)
                    ys.append(weighted * dy)
                part[q, 0:CH] = part[q, 0:CH] + ((xs[0] + xs[1]) + (xs[2] + xs[3]))
                part[q, CH : 2 * CH] = part[q, CH : 2 * CH] + ((ys[0] + ys[1]) + (ys[2] + ys[3]))
            return inner

        lax.fori_loop(start, end, body, 0)
        return carry

    lax.fori_loop(0, SLOTS, slot, 0)

    slot_logs[...] = rows_of_quads(result[2 * CH :])
    for s in range(SLOTS):
        at = lax.rem(info[FIRST, s], LANES)
        moved = pltpu.roll(result[0 : 2 * CH], lax.rem(at + LANES - QUAD * s, LANES), 1)
        here = (lane >= at) & (lane < at + QUAD)
        part[s, 0 : 2 * CH] = part[s, 0 : 2 * CH] + jnp.where(here, moved, 0.0)
        part[s, LOG_ROW : LOG_ROW + 1] = jnp.where(info[VALID, s] > 0, slot_logs[s : s + 1], 0.0)


def call(kernel, out_rows, scratch, scalars, *operands, mib=24):
    vmem = pl.BlockSpec(memory_space=pltpu.VMEM)
    return pl.pallas_call(
        kernel,
        out_shape=[jax.ShapeDtypeStruct(shape, jnp.float32) for shape in out_rows],
        in_specs=[pl.BlockSpec(memory_space=pltpu.SMEM)] * len(scalars) + [vmem] * len(operands),
        out_specs=[vmem] * len(out_rows),
        scratch_shapes=[pltpu.VMEM(shape, jnp.float32) for shape in scratch],
        compiler_params=pltpu.CompilerParams(vmem_limit_bytes=mib * 2**20),
    )(*scalars, *operands)


TIMES = (TILES, LANES)
LOG_T = (LANES, TILES, LANES)
CHILD_B = (LANES, 2 * CH, LANES)
SUMS = (LANES, 3 * CH, LANES)


def pack_kernel(*refs):
    operands, out, scratch, arrived, quad_rows = refs[:6], refs[6], refs[7:13], refs[13], refs[14]
    copies = [pltpu.make_async_copy(operands[i], scratch[i], arrived.at[i]) for i in range(6)]
    for copy in copies:
        copy.start()
    for copy in copies:
        copy.wait()
    window, live, locations, times, background, weights = scratch
    lane = lane_ids()
    alive = lane < live[0]
    numbers = (live[0], window[0], window[1])
    meta = jnp.zeros((1, LANES), jnp.float32)
    for i, number in enumerate(numbers):
        meta = jnp.where(lane == i, number.astype(jnp.float32), meta)
    rows = jnp.concatenate([jnp.where(alive, times[...], DEAD), background[...], meta], axis=0)
    quad_rows[0:SLOTS] = rows_of_quads(jnp.where(alive, weights[...], 0.0))
    quad_rows[SLOTS:] = jnp.zeros((8, LANES), jnp.float32)
    rest = jnp.zeros((ROWS - META_ROW - 1, LANES), jnp.float32)
    chunk = jnp.concatenate([locations[:, 0, :] * SCALE, locations[:, 1, :] * SCALE, rows, rest], axis=0)
    turn = mirrored(lax.axis_index("grp"))
    for to in range(TILES):
        out[to] = chunk
        quad, valid = quad_at(to ^ turn, live[0], window[0], window[1])
        out[to, QUAD_ROW : QUAD_ROW + 1] = quad_rows[pl.ds(jnp.where(valid, quad, SLOTS), 1)]


def pack(*operands):
    spaces = [pltpu.SMEM] * 2 + [pltpu.VMEM] * 4
    return pl.pallas_call(
        pack_kernel,
        out_shape=jax.ShapeDtypeStruct((TILES, ROWS, LANES), jnp.float32),
        in_specs=[pl.BlockSpec(memory_space=pltpu.HBM)] * 6,
        out_specs=pl.BlockSpec(memory_space=pltpu.VMEM),
        scratch_shapes=[space(x.shape, x.dtype) for space, x in zip(spaces, operands)]
        + [pltpu.SemaphoreType.DMA((6,)), pltpu.VMEM((SLOTS + 8, LANES), jnp.float32)],
        compiler_params=pltpu.CompilerParams(vmem_limit_bytes=60 * 2**20),
    )(*operands)


def collect_kernel(window, live, received, grad, logs, log_rows):
    log_rows[...] = jnp.zeros((LANES, LANES), jnp.float32)
    total = received[0, 0 : 2 * CH]
    log_rows[0:1] = received[0, LOG_ROW : LOG_ROW + 1]
    for source in range(1, TILES):
        total = total + received[source, 0 : 2 * CH]
        log_rows[source : source + 1] = received[source, LOG_ROW : LOG_ROW + 1]
    grad[:, 0, :] = total[0:CH]
    grad[:, 1, :] = total[CH:]
    first, ahead, behind = deal(live[0], window[0], window[1])
    lane = lane_ids()
    quad = (lane % BLK) // QUAD
    sooner = lane // BLK == first
    valid = quad < jnp.where(sooner, ahead, behind)
    place = jnp.where(sooner, quad, quad + ahead)
    source = place ^ mirrored(lax.axis_index("grp"))
    logs[...] = place_quads(log_rows[...], jnp.where(valid, source, -1))


def collect(window, live, received):
    vmem = pl.BlockSpec(memory_space=pltpu.VMEM)
    return pl.pallas_call(
        collect_kernel,
        out_shape=[
            jax.ShapeDtypeStruct((CH, 2, LANES), jnp.float32),
            jax.ShapeDtypeStruct((CH, LANES), jnp.float32),
        ],
        in_specs=[pl.BlockSpec(memory_space=pltpu.SMEM)] * 2 + [vmem],
        out_specs=[vmem] * 2,
        scratch_shapes=[pltpu.VMEM((LANES, LANES), jnp.float32)],
        compiler_params=pltpu.CompilerParams(vmem_limit_bytes=24 * 2**20),
    )(window, live, received)


def own_sums(info, own):
    return call(
        own_sums_kernel,
        [(ROWS + CH, LANES), (3 * CH, LANES), CHILD_B, (LANES, LANES)],
        [LOG_T, SUMS, TIMES, (LANES, LANES)],
        (info,), own,
    )


def prev_pairs(info, *operands):
    return call(
        prev_kernel,
        [(TILES, 2 * CH, LANES), (3 * CH, LANES), (CH, LANES)],
        [LOG_T, (LANES, TILES, CH, LANES), SUMS, (TILES, 3 * CH, LANES), TIMES],
        (info,), *operands, mib=48,
    )


def own_push(info, *operands):
    return call(
        own_push_kernel,
        [(TILES, BACK_ROWS, LANES)],
        [LOG_T, (LANES, CH, LANES), TIMES, (SLOTS, LANES)],
        (info,), *operands,
    )[0]


def plan(meta, me, no_prev):
    live, first_window, second_window = [meta[:, i].astype(jnp.int32) for i in range(3)]
    tile = jnp.arange(TILES, dtype=jnp.int32)
    quad, valid = quad_at(me ^ mirrored(tile), live, first_window, second_window)
    window = jnp.where(quad < BLK // QUAD, first_window, second_window)
    low = jnp.maximum(window * BLK, jnp.where(no_prev, TILES * LANES, 0))
    first = (TILES + tile) * LANES + QUAD * quad
    return jnp.stack([valid.astype(jnp.int32), first, jnp.where(valid, low, 2 * TILES * LANES)])


def per_device(locations, times, background, weights, window_start, live):
    sent = pack(window_start, live, locations, times[None], background[None], weights)
    own = lax.all_to_all(sent, "grp", 0, 0)
    prev = from_behind(own, "tm", 1)
    info = plan(own[:, META_ROW, 0:3], lax.axis_index("grp").astype(jnp.int32), lax.axis_index("tm") == 0)
    packed, collected, child_b, child_t = own_sums(info, own)
    part_prev, result, ratio = prev_pairs(info, prev, packed, collected, child_b, child_t)
    back = from_behind(part_prev, "tm", -1)
    part_own = own_push(info, own, result, ratio, child_b, child_t)
    part = jnp.concatenate([part_own[:, 0 : 2 * CH] + back, part_own[:, 2 * CH :]], axis=1)
    grad, log_intensity = collect(window_start, live, lax.all_to_all(part, "grp", 0, 0))
    return (grad, log_intensity)


def solution(mesh):
    return jax.shard_map(
        per_device,
        mesh=mesh,
        in_specs=(
            P(None, None, ("tm", "grp")),
            P(("tm", "grp")),
            P(("tm", "grp")),
            P(None, ("tm", "grp")),
            P(("tm", "grp")),
            P(("tm", "grp")),
        ),
        out_specs=(P(None, None, ("tm", "grp")), P(None, ("tm", "grp"))),
        check_vma=False,
    )
```

```python
import math

import jax
import jax.numpy as jnp
from jax import lax
from jax.experimental import pallas as pl
from jax.experimental.pallas import tpu as pltpu
from jax.sharding import PartitionSpec as P

offspring = 0.8
fast_rate = 0.125
slow_rate = 0.0009765625

CH = 16
LANES = 128
TILES = 32
BLK = 64
QUAD = 4
SLOTS = 32
DEAD = -1e30

HALF = TILES // 2

TIME_ROW, QUAD_ROW = 2 * CH, 2 * CH + 1
ROWS = 2 * CH + 2
META_LANE = (CH + 1) * QUAD
BACK_ROW, W_ROW = TIME_ROW + 1, 40
VALID, FIRST, LOW = range(3)
LOG_ROW = 2 * CH
BACK_ROWS = LOG_ROW + 1
PLACED = 24

SCALE = math.sqrt(0.5 / math.log(2.0))
UNSCALE = 1.0 / SCALE
LOG2E = 1.0 / math.log(2.0)
LOG2_SLOW = math.log2(offspring * 0.5 * slow_rate / (2.0 * math.pi))


def from_behind(value, axis, by):
    count = lax.axis_size(axis)
    pairs = [(i, i + by) for i in range(count) if 0 <= i + by < count]
    return lax.ppermute(value, axis, pairs)


def log2_time_kernel(delta):
    fast = (fast_rate / slow_rate) * jnp.exp2(delta * (-(fast_rate - slow_rate) * LOG2E))
    return (LOG2_SLOW - delta * (slow_rate * LOG2E)) + jnp.log(1.0 + fast) * LOG2E


def slot_lanes(lane, s):
    return (lane >= QUAD * s) & (lane < QUAD * (s + 1))


def lane_ids():
    return lax.broadcasted_iota(jnp.int32, (1, LANES), 1)


def spread_lanes(out, values):
    rows = values.shape[0]
    for child in range(LANES):
        out[child] = jnp.broadcast_to(values[:, child : child + 1], (rows, LANES))


def gather_lanes(sums):
    lane = lane_ids()
    collected = jnp.zeros(sums.shape[1:], jnp.float32)
    for child in range(LANES):
        collected = jnp.where(lane == child, jnp.sum(sums[child], axis=1, keepdims=True), collected)
    return [collected[j * CH : (j + 1) * CH] for j in range(3)]


def mirrored(tile):
    return ((tile & 1) << 4) | ((tile & 2) << 2) | (tile & 4) | ((tile & 8) >> 2) | ((tile & 16) >> 4)


def deal(live, first_window, second_window):
    quads = [jnp.clip((live - BLK * i + QUAD - 1) // QUAD, 0, BLK // QUAD) for i in range(2)]
    second = (first_window >= second_window).astype(jnp.int32)
    swap = second * (quads[1] - quads[0])
    return second, quads[0] + swap, quads[1] - swap


def quad_at(place, live, first_window, second_window):
    first, ahead, behind = deal(live, first_window, second_window)
    later = (place >= ahead).astype(jnp.int32)
    block = first + later * (1 - 2 * first)
    valid = place < ahead + behind
    return jnp.where(valid, block * (BLK // QUAD) + place - later * ahead, 0), valid


def unpack_tiles(flat, tiles, times_q):
    for q in range(TILES):
        tiles[q] = flat[ROWS * q : ROWS * q + 2 * CH]
        times_q[q : q + 1] = flat[ROWS * q + TIME_ROW : ROWS * q + TIME_ROW + 1]


def time_rows(info, s, log_t, child_t, times_q, own):
    pos = lax.broadcasted_iota(jnp.int32, (TILES, LANES), 0) * LANES + (TILES * LANES if own else 0)
    pos = pos + lax.broadcasted_iota(jnp.int32, (TILES, LANES), 1)
    ok = pos >= info[LOW, s]
    for i in range(QUAD):
        at = QUAD * s + i
        delta = jnp.maximum(child_t[pl.ds(at, 1)] - times_q[...], 0.0)
        allowed = ok & (pos < info[FIRST, s] + i) if own else ok
        log_t[at] = jnp.where(allowed, log2_time_kernel(delta), DEAD)


def kernel_of(tiles, q, child_b, log_t, at):
    dx = tiles[q, 0:CH] - child_b[at, 0:CH]
    dy = tiles[q, CH : 2 * CH] - child_b[at, CH : 2 * CH]
    lt = log_t[at, pl.ds(q, 1), :]
    return jnp.exp2((lt - dx * dx) - dy * dy), dx, dy


def slot_sums(tiles, s, start, end, child_b, log_t, sums, kern=None):
    for i in range(QUAD):
        sums[QUAD * s + i] = jnp.zeros((3 * CH, LANES), jnp.float32)

    def body(step, carry):
        for i in range(QUAD):
            at = QUAD * s + i
            k0, dx0, dy0 = kernel_of(tiles, 2 * step, child_b, log_t, at)
            k1, dx1, dy1 = kernel_of(tiles, 2 * step + 1, child_b, log_t, at)
            if kern is not None:
                kern[at, 2 * step] = k0
                kern[at, 2 * step + 1] = k1
            sums[at, 0:CH] = (sums[at, 0:CH] + k0) + k1
            sums[at, CH : 2 * CH] = (sums[at, CH : 2 * CH] + k0 * dx0) + k1 * dx1
            sums[at, 2 * CH :] = (sums[at, 2 * CH :] + k0 * dy0) + k1 * dy1
        return carry

    lax.fori_loop(start, end, body, 0)


def own_steps(info, s):
    return jnp.maximum(info[LOW, s] // (2 * LANES) - HALF, 0), info[FIRST, s] // (2 * LANES) - HALF + 1


def prev_start(info, s):
    return jnp.minimum(info[LOW, s] // (2 * LANES), HALF)


def exact_dot(a, b):
    return jnp.dot(a, b, precision=lax.Precision.HIGHEST, preferred_element_type=jnp.float32)


def square():
    return lax.broadcasted_iota(jnp.int32, (LANES, LANES), 0), lax.broadcasted_iota(jnp.int32, (LANES, LANES), 1)


def rows_of_quads(values):
    wide = jnp.concatenate([values, jnp.zeros((LANES - values.shape[0], LANES), jnp.float32)], axis=0)
    row, lane = square()
    by_lane = exact_dot(jnp.transpose(wide), (lane // QUAD == row).astype(jnp.float32))
    by_lane = jnp.where(lane % QUAD == row % QUAD, by_lane, 0.0)
    slot = lax.broadcasted_iota(jnp.int32, (SLOTS, LANES), 0)
    child = lax.broadcasted_iota(jnp.int32, (SLOTS, LANES), 1)
    return exact_dot((child // QUAD == slot).astype(jnp.float32), by_lane)


def place_quads(rows, source):
    row, lane = square()
    chosen = exact_dot(jnp.transpose(rows), (row == source).astype(jnp.float32))
    chosen = jnp.where(row % QUAD == lane % QUAD, chosen, 0.0)
    chain = lax.broadcasted_iota(jnp.int32, (PLACED, LANES), 0)
    place = lax.broadcasted_iota(jnp.int32, (PLACED, LANES), 1)
    return exact_dot((place // QUAD == chain).astype(jnp.float32), chosen)


def own_sums_kernel(info, flat, packed, collected, child_b, child_t, own, times_q, log_t, sums, quad_rows):
    lane = lane_ids()
    unpack_tiles(flat, own, times_q)
    mine = jnp.zeros((2 * CH, LANES), jnp.float32)
    child_times = jnp.zeros((1, LANES), jnp.float32)
    quad_rows[...] = jnp.zeros((LANES, LANES), jnp.float32)
    for s in range(SLOTS):
        shift = lax.rem(QUAD * s + LANES - lax.rem(info[FIRST, s], LANES), LANES)
        mine = jnp.where(slot_lanes(lane, s), pltpu.roll(own[s], shift, 1), mine)
        child_times = jnp.where(slot_lanes(lane, s), pltpu.roll(times_q[s : s + 1], shift, 1), child_times)
        quad_rows[s : s + 1] = flat[ROWS * s + QUAD_ROW : ROWS * s + QUAD_ROW + 1]
    placed = place_quads(quad_rows[...], lane // QUAD)
    packed[0 : 2 * CH] = mine
    packed[TIME_ROW : TIME_ROW + 1] = child_times
    packed[BACK_ROW : BACK_ROW + 1] = placed[CH : CH + 1]
    packed[W_ROW:] = placed[0:CH]
    spread_lanes(child_b, mine)
    child_t[...] = jnp.transpose(jnp.broadcast_to(child_times, (LANES, LANES)))

    def times(s, carry):
        @pl.when(info[VALID, s] > 0)
        def _():
            time_rows(info, s, log_t, child_t, times_q, True)

        return carry

    lax.fori_loop(0, SLOTS, times, 0)

    def slot(s, carry):
        start, end = own_steps(info, s)
        slot_sums(own, s, start, end, child_b, log_t, sums)
        return carry

    lax.fori_loop(0, SLOTS, slot, 0)
    for j, part in enumerate(gather_lanes(sums)):
        collected[j * CH : (j + 1) * CH] = part


def prev_kernel(
    info, flat, packed, own_sums, child_b, child_t, part, result, ratio_out,
    log_t, kern, sums, total, times_q, prev
):
    unpack_tiles(flat, prev, times_q)

    def times(s, carry):
        @pl.when(info[LOW, s] < TILES * LANES)
        def _():
            time_rows(info, s, log_t, child_t, times_q, False)

        return carry

    lax.fori_loop(0, SLOTS, times, 0)

    def slot(s, carry):
        slot_sums(prev, s, prev_start(info, s), HALF, child_b, log_t, sums, kern)
        return carry

    lax.fori_loop(0, SLOTS, slot, 0)

    here = gather_lanes(sums)
    summed, pull_x, pull_y = [own_sums[j * CH : (j + 1) * CH] + here[j] for j in range(3)]
    xs, ys, weights = packed[0:CH], packed[CH : 2 * CH], packed[W_ROW : W_ROW + CH]
    intensity = packed[BACK_ROW : BACK_ROW + 1] + summed
    alive = packed[TIME_ROW : TIME_ROW + 1] >= 0.0
    ratio = weights / intensity
    ratio_out[...] = ratio
    result[0:CH] = ratio * pull_x * UNSCALE
    result[CH : 2 * CH] = ratio * pull_y * UNSCALE
    result[2 * CH :] = jnp.where(alive, jnp.log(intensity), 0.0)
    spread_lanes(sums, jnp.concatenate([ratio, ratio * xs, ratio * ys], axis=0))

    def clear(q, carry):
        total[q] = jnp.zeros((3 * CH, LANES), jnp.float32)
        return carry

    lax.fori_loop(0, TILES, clear, 0)

    def push(s, carry):
        def body(step, inner):
            for u in range(2):
                q = 2 * step + u
                ks = [kern[QUAD * s + i, q] for i in range(QUAD)]
                for j in range(3):
                    at = slice(j * CH, (j + 1) * CH)
                    add = [ks[i] * sums[QUAD * s + i, at] for i in range(QUAD)]
                    total[q, at] = total[q, at] + ((add[0] + add[1]) + (add[2] + add[3]))
            return inner

        lax.fori_loop(prev_start(info, s), HALF, body, 0)
        return carry

    lax.fori_loop(0, SLOTS, push, 0)

    for q in range(TILES):
        weight = total[q, 0:CH]
        for j in range(2):
            pulled = total[q, (j + 1) * CH : (j + 2) * CH] - prev[q, j * CH : (j + 1) * CH] * weight
            part[BACK_ROWS * q + j * CH : BACK_ROWS * q + (j + 1) * CH] = pulled * UNSCALE
        part[BACK_ROWS * q + LOG_ROW : BACK_ROWS * (q + 1)] = jnp.zeros((1, LANES), jnp.float32)


def own_push_kernel(info, own, times_q, result, ratio, child_b, child_t, flat, log_t, ratio_b, part, slot_logs):
    lane = lane_ids()
    spread_lanes(ratio_b, ratio[...] * -UNSCALE)

    def times(s, carry):
        @pl.when(info[VALID, s] > 0)
        def _():
            time_rows(info, s, log_t, child_t, times_q, True)

        return carry

    lax.fori_loop(0, SLOTS, times, 0)

    def clear(q, carry):
        part[q] = jnp.zeros((2 * CH, LANES), jnp.float32)
        return carry

    lax.fori_loop(0, TILES, clear, 0)

    def slot(s, carry):
        start, end = own_steps(info, s)

        def body(step, inner):
            for u in range(2):
                q = 2 * step + u
                xs, ys = [], []
                for i in range(QUAD):
                    k, dx, dy = kernel_of(own, q, child_b, log_t, QUAD * s + i)
                    weighted = k * ratio_b[QUAD * s + i]
                    xs.append(weighted * dx)
                    ys.append(weighted * dy)
                part[q, 0:CH] = part[q, 0:CH] + ((xs[0] + xs[1]) + (xs[2] + xs[3]))
                part[q, CH : 2 * CH] = part[q, CH : 2 * CH] + ((ys[0] + ys[1]) + (ys[2] + ys[3]))
            return inner

        lax.fori_loop(start, end, body, 0)
        return carry

    lax.fori_loop(0, SLOTS, slot, 0)

    slot_logs[...] = rows_of_quads(result[2 * CH :])
    for s in range(SLOTS):
        at = lax.rem(info[FIRST, s], LANES)
        moved = pltpu.roll(result[0 : 2 * CH], lax.rem(at + LANES - QUAD * s, LANES), 1)
        here = (lane >= at) & (lane < at + QUAD)
        at = BACK_ROWS * s
        flat[at : at + 2 * CH] = part[s] + jnp.where(here, moved, 0.0)
        flat[at + LOG_ROW : at + BACK_ROWS] = jnp.where(info[VALID, s] > 0, slot_logs[s : s + 1], 0.0)


def call(kernel, out_rows, scratch, scalars, *operands, mib=24):
    vmem = pl.BlockSpec(memory_space=pltpu.VMEM)
    return pl.pallas_call(
        kernel,
        out_shape=[jax.ShapeDtypeStruct(shape, jnp.float32) for shape in out_rows],
        in_specs=[pl.BlockSpec(memory_space=pltpu.SMEM)] * len(scalars) + [vmem] * len(operands),
        out_specs=[vmem] * len(out_rows),
        scratch_shapes=[pltpu.VMEM(shape, jnp.float32) for shape in scratch],
        compiler_params=pltpu.CompilerParams(vmem_limit_bytes=mib * 2**20),
    )(*scalars, *operands)


TIMES = (TILES, LANES)
XY = (TILES, 2 * CH, LANES)
LOG_T = (LANES, TILES, LANES)
CHILD_B = (LANES, 2 * CH, LANES)
SUMS = (LANES, 3 * CH, LANES)


def pack_kernel(*refs):
    operands, out, scratch, arrived, quad_rows = refs[:6], refs[6], refs[7:13], refs[13], refs[14]
    copies = [pltpu.make_async_copy(operands[i], scratch[i], arrived.at[i]) for i in range(6)]
    for copy in copies:
        copy.start()
    for copy in copies:
        copy.wait()
    window, live, locations, times, background, weights = scratch
    lane = lane_ids()
    alive = lane < live[0]
    meta = jnp.zeros((1, LANES), jnp.float32)
    for i, number in enumerate((live[0], window[0], window[1])):
        meta = jnp.where(lane == META_LANE + i, number.astype(jnp.float32), meta)
    quad_rows[0:SLOTS] = rows_of_quads(jnp.concatenate([jnp.where(alive, weights[...], 0.0), background[...]], axis=0))
    none = ((lane >= CH * QUAD) & (lane < META_LANE)).astype(jnp.float32)
    quad_rows[SLOTS:] = jnp.broadcast_to(none, (8, LANES))
    xs, ys = locations[:, 0, :] * SCALE, locations[:, 1, :] * SCALE
    time = jnp.where(alive, times[...], DEAD)
    turn = mirrored(lax.axis_index("grp"))
    for to in range(TILES):
        at = ROWS * to
        out[at : at + CH] = xs
        out[at + CH : at + 2 * CH] = ys
        out[at + TIME_ROW : at + TIME_ROW + 1] = time
        quad, valid = quad_at(to ^ turn, live[0], window[0], window[1])
        out[at + QUAD_ROW : at + ROWS] = quad_rows[pl.ds(jnp.where(valid, quad, SLOTS), 1)] + meta


def pack(*operands):
    spaces = [pltpu.SMEM] * 2 + [pltpu.VMEM] * 4
    return pl.pallas_call(
        pack_kernel,
        out_shape=jax.ShapeDtypeStruct((TILES * ROWS, LANES), jnp.float32),
        in_specs=[pl.BlockSpec(memory_space=pltpu.HBM)] * 6,
        out_specs=pl.BlockSpec(memory_space=pltpu.VMEM),
        scratch_shapes=[space(x.shape, x.dtype) for space, x in zip(spaces, operands)]
        + [pltpu.SemaphoreType.DMA((6,)), pltpu.VMEM((SLOTS + 8, LANES), jnp.float32)],
        compiler_params=pltpu.CompilerParams(vmem_limit_bytes=60 * 2**20),
    )(*operands)


def collect_kernel(window, live, received, grad, logs, log_rows):
    log_rows[...] = jnp.zeros((LANES, LANES), jnp.float32)
    total = jnp.zeros((2 * CH, LANES), jnp.float32)
    for source in range(TILES):
        at = BACK_ROWS * source
        total = total + received[at : at + 2 * CH]
        log_rows[source : source + 1] = received[at + LOG_ROW : at + BACK_ROWS]
    grad[:, 0, :] = total[0:CH]
    grad[:, 1, :] = total[CH:]
    first, ahead, behind = deal(live[0], window[0], window[1])
    lane = lane_ids()
    quad = (lane % BLK) // QUAD
    sooner = lane // BLK == first
    valid = quad < jnp.where(sooner, ahead, behind)
    place = jnp.where(sooner, quad, quad + ahead)
    source = place ^ mirrored(lax.axis_index("grp"))
    logs[...] = place_quads(log_rows[...], jnp.where(valid, source, -1))[0:CH]


def collect(window, live, received):
    vmem = pl.BlockSpec(memory_space=pltpu.VMEM)
    return pl.pallas_call(
        collect_kernel,
        out_shape=[
            jax.ShapeDtypeStruct((CH, 2, LANES), jnp.float32),
            jax.ShapeDtypeStruct((CH, LANES), jnp.float32),
        ],
        in_specs=[pl.BlockSpec(memory_space=pltpu.SMEM)] * 2 + [vmem],
        out_specs=[vmem] * 2,
        scratch_shapes=[pltpu.VMEM((LANES, LANES), jnp.float32)],
        compiler_params=pltpu.CompilerParams(vmem_limit_bytes=24 * 2**20),
    )(window, live, received)


def own_sums(info, flat):
    return call(
        own_sums_kernel,
        [(W_ROW + CH, LANES), (3 * CH, LANES), CHILD_B, (LANES, LANES), XY, TIMES],
        [LOG_T, SUMS, (LANES, LANES)],
        (info,), flat,
    )


def prev_pairs(info, *operands):
    return call(
        prev_kernel,
        [(TILES * BACK_ROWS, LANES), (3 * CH, LANES), (CH, LANES)],
        [LOG_T, (LANES, TILES, CH, LANES), SUMS, (TILES, 3 * CH, LANES), TIMES, XY],
        (info,), *operands, mib=48,
    )


def own_push(info, *operands):
    return call(
        own_push_kernel,
        [(TILES * BACK_ROWS, LANES)],
        [LOG_T, (LANES, CH, LANES), XY, (SLOTS, LANES)],
        (info,), *operands,
    )[0]


def plan(meta, me, no_prev):
    live, first_window, second_window = [meta[:, i].astype(jnp.int32) for i in range(3)]
    tile = jnp.arange(TILES, dtype=jnp.int32)
    quad, valid = quad_at(me ^ mirrored(tile), live, first_window, second_window)
    window = jnp.where(quad < BLK // QUAD, first_window, second_window)
    low = jnp.maximum(window * BLK, jnp.where(no_prev, TILES * LANES, 0))
    first = (TILES + tile) * LANES + QUAD * quad
    return jnp.stack([valid.astype(jnp.int32), first, jnp.where(valid, low, 2 * TILES * LANES)])


def per_device(locations, times, background, weights, window_start, live):
    sent = pack(window_start, live, locations, times[None], background[None], weights)
    own = lax.all_to_all(sent.reshape(TILES, ROWS // 2, 2, LANES), "grp", 0, 0)
    flat = own.reshape(TILES * ROWS, LANES)
    prev = from_behind(flat, "tm", 1)
    meta = own[:, QUAD_ROW // 2, QUAD_ROW % 2, META_LANE : META_LANE + 3]
    info = plan(meta, lax.axis_index("grp").astype(jnp.int32), lax.axis_index("tm") == 0)
    packed, collected, child_b, child_t, tiles, times_q = own_sums(info, flat)
    part_prev, result, ratio = prev_pairs(info, prev, packed, collected, child_b, child_t)
    back = from_behind(part_prev, "tm", -1)
    part = own_push(info, tiles, times_q, result, ratio, child_b, child_t) + back
    received = lax.all_to_all(part.reshape(TILES, BACK_ROWS, 1, LANES), "grp", 0, 0)
    grad, log_intensity = collect(window_start, live, received.reshape(TILES * BACK_ROWS, LANES))
    return (grad, log_intensity)


def solution(mesh):
    return jax.shard_map(
        per_device,
        mesh=mesh,
        in_specs=(
            P(None, None, ("tm", "grp")),
            P(("tm", "grp")),
            P(("tm", "grp")),
            P(None, ("tm", "grp")),
            P(("tm", "grp")),
            P(("tm", "grp")),
        ),
        out_specs=(P(None, None, ("tm", "grp")), P(None, ("tm", "grp"))),
        check_vma=False,
    )
```

```python
import math

import jax
import jax.numpy as jnp
from jax import lax
from jax.experimental import pallas as pl
from jax.experimental.pallas import tpu as pltpu
from jax.sharding import PartitionSpec as P

offspring = 0.8
fast_rate = 0.125
slow_rate = 0.0009765625

CH = 16
LANES = 128
TILES = 32
BLK = 64
QUAD = 4
SLOTS = 32
DEAD = -1e30

HALF = TILES // 2

TIME_ROW, QUAD_ROW = 2 * CH, 2 * CH + 1
ROWS = 2 * CH + 2
META_LANE = (CH + 1) * QUAD
BACK_ROW, W_ROW = TIME_ROW + 1, 40
VALID, FIRST, LOW = range(3)
LOG_ROW = 2 * CH
BACK_ROWS = LOG_ROW + 1
PLACED = 24

SCALE = math.sqrt(0.5 / math.log(2.0))
UNSCALE = 1.0 / SCALE
LOG2E = 1.0 / math.log(2.0)
LOG2_SLOW = math.log2(offspring * 0.5 * slow_rate / (2.0 * math.pi))


def from_behind(value, axis, by):
    count = lax.axis_size(axis)
    pairs = [(i, i + by) for i in range(count) if 0 <= i + by < count]
    return lax.ppermute(value, axis, pairs)


def log2_time_kernel(delta):
    fast = (fast_rate / slow_rate) * jnp.exp2(delta * (-(fast_rate - slow_rate) * LOG2E))
    return (LOG2_SLOW - delta * (slow_rate * LOG2E)) + jnp.log(1.0 + fast) * LOG2E


def slot_lanes(lane, s):
    return (lane >= QUAD * s) & (lane < QUAD * (s + 1))


def lane_ids():
    return lax.broadcasted_iota(jnp.int32, (1, LANES), 1)


def spread_lanes(out, values):
    rows = values.shape[0]
    for child in range(LANES):
        out[child] = jnp.broadcast_to(values[:, child : child + 1], (rows, LANES))


def gather_lanes(sums):
    lane = lane_ids()
    collected = jnp.zeros(sums.shape[1:], jnp.float32)
    for child in range(LANES):
        collected = jnp.where(lane == child, jnp.sum(sums[child], axis=1, keepdims=True), collected)
    return [collected[j * CH : (j + 1) * CH] for j in range(3)]


def mirrored(tile):
    return ((tile & 1) << 4) | ((tile & 2) << 2) | (tile & 4) | ((tile & 8) >> 2) | ((tile & 16) >> 4)


def deal(live, first_window, second_window):
    quads = [jnp.clip((live - BLK * i + QUAD - 1) // QUAD, 0, BLK // QUAD) for i in range(2)]
    second = (first_window >= second_window).astype(jnp.int32)
    swap = second * (quads[1] - quads[0])
    return second, quads[0] + swap, quads[1] - swap


def quad_at(place, live, first_window, second_window):
    first, ahead, behind = deal(live, first_window, second_window)
    later = (place >= ahead).astype(jnp.int32)
    block = first + later * (1 - 2 * first)
    valid = place < ahead + behind
    return jnp.where(valid, block * (BLK // QUAD) + place - later * ahead, 0), valid


def unpack_tiles(flat, tiles, times_q):
    for q in range(TILES):
        tiles[q] = flat[ROWS * q : ROWS * q + 2 * CH]
        times_q[q : q + 1] = flat[ROWS * q + TIME_ROW : ROWS * q + TIME_ROW + 1]


def time_rows(info, s, log_t, child_t, times_q, own):
    pos = lax.broadcasted_iota(jnp.int32, (TILES, LANES), 0) * LANES + (TILES * LANES if own else 0)
    pos = pos + lax.broadcasted_iota(jnp.int32, (TILES, LANES), 1)
    ok = pos >= info[LOW, s]
    for i in range(QUAD):
        at = QUAD * s + i
        delta = jnp.maximum(child_t[pl.ds(at, 1)] - times_q[...], 0.0)
        allowed = ok & (pos < info[FIRST, s] + i) if own else ok
        log_t[at] = jnp.where(allowed, log2_time_kernel(delta), DEAD)


def kernel_of(tiles, q, child_b, log_t, at):
    dx = tiles[q, 0:CH] - child_b[at, 0:CH]
    dy = tiles[q, CH : 2 * CH] - child_b[at, CH : 2 * CH]
    lt = log_t[at, pl.ds(q, 1), :]
    return jnp.exp2((lt - dx * dx) - dy * dy), dx, dy


def short_steps(start, end, body):
    def once(step, carry):
        body([2 * step, 2 * step + 1])
        return carry

    lax.fori_loop(start, end, once, 0)


def steps(start, end, body):
    count = jnp.maximum(end - start, 0)

    def twice(i, carry):
        tile = 2 * start + 4 * i
        body([tile + u for u in range(4)])
        return carry

    lax.fori_loop(0, count // 2, twice, 0)

    @pl.when(count % 2 == 1)
    def _():
        body([2 * end - 2, 2 * end - 1])


def slot_sums(tiles, s, start, end, child_b, log_t, sums, steps, kern=None):
    def body(qs):
        for i in range(QUAD):
            at = QUAD * s + i
            acc = [sums[at, j * CH : (j + 1) * CH] for j in range(3)]
            for q in qs:
                k, dx, dy = kernel_of(tiles, q, child_b, log_t, at)
                if kern is not None:
                    kern[at, q] = k
                acc = [acc[0] + k, acc[1] + k * dx, acc[2] + k * dy]
            for j in range(3):
                sums[at, j * CH : (j + 1) * CH] = acc[j]

    steps(start, end, body)


def own_steps(info, s):
    return jnp.maximum(info[LOW, s] // (2 * LANES) - HALF, 0), info[FIRST, s] // (2 * LANES) - HALF + 1


def prev_start(info, s):
    return jnp.minimum(info[LOW, s] // (2 * LANES), HALF)


def exact_dot(a, b):
    return jnp.dot(a, b, precision=lax.Precision.HIGHEST, preferred_element_type=jnp.float32)


def square():
    return lax.broadcasted_iota(jnp.int32, (LANES, LANES), 0), lax.broadcasted_iota(jnp.int32, (LANES, LANES), 1)


def rows_of_quads(values):
    wide = jnp.concatenate([values, jnp.zeros((LANES - values.shape[0], LANES), jnp.float32)], axis=0)
    row, lane = square()
    by_lane = exact_dot(jnp.transpose(wide), (lane // QUAD == row).astype(jnp.float32))
    by_lane = jnp.where(lane % QUAD == row % QUAD, by_lane, 0.0)
    slot = lax.broadcasted_iota(jnp.int32, (SLOTS, LANES), 0)
    child = lax.broadcasted_iota(jnp.int32, (SLOTS, LANES), 1)
    return exact_dot((child // QUAD == slot).astype(jnp.float32), by_lane)


def place_quads(rows, source):
    row, lane = square()
    chosen = exact_dot(jnp.transpose(rows), (row == source).astype(jnp.float32))
    chosen = jnp.where(row % QUAD == lane % QUAD, chosen, 0.0)
    chain = lax.broadcasted_iota(jnp.int32, (PLACED, LANES), 0)
    place = lax.broadcasted_iota(jnp.int32, (PLACED, LANES), 1)
    return exact_dot((place // QUAD == chain).astype(jnp.float32), chosen)


def own_sums_kernel(info, flat, packed, sums, child_b, child_t, own, times_q, log_t, quad_rows):
    lane = lane_ids()
    unpack_tiles(flat, own, times_q)
    mine = jnp.zeros((2 * CH, LANES), jnp.float32)
    child_times = jnp.zeros((1, LANES), jnp.float32)
    quad_rows[...] = jnp.zeros((LANES, LANES), jnp.float32)
    for s in range(SLOTS):
        shift = lax.rem(QUAD * s + LANES - lax.rem(info[FIRST, s], LANES), LANES)
        mine = jnp.where(slot_lanes(lane, s), pltpu.roll(own[s], shift, 1), mine)
        child_times = jnp.where(slot_lanes(lane, s), pltpu.roll(times_q[s : s + 1], shift, 1), child_times)
        quad_rows[s : s + 1] = flat[ROWS * s + QUAD_ROW : ROWS * s + QUAD_ROW + 1]
    placed = place_quads(quad_rows[...], lane // QUAD)
    packed[0 : 2 * CH] = mine
    packed[TIME_ROW : TIME_ROW + 1] = child_times
    packed[BACK_ROW : BACK_ROW + 1] = placed[CH : CH + 1]
    packed[W_ROW:] = placed[0:CH]
    spread_lanes(child_b, mine)
    child_t[...] = jnp.transpose(jnp.broadcast_to(child_times, (LANES, LANES)))

    def times(s, carry):
        @pl.when(info[VALID, s] > 0)
        def _():
            time_rows(info, s, log_t, child_t, times_q, True)

        return carry

    lax.fori_loop(0, SLOTS, times, 0)

    def clear(s, carry):
        for i in range(QUAD):
            sums[QUAD * s + i] = jnp.zeros((3 * CH, LANES), jnp.float32)
        return carry

    lax.fori_loop(0, SLOTS, clear, 0)

    def slot(s, carry):
        start, end = own_steps(info, s)
        slot_sums(own, s, start, end, child_b, log_t, sums, steps)
        return carry

    lax.fori_loop(0, SLOTS, slot, 0)


def prev_kernel(
    info, flat, packed, own_sums, child_b, child_t, part, result, ratio_out,
    log_t, kern, sums, total, times_q, prev
):
    unpack_tiles(flat, prev, times_q)

    def times(s, carry):
        @pl.when(info[LOW, s] < TILES * LANES)
        def _():
            time_rows(info, s, log_t, child_t, times_q, False)

        return carry

    lax.fori_loop(0, SLOTS, times, 0)

    def slot(s, carry):
        for i in range(QUAD):
            sums[QUAD * s + i] = own_sums[QUAD * s + i]
        slot_sums(prev, s, prev_start(info, s), HALF, child_b, log_t, sums, short_steps, kern)
        return carry

    lax.fori_loop(0, SLOTS, slot, 0)

    summed, pull_x, pull_y = gather_lanes(sums)
    xs, ys, weights = packed[0:CH], packed[CH : 2 * CH], packed[W_ROW : W_ROW + CH]
    intensity = packed[BACK_ROW : BACK_ROW + 1] + summed
    alive = packed[TIME_ROW : TIME_ROW + 1] >= 0.0
    ratio = weights / intensity
    ratio_out[...] = ratio
    result[0:CH] = ratio * pull_x * UNSCALE
    result[CH : 2 * CH] = ratio * pull_y * UNSCALE
    result[2 * CH :] = jnp.where(alive, jnp.log(intensity), 0.0)
    spread_lanes(sums, jnp.concatenate([ratio, ratio * xs, ratio * ys], axis=0))

    def clear(q, carry):
        total[q] = jnp.zeros((3 * CH, LANES), jnp.float32)
        return carry

    lax.fori_loop(0, TILES, clear, 0)

    def push(s, carry):
        def body(qs):
            for q in qs:
                ks = [kern[QUAD * s + i, q] for i in range(QUAD)]
                for j in range(3):
                    at = slice(j * CH, (j + 1) * CH)
                    add = [ks[i] * sums[QUAD * s + i, at] for i in range(QUAD)]
                    total[q, at] = total[q, at] + ((add[0] + add[1]) + (add[2] + add[3]))

        short_steps(prev_start(info, s), HALF, body)
        return carry

    lax.fori_loop(0, SLOTS, push, 0)

    for q in range(TILES):
        weight = total[q, 0:CH]
        for j in range(2):
            pulled = total[q, (j + 1) * CH : (j + 2) * CH] - prev[q, j * CH : (j + 1) * CH] * weight
            part[BACK_ROWS * q + j * CH : BACK_ROWS * q + (j + 1) * CH] = pulled * UNSCALE
        part[BACK_ROWS * q + LOG_ROW : BACK_ROWS * (q + 1)] = jnp.zeros((1, LANES), jnp.float32)


def own_push_kernel(info, own, times_q, result, ratio, child_b, child_t, flat, log_t, ratio_b, part, slot_logs):
    lane = lane_ids()
    spread_lanes(ratio_b, ratio[...] * -UNSCALE)

    def times(s, carry):
        @pl.when(info[VALID, s] > 0)
        def _():
            time_rows(info, s, log_t, child_t, times_q, True)

        return carry

    lax.fori_loop(0, SLOTS, times, 0)

    def clear(q, carry):
        part[q] = jnp.zeros((2 * CH, LANES), jnp.float32)
        return carry

    lax.fori_loop(0, TILES, clear, 0)

    def slot(s, carry):
        start, end = own_steps(info, s)

        def body(qs):
            for q in qs:
                xs, ys = [], []
                for i in range(QUAD):
                    k, dx, dy = kernel_of(own, q, child_b, log_t, QUAD * s + i)
                    weighted = k * ratio_b[QUAD * s + i]
                    xs.append(weighted * dx)
                    ys.append(weighted * dy)
                part[q, 0:CH] = part[q, 0:CH] + ((xs[0] + xs[1]) + (xs[2] + xs[3]))
                part[q, CH : 2 * CH] = part[q, CH : 2 * CH] + ((ys[0] + ys[1]) + (ys[2] + ys[3]))

        steps(start, end, body)
        return carry

    lax.fori_loop(0, SLOTS, slot, 0)

    slot_logs[...] = rows_of_quads(result[2 * CH :])
    for s in range(SLOTS):
        at = lax.rem(info[FIRST, s], LANES)
        moved = pltpu.roll(result[0 : 2 * CH], lax.rem(at + LANES - QUAD * s, LANES), 1)
        here = (lane >= at) & (lane < at + QUAD)
        at = BACK_ROWS * s
        flat[at : at + 2 * CH] = part[s] + jnp.where(here, moved, 0.0)
        flat[at + LOG_ROW : at + BACK_ROWS] = jnp.where(info[VALID, s] > 0, slot_logs[s : s + 1], 0.0)


def call(kernel, out_rows, scratch, scalars, *operands, mib=8):
    vmem = pl.BlockSpec(memory_space=pltpu.VMEM)
    return pl.pallas_call(
        kernel,
        out_shape=[jax.ShapeDtypeStruct(shape, jnp.float32) for shape in out_rows],
        in_specs=[pl.BlockSpec(memory_space=pltpu.SMEM)] * len(scalars) + [vmem] * len(operands),
        out_specs=[vmem] * len(out_rows),
        scratch_shapes=[pltpu.VMEM(shape, jnp.float32) for shape in scratch],
        compiler_params=pltpu.CompilerParams(vmem_limit_bytes=mib * 2**20),
    )(*scalars, *operands)


TIMES = (TILES, LANES)
XY = (TILES, 2 * CH, LANES)
LOG_T = (LANES, TILES, LANES)
CHILD_B = (LANES, 2 * CH, LANES)
SUMS = (LANES, 3 * CH, LANES)


def pack_kernel(*refs):
    operands, out, scratch, arrived, quad_rows = refs[:6], refs[6], refs[7:13], refs[13], refs[14]
    copies = [pltpu.make_async_copy(operands[i], scratch[i], arrived.at[i]) for i in range(6)]
    for copy in copies:
        copy.start()
    for copy in copies:
        copy.wait()
    window, live, locations, times, background, weights = scratch
    lane = lane_ids()
    alive = lane < live[0]
    meta = jnp.zeros((1, LANES), jnp.float32)
    for i, number in enumerate((live[0], window[0], window[1])):
        meta = jnp.where(lane == META_LANE + i, number.astype(jnp.float32), meta)
    quad_rows[0:SLOTS] = rows_of_quads(jnp.concatenate([jnp.where(alive, weights[...], 0.0), background[...]], axis=0))
    none = ((lane >= CH * QUAD) & (lane < META_LANE)).astype(jnp.float32)
    quad_rows[SLOTS:] = jnp.broadcast_to(none, (8, LANES))
    xs, ys = locations[:, 0, :] * SCALE, locations[:, 1, :] * SCALE
    time = jnp.where(alive, times[...], DEAD)
    turn = mirrored(lax.axis_index("grp"))
    for to in range(TILES):
        at = ROWS * to
        out[at : at + CH] = xs
        out[at + CH : at + 2 * CH] = ys
        out[at + TIME_ROW : at + TIME_ROW + 1] = time
        quad, valid = quad_at(to ^ turn, live[0], window[0], window[1])
        out[at + QUAD_ROW : at + ROWS] = quad_rows[pl.ds(jnp.where(valid, quad, SLOTS), 1)] + meta


def pack(*operands):
    spaces = [pltpu.SMEM] * 2 + [pltpu.VMEM] * 4
    return pl.pallas_call(
        pack_kernel,
        out_shape=jax.ShapeDtypeStruct((TILES * ROWS, LANES), jnp.float32),
        in_specs=[pl.BlockSpec(memory_space=pltpu.HBM)] * 6,
        out_specs=pl.BlockSpec(memory_space=pltpu.VMEM),
        scratch_shapes=[space(x.shape, x.dtype) for space, x in zip(spaces, operands)]
        + [pltpu.SemaphoreType.DMA((6,)), pltpu.VMEM((SLOTS + 8, LANES), jnp.float32)],
        compiler_params=pltpu.CompilerParams(vmem_limit_bytes=60 * 2**20),
    )(*operands)


def collect_kernel(window, live, received, grad, logs, log_rows):
    log_rows[...] = jnp.zeros((LANES, LANES), jnp.float32)
    total = jnp.zeros((2 * CH, LANES), jnp.float32)
    for source in range(TILES):
        at = BACK_ROWS * source
        total = total + received[at : at + 2 * CH]
        log_rows[source : source + 1] = received[at + LOG_ROW : at + BACK_ROWS]
    grad[:, 0, :] = total[0:CH]
    grad[:, 1, :] = total[CH:]
    first, ahead, behind = deal(live[0], window[0], window[1])
    lane = lane_ids()
    quad = (lane % BLK) // QUAD
    sooner = lane // BLK == first
    valid = quad < jnp.where(sooner, ahead, behind)
    place = jnp.where(sooner, quad, quad + ahead)
    source = place ^ mirrored(lax.axis_index("grp"))
    logs[...] = place_quads(log_rows[...], jnp.where(valid, source, -1))[0:CH]


def collect(window, live, received):
    vmem = pl.BlockSpec(memory_space=pltpu.VMEM)
    return pl.pallas_call(
        collect_kernel,
        out_shape=[
            jax.ShapeDtypeStruct((CH, 2, LANES), jnp.float32),
            jax.ShapeDtypeStruct((CH, LANES), jnp.float32),
        ],
        in_specs=[pl.BlockSpec(memory_space=pltpu.SMEM)] * 2 + [vmem],
        out_specs=[vmem] * 2,
        scratch_shapes=[pltpu.VMEM((LANES, LANES), jnp.float32)],
        compiler_params=pltpu.CompilerParams(vmem_limit_bytes=24 * 2**20),
    )(window, live, received)


def own_sums(info, flat):
    return call(
        own_sums_kernel,
        [(W_ROW + CH, LANES), SUMS, CHILD_B, (LANES, LANES), XY, TIMES],
        [LOG_T, (LANES, LANES)],
        (info,), flat,
    )


def prev_pairs(info, *operands):
    return call(
        prev_kernel,
        [(TILES * BACK_ROWS, LANES), (3 * CH, LANES), (CH, LANES)],
        [LOG_T, (LANES, TILES, CH, LANES), SUMS, (TILES, 3 * CH, LANES), TIMES, XY],
        (info,), *operands, mib=42,
    )


def own_push(info, *operands):
    return call(
        own_push_kernel,
        [(TILES * BACK_ROWS, LANES)],
        [LOG_T, (LANES, CH, LANES), XY, (SLOTS, LANES)],
        (info,), *operands,
    )[0]


def plan(meta, me, no_prev):
    live, first_window, second_window = [meta[:, i].astype(jnp.int32) for i in range(3)]
    tile = jnp.arange(TILES, dtype=jnp.int32)
    quad, valid = quad_at(me ^ mirrored(tile), live, first_window, second_window)
    window = jnp.where(quad < BLK // QUAD, first_window, second_window)
    low = jnp.maximum(window * BLK, jnp.where(no_prev, TILES * LANES, 0))
    first = (TILES + tile) * LANES + QUAD * quad
    return jnp.stack([valid.astype(jnp.int32), first, jnp.where(valid, low, 2 * TILES * LANES)])


def per_device(locations, times, background, weights, window_start, live):
    sent = pack(window_start, live, locations, times[None], background[None], weights)
    own = lax.all_to_all(sent.reshape(TILES, ROWS // 2, 2, LANES), "grp", 0, 0)
    flat = own.reshape(TILES * ROWS, LANES)
    prev = from_behind(flat, "tm", 1)
    meta = own[:, QUAD_ROW // 2, QUAD_ROW % 2, META_LANE : META_LANE + 3]
    info = plan(meta, lax.axis_index("grp").astype(jnp.int32), lax.axis_index("tm") == 0)
    packed, sums, child_b, child_t, tiles, times_q = own_sums(info, flat)
    part_prev, result, ratio = prev_pairs(info, prev, packed, sums, child_b, child_t)
    back = from_behind(part_prev, "tm", -1)
    part = own_push(info, tiles, times_q, result, ratio, child_b, child_t) + back
    received = lax.all_to_all(part.reshape(TILES, BACK_ROWS, 1, LANES), "grp", 0, 0)
    grad, log_intensity = collect(window_start, live, received.reshape(TILES * BACK_ROWS, LANES))
    return (grad, log_intensity)


def solution(mesh):
    return jax.shard_map(
        per_device,
        mesh=mesh,
        in_specs=(
            P(None, None, ("tm", "grp")),
            P(("tm", "grp")),
            P(("tm", "grp")),
            P(None, ("tm", "grp")),
            P(("tm", "grp")),
            P(("tm", "grp")),
        ),
        out_specs=(P(None, None, ("tm", "grp")), P(None, ("tm", "grp"))),
        check_vma=False,
    )
```

```python
import math

import jax
import jax.numpy as jnp
from jax import lax
from jax.experimental import pallas as pl
from jax.experimental.pallas import tpu as pltpu
from jax.sharding import PartitionSpec as P

offspring = 0.8
fast_rate = 0.125
slow_rate = 0.0009765625

CH = 16
LANES = 128
TILES = 32
BLK = 64
QUAD = 4
SLOTS = 32
DEAD = -1e30

HALF = TILES // 2

TIME_ROW, QUAD_ROW = 2 * CH, 2 * CH + 1
ROWS = 2 * CH + 2
META_LANE = (CH + 1) * QUAD
BACK_ROW, W_ROW = TIME_ROW + 1, 40
VALID, FIRST, LOW = range(3)
LOG_ROW = 2 * CH
BACK_ROWS = LOG_ROW + 1
PLACED = 24

SCALE = math.sqrt(0.5 / math.log(2.0))
UNSCALE = 1.0 / SCALE
LOG2E = 1.0 / math.log(2.0)
LOG2_SLOW = math.log2(offspring * 0.5 * slow_rate / (2.0 * math.pi))


def from_behind(value, axis, by):
    count = lax.axis_size(axis)
    pairs = [(i, i + by) for i in range(count) if 0 <= i + by < count]
    return lax.ppermute(value, axis, pairs)


def log2_time_kernel(delta):
    fast = (fast_rate / slow_rate) * jnp.exp2(delta * (-(fast_rate - slow_rate) * LOG2E))
    return (LOG2_SLOW - delta * (slow_rate * LOG2E)) + jnp.log(1.0 + fast) * LOG2E


def slot_lanes(lane, s):
    return (lane >= QUAD * s) & (lane < QUAD * (s + 1))


def lane_ids():
    return lax.broadcasted_iota(jnp.int32, (1, LANES), 1)


def spread_lanes(out, values):
    rows = values.shape[0]
    for child in range(LANES):
        out[child] = jnp.broadcast_to(values[:, child : child + 1], (rows, LANES))


def gather_lanes(sums):
    lane = lane_ids()
    collected = jnp.zeros(sums.shape[1:], jnp.float32)
    for child in range(LANES):
        collected = jnp.where(lane == child, jnp.sum(sums[child], axis=1, keepdims=True), collected)
    return [collected[j * CH : (j + 1) * CH] for j in range(3)]


def mirrored(tile):
    return ((tile & 1) << 4) | ((tile & 2) << 2) | (tile & 4) | ((tile & 8) >> 2) | ((tile & 16) >> 4)


def deal(live, first_window, second_window):
    quads = [jnp.clip((live - BLK * i + QUAD - 1) // QUAD, 0, BLK // QUAD) for i in range(2)]
    second = (first_window >= second_window).astype(jnp.int32)
    swap = second * (quads[1] - quads[0])
    return second, quads[0] + swap, quads[1] - swap


def quad_at(place, live, first_window, second_window):
    first, ahead, behind = deal(live, first_window, second_window)
    later = (place >= ahead).astype(jnp.int32)
    block = first + later * (1 - 2 * first)
    valid = place < ahead + behind
    return jnp.where(valid, block * (BLK // QUAD) + place - later * ahead, 0), valid


def unpack_tiles(flat, tiles, times_q):
    for q in range(TILES):
        tiles[q] = flat[ROWS * q : ROWS * q + 2 * CH]
        times_q[q : q + 1] = flat[ROWS * q + TIME_ROW : ROWS * q + TIME_ROW + 1]


def time_rows(info, s, log_t, child_t, times_q, own):
    pos = lax.broadcasted_iota(jnp.int32, (TILES, LANES), 0) * LANES + (TILES * LANES if own else 0)
    pos = pos + lax.broadcasted_iota(jnp.int32, (TILES, LANES), 1)
    ok = pos >= info[LOW, s]
    for i in range(QUAD):
        at = QUAD * s + i
        delta = jnp.maximum(child_t[pl.ds(at, 1)] - times_q[...], 0.0)
        allowed = ok & (pos < info[FIRST, s] + i) if own else ok
        log_t[at] = jnp.where(allowed, log2_time_kernel(delta), DEAD)


def kernel_of(tiles, q, child_b, log_t, at):
    dx = tiles[q, 0:CH] - child_b[at, 0:CH]
    dy = tiles[q, CH : 2 * CH] - child_b[at, CH : 2 * CH]
    lt = log_t[at, pl.ds(q, 1), :]
    return jnp.exp2((lt - dx * dx) - dy * dy), dx, dy


def short_steps(start, end, body):
    def once(step, carry):
        body([2 * step, 2 * step + 1])
        return carry

    lax.fori_loop(start, end, once, 0)


def steps(start, end, body):
    count = jnp.maximum(end - start, 0)

    def twice(i, carry):
        tile = 2 * start + 4 * i
        body([tile + u for u in range(4)])
        return carry

    lax.fori_loop(0, count // 2, twice, 0)

    @pl.when(count % 2 == 1)
    def _():
        body([2 * end - 2, 2 * end - 1])


def slot_sums(tiles, s, start, end, child_b, log_t, sums, steps, kern=None):
    def body(qs):
        for i in range(QUAD):
            at = QUAD * s + i
            acc = [sums[at, j * CH : (j + 1) * CH] for j in range(3)]
            for q in qs:
                k, dx, dy = kernel_of(tiles, q, child_b, log_t, at)
                if kern is not None:
                    kern[at, q] = k
                acc = [acc[0] + k, acc[1] + k * dx, acc[2] + k * dy]
            for j in range(3):
                sums[at, j * CH : (j + 1) * CH] = acc[j]

    steps(start, end, body)


def own_steps(info, s):
    return jnp.maximum(info[LOW, s] // (2 * LANES) - HALF, 0), info[FIRST, s] // (2 * LANES) - HALF + 1


def prev_start(info, s):
    return jnp.minimum(info[LOW, s] // (2 * LANES), HALF)


def exact_dot(a, b):
    return jnp.dot(a, b, precision=lax.Precision.HIGHEST, preferred_element_type=jnp.float32)


def square():
    return lax.broadcasted_iota(jnp.int32, (LANES, LANES), 0), lax.broadcasted_iota(jnp.int32, (LANES, LANES), 1)


def rows_of_quads(values):
    wide = jnp.concatenate([values, jnp.zeros((LANES - values.shape[0], LANES), jnp.float32)], axis=0)
    row, lane = square()
    by_lane = exact_dot(jnp.transpose(wide), (lane // QUAD == row).astype(jnp.float32))
    by_lane = jnp.where(lane % QUAD == row % QUAD, by_lane, 0.0)
    slot = lax.broadcasted_iota(jnp.int32, (SLOTS, LANES), 0)
    child = lax.broadcasted_iota(jnp.int32, (SLOTS, LANES), 1)
    return exact_dot((child // QUAD == slot).astype(jnp.float32), by_lane)


def place_quads(rows, source):
    row, lane = square()
    chosen = exact_dot(jnp.transpose(rows), (row == source).astype(jnp.float32))
    chosen = jnp.where(row % QUAD == lane % QUAD, chosen, 0.0)
    chain = lax.broadcasted_iota(jnp.int32, (PLACED, LANES), 0)
    place = lax.broadcasted_iota(jnp.int32, (PLACED, LANES), 1)
    return exact_dot((place // QUAD == chain).astype(jnp.float32), chosen)


def own_sums_kernel(info, flat, packed, sums, child_b, child_t, own, log_t, times_q, quad_rows):
    lane = lane_ids()
    unpack_tiles(flat, own, times_q)
    mine = jnp.zeros((2 * CH, LANES), jnp.float32)
    child_times = jnp.zeros((1, LANES), jnp.float32)
    quad_rows[...] = jnp.zeros((LANES, LANES), jnp.float32)
    for s in range(SLOTS):
        shift = lax.rem(QUAD * s + LANES - lax.rem(info[FIRST, s], LANES), LANES)
        mine = jnp.where(slot_lanes(lane, s), pltpu.roll(own[s], shift, 1), mine)
        child_times = jnp.where(slot_lanes(lane, s), pltpu.roll(times_q[s : s + 1], shift, 1), child_times)
        quad_rows[s : s + 1] = flat[ROWS * s + QUAD_ROW : ROWS * s + QUAD_ROW + 1]
    placed = place_quads(quad_rows[...], lane // QUAD)
    packed[0 : 2 * CH] = mine
    packed[TIME_ROW : TIME_ROW + 1] = child_times
    packed[BACK_ROW : BACK_ROW + 1] = placed[CH : CH + 1]
    packed[W_ROW:] = placed[0:CH]
    spread_lanes(child_b, mine)
    child_t[...] = jnp.transpose(jnp.broadcast_to(child_times, (LANES, LANES)))

    def times(s, carry):
        @pl.when(info[VALID, s] > 0)
        def _():
            time_rows(info, s, log_t, child_t, times_q, True)

        return carry

    lax.fori_loop(0, SLOTS, times, 0)

    def clear(s, carry):
        for i in range(QUAD):
            sums[QUAD * s + i] = jnp.zeros((3 * CH, LANES), jnp.float32)
        return carry

    lax.fori_loop(0, SLOTS, clear, 0)

    def slot(s, carry):
        start, end = own_steps(info, s)
        slot_sums(own, s, start, end, child_b, log_t, sums, steps)
        return carry

    lax.fori_loop(0, SLOTS, slot, 0)


def prev_kernel(
    info, flat, packed, own_sums, child_b, child_t, part, result, ratio_out,
    log_t, kern, sums, total, times_q, prev
):
    unpack_tiles(flat, prev, times_q)

    def times(s, carry):
        @pl.when(info[LOW, s] < TILES * LANES)
        def _():
            time_rows(info, s, log_t, child_t, times_q, False)

        return carry

    lax.fori_loop(0, SLOTS, times, 0)

    def slot(s, carry):
        for i in range(QUAD):
            sums[QUAD * s + i] = own_sums[QUAD * s + i]
        slot_sums(prev, s, prev_start(info, s), HALF, child_b, log_t, sums, short_steps, kern)
        return carry

    lax.fori_loop(0, SLOTS, slot, 0)

    summed, pull_x, pull_y = gather_lanes(sums)
    xs, ys, weights = packed[0:CH], packed[CH : 2 * CH], packed[W_ROW : W_ROW + CH]
    intensity = packed[BACK_ROW : BACK_ROW + 1] + summed
    alive = packed[TIME_ROW : TIME_ROW + 1] >= 0.0
    ratio = weights / intensity
    ratio_out[...] = ratio
    result[0:CH] = ratio * pull_x * UNSCALE
    result[CH : 2 * CH] = ratio * pull_y * UNSCALE
    result[2 * CH :] = jnp.where(alive, jnp.log(intensity), 0.0)
    spread_lanes(sums, jnp.concatenate([ratio, ratio * xs, ratio * ys], axis=0))

    def clear(q, carry):
        total[q] = jnp.zeros((3 * CH, LANES), jnp.float32)
        return carry

    lax.fori_loop(0, TILES, clear, 0)

    def push(s, carry):
        def body(qs):
            for q in qs:
                ks = [kern[QUAD * s + i, q] for i in range(QUAD)]
                for j in range(3):
                    at = slice(j * CH, (j + 1) * CH)
                    add = [ks[i] * sums[QUAD * s + i, at] for i in range(QUAD)]
                    total[q, at] = total[q, at] + ((add[0] + add[1]) + (add[2] + add[3]))

        short_steps(prev_start(info, s), HALF, body)
        return carry

    lax.fori_loop(0, SLOTS, push, 0)

    for q in range(TILES):
        weight = total[q, 0:CH]
        for j in range(2):
            pulled = total[q, (j + 1) * CH : (j + 2) * CH] - prev[q, j * CH : (j + 1) * CH] * weight
            part[BACK_ROWS * q + j * CH : BACK_ROWS * q + (j + 1) * CH] = pulled * UNSCALE
        part[BACK_ROWS * q + LOG_ROW : BACK_ROWS * (q + 1)] = jnp.zeros((1, LANES), jnp.float32)


def own_push_kernel(info, own, log_t, result, ratio, child_b, flat, ratio_b, part, slot_logs):
    lane = lane_ids()
    spread_lanes(ratio_b, ratio[...] * -UNSCALE)

    def clear(q, carry):
        part[q] = jnp.zeros((2 * CH, LANES), jnp.float32)
        return carry

    lax.fori_loop(0, TILES, clear, 0)

    def slot(s, carry):
        start, end = own_steps(info, s)

        def body(qs):
            for q in qs:
                xs, ys = [], []
                for i in range(QUAD):
                    k, dx, dy = kernel_of(own, q, child_b, log_t, QUAD * s + i)
                    weighted = k * ratio_b[QUAD * s + i]
                    xs.append(weighted * dx)
                    ys.append(weighted * dy)
                part[q, 0:CH] = part[q, 0:CH] + ((xs[0] + xs[1]) + (xs[2] + xs[3]))
                part[q, CH : 2 * CH] = part[q, CH : 2 * CH] + ((ys[0] + ys[1]) + (ys[2] + ys[3]))

        steps(start, end, body)
        return carry

    lax.fori_loop(0, SLOTS, slot, 0)

    slot_logs[...] = rows_of_quads(result[2 * CH :])
    for s in range(SLOTS):
        at = lax.rem(info[FIRST, s], LANES)
        moved = pltpu.roll(result[0 : 2 * CH], lax.rem(at + LANES - QUAD * s, LANES), 1)
        here = (lane >= at) & (lane < at + QUAD)
        at = BACK_ROWS * s
        flat[at : at + 2 * CH] = part[s] + jnp.where(here, moved, 0.0)
        flat[at + LOG_ROW : at + BACK_ROWS] = jnp.where(info[VALID, s] > 0, slot_logs[s : s + 1], 0.0)


def call(kernel, out_rows, scratch, scalars, *operands, mib=8):
    vmem = pl.BlockSpec(memory_space=pltpu.VMEM)
    return pl.pallas_call(
        kernel,
        out_shape=[jax.ShapeDtypeStruct(shape, jnp.float32) for shape in out_rows],
        in_specs=[pl.BlockSpec(memory_space=pltpu.SMEM)] * len(scalars) + [vmem] * len(operands),
        out_specs=[vmem] * len(out_rows),
        scratch_shapes=[pltpu.VMEM(shape, jnp.float32) for shape in scratch],
        compiler_params=pltpu.CompilerParams(vmem_limit_bytes=mib * 2**20),
    )(*scalars, *operands)


TIMES = (TILES, LANES)
XY = (TILES, 2 * CH, LANES)
LOG_T = (LANES, TILES, LANES)
CHILD_B = (LANES, 2 * CH, LANES)
SUMS = (LANES, 3 * CH, LANES)


def pack_kernel(*refs):
    operands, out, source, scratch, arrived, quad_rows = refs[:6], refs[6], refs[7], refs[8:14], refs[14], refs[15]
    copies = [pltpu.make_async_copy(operands[i], scratch[i], arrived.at[i]) for i in range(6)]
    for copy in copies:
        copy.start()
    for copy in copies:
        copy.wait()
    window, live, locations, times, background, weights = scratch
    lane = lane_ids()
    alive = lane < live[0]
    meta = jnp.zeros((1, LANES), jnp.float32)
    for i, number in enumerate((live[0], window[0], window[1])):
        meta = jnp.where(lane == META_LANE + i, number.astype(jnp.float32), meta)
    quad_rows[0:SLOTS] = rows_of_quads(jnp.concatenate([jnp.where(alive, weights[...], 0.0), background[...]], axis=0))
    none = ((lane >= CH * QUAD) & (lane < META_LANE)).astype(jnp.float32)
    quad_rows[SLOTS:] = jnp.broadcast_to(none, (8, LANES))
    xs, ys = locations[:, 0, :] * SCALE, locations[:, 1, :] * SCALE
    time = jnp.where(alive, times[...], DEAD)
    turn = mirrored(lax.axis_index("grp"))
    for to in range(TILES):
        at = ROWS * to
        out[at : at + CH] = xs
        out[at + CH : at + 2 * CH] = ys
        out[at + TIME_ROW : at + TIME_ROW + 1] = time
        quad, valid = quad_at(to ^ turn, live[0], window[0], window[1])
        out[at + QUAD_ROW : at + ROWS] = quad_rows[pl.ds(jnp.where(valid, quad, SLOTS), 1)] + meta
    first, ahead, behind = deal(live[0], window[0], window[1])
    quad = (lane % BLK) // QUAD
    sooner = lane // BLK == first
    valid = quad < jnp.where(sooner, ahead, behind)
    dealt = jnp.where(valid, jnp.where(sooner, quad, quad + ahead) ^ turn, -1)
    source[...] = jnp.broadcast_to(dealt, (8, LANES))


def pack(*operands):
    spaces = [pltpu.SMEM] * 2 + [pltpu.VMEM] * 4
    return pl.pallas_call(
        pack_kernel,
        out_shape=[
            jax.ShapeDtypeStruct((TILES * ROWS, LANES), jnp.float32),
            jax.ShapeDtypeStruct((8, LANES), jnp.int32),
        ],
        in_specs=[pl.BlockSpec(memory_space=pltpu.HBM)] * 6,
        out_specs=[pl.BlockSpec(memory_space=pltpu.VMEM)] * 2,
        scratch_shapes=[space(x.shape, x.dtype) for space, x in zip(spaces, operands)]
        + [pltpu.SemaphoreType.DMA((6,)), pltpu.VMEM((SLOTS + 8, LANES), jnp.float32)],
        compiler_params=pltpu.CompilerParams(vmem_limit_bytes=60 * 2**20),
    )(*operands)


def collect_kernel(dealt, received, grad, logs, log_rows):
    log_rows[...] = jnp.zeros((LANES, LANES), jnp.float32)
    total = jnp.zeros((2 * CH, LANES), jnp.float32)
    for source in range(TILES):
        at = BACK_ROWS * source
        total = total + received[at : at + 2 * CH]
        log_rows[source : source + 1] = received[at + LOG_ROW : at + BACK_ROWS]
    grad[:, 0, :] = total[0:CH]
    grad[:, 1, :] = total[CH:]
    logs[...] = place_quads(log_rows[...], dealt[0:1])[0:CH]


def collect(dealt, received):
    vmem = pl.BlockSpec(memory_space=pltpu.VMEM)
    return pl.pallas_call(
        collect_kernel,
        out_shape=[
            jax.ShapeDtypeStruct((CH, 2, LANES), jnp.float32),
            jax.ShapeDtypeStruct((CH, LANES), jnp.float32),
        ],
        in_specs=[vmem] * 2,
        out_specs=[vmem] * 2,
        scratch_shapes=[pltpu.VMEM((LANES, LANES), jnp.float32)],
        compiler_params=pltpu.CompilerParams(vmem_limit_bytes=24 * 2**20),
    )(dealt, received)


def own_sums(info, flat):
    return call(
        own_sums_kernel,
        [(W_ROW + CH, LANES), SUMS, CHILD_B, (LANES, LANES), XY, LOG_T],
        [TIMES, (LANES, LANES)],
        (info,), flat,
    )


def prev_pairs(info, *operands):
    return call(
        prev_kernel,
        [(TILES * BACK_ROWS, LANES), (3 * CH, LANES), (CH, LANES)],
        [LOG_T, (LANES, TILES, CH, LANES), SUMS, (TILES, 3 * CH, LANES), TIMES, XY],
        (info,), *operands, mib=42,
    )


def own_push(info, *operands):
    return call(
        own_push_kernel,
        [(TILES * BACK_ROWS, LANES)],
        [(LANES, CH, LANES), XY, (SLOTS, LANES)],
        (info,), *operands,
    )[0]


def plan(meta, me, no_prev):
    live, first_window, second_window = [meta[:, i].astype(jnp.int32) for i in range(3)]
    tile = jnp.arange(TILES, dtype=jnp.int32)
    quad, valid = quad_at(me ^ mirrored(tile), live, first_window, second_window)
    window = jnp.where(quad < BLK // QUAD, first_window, second_window)
    low = jnp.maximum(window * BLK, jnp.where(no_prev, TILES * LANES, 0))
    first = (TILES + tile) * LANES + QUAD * quad
    return jnp.stack([valid.astype(jnp.int32), first, jnp.where(valid, low, 2 * TILES * LANES)])


def per_device(locations, times, background, weights, window_start, live):
    sent, dealt = pack(window_start, live, locations, times[None], background[None], weights)
    own = lax.all_to_all(sent.reshape(TILES, ROWS // 2, 2, LANES), "grp", 0, 0)
    flat = own.reshape(TILES * ROWS, LANES)
    prev = from_behind(flat, "tm", 1)
    meta = own[:, QUAD_ROW // 2, QUAD_ROW % 2, META_LANE : META_LANE + 3]
    info = plan(meta, lax.axis_index("grp").astype(jnp.int32), lax.axis_index("tm") == 0)
    packed, sums, child_b, child_t, tiles, log_t = own_sums(info, flat)
    part_prev, result, ratio = prev_pairs(info, prev, packed, sums, child_b, child_t)
    back = from_behind(part_prev, "tm", -1)
    part = own_push(info, tiles, log_t, result, ratio, child_b) + back
    received = lax.all_to_all(part.reshape(TILES, BACK_ROWS, 1, LANES), "grp", 0, 0)
    grad, log_intensity = collect(dealt, received.reshape(TILES * BACK_ROWS, LANES))
    return (grad, log_intensity)


def solution(mesh):
    return jax.shard_map(
        per_device,
        mesh=mesh,
        in_specs=(
            P(None, None, ("tm", "grp")),
            P(("tm", "grp")),
            P(("tm", "grp")),
            P(None, ("tm", "grp")),
            P(("tm", "grp")),
            P(("tm", "grp")),
        ),
        out_specs=(P(None, None, ("tm", "grp")), P(None, ("tm", "grp"))),
        check_vma=False,
    )
```

```python
import math

import jax
import jax.numpy as jnp
from jax import lax
from jax.experimental import pallas as pl
from jax.experimental.pallas import tpu as pltpu
from jax.sharding import PartitionSpec as P

offspring = 0.8
fast_rate = 0.125
slow_rate = 0.0009765625

CH = 16
LANES = 128
TILES = 32
BLK = 64
QUAD = 4
SLOTS = 32
DEAD = -1e30

HALF = TILES // 2

TIME_ROW, QUAD_ROW = 2 * CH, 2 * CH + 1
ROWS = 2 * CH + 2
META_LANE = (CH + 1) * QUAD
BACK_ROW, W_ROW = TIME_ROW + 1, 40
VALID, FIRST, LOW = range(3)
LOG_ROW = 2 * CH
BACK_ROWS = LOG_ROW + 1
PLACED = 24

SCALE = math.sqrt(0.5 / math.log(2.0))
UNSCALE = 1.0 / SCALE
LOG2E = 1.0 / math.log(2.0)
LOG2_SLOW = math.log2(offspring * 0.5 * slow_rate / (2.0 * math.pi))


def from_behind(value, axis, by):
    count = lax.axis_size(axis)
    pairs = [(i, i + by) for i in range(count) if 0 <= i + by < count]
    return lax.ppermute(value, axis, pairs)


def log2_time_kernel(delta):
    fast = (fast_rate / slow_rate) * jnp.exp2(delta * (-(fast_rate - slow_rate) * LOG2E))
    return (LOG2_SLOW - delta * (slow_rate * LOG2E)) + jnp.log(1.0 + fast) * LOG2E


def slot_lanes(lane, s):
    return (lane >= QUAD * s) & (lane < QUAD * (s + 1))


def lane_ids():
    return lax.broadcasted_iota(jnp.int32, (1, LANES), 1)


def spread_lanes(out, values):
    rows = values.shape[0]
    for child in range(LANES):
        out[child] = jnp.broadcast_to(values[:, child : child + 1], (rows, LANES))


def gather_lanes(sums, rows):
    lane = lane_ids()
    collected = jnp.zeros((rows.stop - rows.start, LANES), jnp.float32)
    for child in range(LANES):
        collected = jnp.where(lane == child, jnp.sum(sums[child, rows], axis=1, keepdims=True), collected)
    return collected


def mirrored(tile):
    return ((tile & 1) << 4) | ((tile & 2) << 2) | (tile & 4) | ((tile & 8) >> 2) | ((tile & 16) >> 4)


def deal(live, first_window, second_window):
    quads = [jnp.clip((live - BLK * i + QUAD - 1) // QUAD, 0, BLK // QUAD) for i in range(2)]
    second = (first_window >= second_window).astype(jnp.int32)
    swap = second * (quads[1] - quads[0])
    return second, quads[0] + swap, quads[1] - swap


def quad_at(place, live, first_window, second_window):
    first, ahead, behind = deal(live, first_window, second_window)
    later = (place >= ahead).astype(jnp.int32)
    block = first + later * (1 - 2 * first)
    valid = place < ahead + behind
    return jnp.where(valid, block * (BLK // QUAD) + place - later * ahead, 0), valid


def unpack_tiles(flat, tiles, times_q):
    for q in range(TILES):
        tiles[q] = flat[ROWS * q : ROWS * q + 2 * CH]
        times_q[q : q + 1] = flat[ROWS * q + TIME_ROW : ROWS * q + TIME_ROW + 1]


def time_rows(info, s, log_t, child_t, times_q, own):
    pos = lax.broadcasted_iota(jnp.int32, (TILES, LANES), 0) * LANES + (TILES * LANES if own else 0)
    pos = pos + lax.broadcasted_iota(jnp.int32, (TILES, LANES), 1)
    ok = pos >= info[LOW, s]
    for i in range(QUAD):
        at = QUAD * s + i
        delta = jnp.maximum(child_t[pl.ds(at, 1)] - times_q[...], 0.0)
        allowed = ok & (pos < info[FIRST, s] + i) if own else ok
        log_t[at] = jnp.where(allowed, log2_time_kernel(delta), DEAD)


def kernel_of(tiles, q, child_b, log_t, at):
    dx = tiles[q, 0:CH] - child_b[at, 0:CH]
    dy = tiles[q, CH : 2 * CH] - child_b[at, CH : 2 * CH]
    lt = log_t[at, pl.ds(q, 1), :]
    return jnp.exp2((lt - dx * dx) - dy * dy), dx, dy


def short_steps(start, end, body):
    def once(step, carry):
        body([2 * step, 2 * step + 1])
        return carry

    lax.fori_loop(start, end, once, 0)


def steps(start, end, body):
    count = jnp.maximum(end - start, 0)

    def twice(i, carry):
        tile = 2 * start + 4 * i
        body([tile + u for u in range(4)])
        return carry

    lax.fori_loop(0, count // 2, twice, 0)

    @pl.when(count % 2 == 1)
    def _():
        body([2 * end - 2, 2 * end - 1])


def slot_sums(tiles, s, start, end, child_b, log_t, sums, steps, kern=None):
    def body(qs):
        for i in range(QUAD):
            at = QUAD * s + i
            acc = [sums[at, j * CH : (j + 1) * CH] for j in range(3)]
            for q in qs:
                k, dx, dy = kernel_of(tiles, q, child_b, log_t, at)
                if kern is not None:
                    kern[at, q] = k
                acc = [acc[0] + k, acc[1] + k * dx, acc[2] + k * dy]
            for j in range(3):
                sums[at, j * CH : (j + 1) * CH] = acc[j]

    steps(start, end, body)


def own_steps(info, s):
    return jnp.maximum(info[LOW, s] // (2 * LANES) - HALF, 0), info[FIRST, s] // (2 * LANES) - HALF + 1


def prev_start(info, s):
    return jnp.minimum(info[LOW, s] // (2 * LANES), HALF)


def exact_dot(a, b):
    return jnp.dot(a, b, precision=lax.Precision.HIGHEST, preferred_element_type=jnp.float32)


def square():
    return lax.broadcasted_iota(jnp.int32, (LANES, LANES), 0), lax.broadcasted_iota(jnp.int32, (LANES, LANES), 1)


def rows_of_quads(values):
    wide = jnp.concatenate([values, jnp.zeros((LANES - values.shape[0], LANES), jnp.float32)], axis=0)
    row, lane = square()
    by_lane = exact_dot(jnp.transpose(wide), (lane // QUAD == row).astype(jnp.float32))
    by_lane = jnp.where(lane % QUAD == row % QUAD, by_lane, 0.0)
    slot = lax.broadcasted_iota(jnp.int32, (SLOTS, LANES), 0)
    child = lax.broadcasted_iota(jnp.int32, (SLOTS, LANES), 1)
    return exact_dot((child // QUAD == slot).astype(jnp.float32), by_lane)


def place_quads(rows, source):
    row, lane = square()
    chosen = exact_dot(jnp.transpose(rows), (row == source).astype(jnp.float32))
    chosen = jnp.where(row % QUAD == lane % QUAD, chosen, 0.0)
    chain = lax.broadcasted_iota(jnp.int32, (PLACED, LANES), 0)
    place = lax.broadcasted_iota(jnp.int32, (PLACED, LANES), 1)
    return exact_dot((place // QUAD == chain).astype(jnp.float32), chosen)


def own_sums_kernel(info, flat, packed, sums, child_b, child_t, own, log_t, times_q, quad_rows):
    lane = lane_ids()
    unpack_tiles(flat, own, times_q)
    mine = jnp.zeros((2 * CH, LANES), jnp.float32)
    child_times = jnp.zeros((1, LANES), jnp.float32)
    quad_rows[...] = jnp.zeros((LANES, LANES), jnp.float32)
    for s in range(SLOTS):
        shift = lax.rem(QUAD * s + LANES - lax.rem(info[FIRST, s], LANES), LANES)
        mine = jnp.where(slot_lanes(lane, s), pltpu.roll(own[s], shift, 1), mine)
        child_times = jnp.where(slot_lanes(lane, s), pltpu.roll(times_q[s : s + 1], shift, 1), child_times)
        quad_rows[s : s + 1] = flat[ROWS * s + QUAD_ROW : ROWS * s + QUAD_ROW + 1]
    placed = place_quads(quad_rows[...], lane // QUAD)
    packed[0 : 2 * CH] = mine
    packed[TIME_ROW : TIME_ROW + 1] = child_times
    packed[BACK_ROW : BACK_ROW + 1] = placed[CH : CH + 1]
    packed[W_ROW:] = placed[0:CH]
    spread_lanes(child_b, mine)
    child_t[...] = jnp.transpose(jnp.broadcast_to(child_times, (LANES, LANES)))

    def times(s, carry):
        @pl.when(info[VALID, s] > 0)
        def _():
            time_rows(info, s, log_t, child_t, times_q, True)

        return carry

    lax.fori_loop(0, SLOTS, times, 0)

    def clear(s, carry):
        for i in range(QUAD):
            sums[QUAD * s + i] = jnp.zeros((3 * CH, LANES), jnp.float32)
        return carry

    lax.fori_loop(0, SLOTS, clear, 0)

    def slot(s, carry):
        start, end = own_steps(info, s)
        slot_sums(own, s, start, end, child_b, log_t, sums, steps)
        return carry

    lax.fori_loop(0, SLOTS, slot, 0)


def prev_kernel(
    info, flat, packed, own_sums, child_b, child_t, part, logs, ratio_out, sums,
    log_t, kern, terms, total, times_q, prev
):
    unpack_tiles(flat, prev, times_q)

    def times(s, carry):
        @pl.when(info[LOW, s] < TILES * LANES)
        def _():
            time_rows(info, s, log_t, child_t, times_q, False)

        return carry

    lax.fori_loop(0, SLOTS, times, 0)

    def slot(s, carry):
        for i in range(QUAD):
            sums[QUAD * s + i] = own_sums[QUAD * s + i]
        slot_sums(prev, s, prev_start(info, s), HALF, child_b, log_t, sums, short_steps, kern)
        return carry

    lax.fori_loop(0, SLOTS, slot, 0)

    summed = gather_lanes(sums, slice(0, CH))
    xs, ys, weights = packed[0:CH], packed[CH : 2 * CH], packed[W_ROW : W_ROW + CH]
    intensity = packed[BACK_ROW : BACK_ROW + 1] + summed
    alive = packed[TIME_ROW : TIME_ROW + 1] >= 0.0
    ratio = weights / intensity
    ratio_out[...] = ratio
    logs[...] = jnp.where(alive, jnp.log(intensity), 0.0)
    spread_lanes(terms, jnp.concatenate([ratio, ratio * xs, ratio * ys], axis=0))

    def clear(q, carry):
        total[q] = jnp.zeros((3 * CH, LANES), jnp.float32)
        return carry

    lax.fori_loop(0, TILES, clear, 0)

    def push(s, carry):
        def body(qs):
            for q in qs:
                ks = [kern[QUAD * s + i, q] for i in range(QUAD)]
                for j in range(3):
                    at = slice(j * CH, (j + 1) * CH)
                    add = [ks[i] * terms[QUAD * s + i, at] for i in range(QUAD)]
                    total[q, at] = total[q, at] + ((add[0] + add[1]) + (add[2] + add[3]))

        short_steps(prev_start(info, s), HALF, body)
        return carry

    lax.fori_loop(0, SLOTS, push, 0)

    for q in range(TILES):
        weight = total[q, 0:CH]
        for j in range(2):
            pulled = total[q, (j + 1) * CH : (j + 2) * CH] - prev[q, j * CH : (j + 1) * CH] * weight
            part[BACK_ROWS * q + j * CH : BACK_ROWS * q + (j + 1) * CH] = pulled * UNSCALE
        part[BACK_ROWS * q + LOG_ROW : BACK_ROWS * (q + 1)] = jnp.zeros((1, LANES), jnp.float32)


def own_push_kernel(info, own, log_t, logs, ratio, sums, child_b, flat, ratio_b, part, slot_logs):
    lane = lane_ids()
    spread_lanes(ratio_b, ratio[...] * -UNSCALE)

    def clear(q, carry):
        part[q] = jnp.zeros((2 * CH, LANES), jnp.float32)
        return carry

    lax.fori_loop(0, TILES, clear, 0)

    def slot(s, carry):
        start, end = own_steps(info, s)

        def body(qs):
            for q in qs:
                xs, ys = [], []
                for i in range(QUAD):
                    k, dx, dy = kernel_of(own, q, child_b, log_t, QUAD * s + i)
                    weighted = k * ratio_b[QUAD * s + i]
                    xs.append(weighted * dx)
                    ys.append(weighted * dy)
                part[q, 0:CH] = part[q, 0:CH] + ((xs[0] + xs[1]) + (xs[2] + xs[3]))
                part[q, CH : 2 * CH] = part[q, CH : 2 * CH] + ((ys[0] + ys[1]) + (ys[2] + ys[3]))

        steps(start, end, body)
        return carry

    lax.fori_loop(0, SLOTS, slot, 0)

    slot_logs[...] = rows_of_quads(logs[...])
    side = jnp.concatenate([ratio[...], ratio[...]], axis=0) * gather_lanes(sums, slice(CH, 3 * CH)) * UNSCALE
    for s in range(SLOTS):
        at = lax.rem(info[FIRST, s], LANES)
        moved = pltpu.roll(side, lax.rem(at + LANES - QUAD * s, LANES), 1)
        here = (lane >= at) & (lane < at + QUAD)
        at = BACK_ROWS * s
        flat[at : at + 2 * CH] = part[s] + jnp.where(here, moved, 0.0)
        flat[at + LOG_ROW : at + BACK_ROWS] = jnp.where(info[VALID, s] > 0, slot_logs[s : s + 1], 0.0)


def call(kernel, out_rows, scratch, scalars, *operands, mib=8):
    vmem = pl.BlockSpec(memory_space=pltpu.VMEM)
    return pl.pallas_call(
        kernel,
        out_shape=[jax.ShapeDtypeStruct(shape, jnp.float32) for shape in out_rows],
        in_specs=[pl.BlockSpec(memory_space=pltpu.SMEM)] * len(scalars) + [vmem] * len(operands),
        out_specs=[vmem] * len(out_rows),
        scratch_shapes=[pltpu.VMEM(shape, jnp.float32) for shape in scratch],
        compiler_params=pltpu.CompilerParams(vmem_limit_bytes=mib * 2**20),
    )(*scalars, *operands)


TIMES = (TILES, LANES)
XY = (TILES, 2 * CH, LANES)
LOG_T = (LANES, TILES, LANES)
CHILD_B = (LANES, 2 * CH, LANES)
SUMS = (LANES, 3 * CH, LANES)


def pack_kernel(*refs):
    operands, out, source, scratch, arrived, quad_rows = refs[:6], refs[6], refs[7], refs[8:14], refs[14], refs[15]
    copies = [pltpu.make_async_copy(operands[i], scratch[i], arrived.at[i]) for i in range(6)]
    for copy in copies:
        copy.start()
    for copy in copies:
        copy.wait()
    window, live, locations, times, background, weights = scratch
    lane = lane_ids()
    alive = lane < live[0]
    meta = jnp.zeros((1, LANES), jnp.float32)
    for i, number in enumerate((live[0], window[0], window[1])):
        meta = jnp.where(lane == META_LANE + i, number.astype(jnp.float32), meta)
    quad_rows[0:SLOTS] = rows_of_quads(jnp.concatenate([jnp.where(alive, weights[...], 0.0), background[...]], axis=0))
    none = ((lane >= CH * QUAD) & (lane < META_LANE)).astype(jnp.float32)
    quad_rows[SLOTS:] = jnp.broadcast_to(none, (8, LANES))
    xs, ys = locations[:, 0, :] * SCALE, locations[:, 1, :] * SCALE
    time = jnp.where(alive, times[...], DEAD)
    turn = mirrored(lax.axis_index("grp"))
    for to in range(TILES):
        at = ROWS * to
        out[at : at + CH] = xs
        out[at + CH : at + 2 * CH] = ys
        out[at + TIME_ROW : at + TIME_ROW + 1] = time
        quad, valid = quad_at(to ^ turn, live[0], window[0], window[1])
        out[at + QUAD_ROW : at + ROWS] = quad_rows[pl.ds(jnp.where(valid, quad, SLOTS), 1)] + meta
    first, ahead, behind = deal(live[0], window[0], window[1])
    quad = (lane % BLK) // QUAD
    sooner = lane // BLK == first
    valid = quad < jnp.where(sooner, ahead, behind)
    dealt = jnp.where(valid, jnp.where(sooner, quad, quad + ahead) ^ turn, -1)
    source[...] = jnp.broadcast_to(dealt, (8, LANES))


def pack(*operands):
    spaces = [pltpu.SMEM] * 2 + [pltpu.VMEM] * 4
    return pl.pallas_call(
        pack_kernel,
        out_shape=[
            jax.ShapeDtypeStruct((TILES * ROWS, LANES), jnp.float32),
            jax.ShapeDtypeStruct((8, LANES), jnp.int32),
        ],
        in_specs=[pl.BlockSpec(memory_space=pltpu.HBM)] * 6,
        out_specs=[pl.BlockSpec(memory_space=pltpu.VMEM)] * 2,
        scratch_shapes=[space(x.shape, x.dtype) for space, x in zip(spaces, operands)]
        + [pltpu.SemaphoreType.DMA((6,)), pltpu.VMEM((SLOTS + 8, LANES), jnp.float32)],
        compiler_params=pltpu.CompilerParams(vmem_limit_bytes=60 * 2**20),
    )(*operands)


def collect_kernel(dealt, received, grad, logs, log_rows):
    log_rows[...] = jnp.zeros((LANES, LANES), jnp.float32)
    total = jnp.zeros((2 * CH, LANES), jnp.float32)
    for source in range(TILES):
        at = BACK_ROWS * source
        total = total + received[at : at + 2 * CH]
        log_rows[source : source + 1] = received[at + LOG_ROW : at + BACK_ROWS]
    grad[:, 0, :] = total[0:CH]
    grad[:, 1, :] = total[CH:]
    logs[...] = place_quads(log_rows[...], dealt[0:1])[0:CH]


def collect(dealt, received):
    vmem = pl.BlockSpec(memory_space=pltpu.VMEM)
    return pl.pallas_call(
        collect_kernel,
        out_shape=[
            jax.ShapeDtypeStruct((CH, 2, LANES), jnp.float32),
            jax.ShapeDtypeStruct((CH, LANES), jnp.float32),
        ],
        in_specs=[vmem] * 2,
        out_specs=[vmem] * 2,
        scratch_shapes=[pltpu.VMEM((LANES, LANES), jnp.float32)],
        compiler_params=pltpu.CompilerParams(vmem_limit_bytes=24 * 2**20),
    )(dealt, received)


def own_sums(info, flat):
    return call(
        own_sums_kernel,
        [(W_ROW + CH, LANES), SUMS, CHILD_B, (LANES, LANES), XY, LOG_T],
        [TIMES, (LANES, LANES)],
        (info,), flat,
    )


def prev_pairs(info, *operands):
    return call(
        prev_kernel,
        [(TILES * BACK_ROWS, LANES), (CH, LANES), (CH, LANES), SUMS],
        [LOG_T, (LANES, TILES, CH, LANES), SUMS, (TILES, 3 * CH, LANES), TIMES, XY],
        (info,), *operands, mib=42,
    )


def own_push(info, *operands):
    return call(
        own_push_kernel,
        [(TILES * BACK_ROWS, LANES)],
        [(LANES, CH, LANES), XY, (SLOTS, LANES)],
        (info,), *operands,
    )[0]


def plan(meta, me, no_prev):
    live, first_window, second_window = [meta[:, i].astype(jnp.int32) for i in range(3)]
    tile = jnp.arange(TILES, dtype=jnp.int32)
    quad, valid = quad_at(me ^ mirrored(tile), live, first_window, second_window)
    window = jnp.where(quad < BLK // QUAD, first_window, second_window)
    low = jnp.maximum(window * BLK, jnp.where(no_prev, TILES * LANES, 0))
    first = (TILES + tile) * LANES + QUAD * quad
    return jnp.stack([valid.astype(jnp.int32), first, jnp.where(valid, low, 2 * TILES * LANES)])


def per_device(locations, times, background, weights, window_start, live):
    sent, dealt = pack(window_start, live, locations, times[None], background[None], weights)
    own = lax.all_to_all(sent.reshape(TILES, ROWS // 2, 2, LANES), "grp", 0, 0)
    flat = own.reshape(TILES * ROWS, LANES)
    prev = from_behind(flat, "tm", 1)
    meta = own[:, QUAD_ROW // 2, QUAD_ROW % 2, META_LANE : META_LANE + 3]
    info = plan(meta, lax.axis_index("grp").astype(jnp.int32), lax.axis_index("tm") == 0)
    packed, sums, child_b, child_t, tiles, log_t = own_sums(info, flat)
    part_prev, logs, ratio, pulls = prev_pairs(info, prev, packed, sums, child_b, child_t)
    back = from_behind(part_prev, "tm", -1)
    part = own_push(info, tiles, log_t, logs, ratio, pulls, child_b) + back
    received = lax.all_to_all(part.reshape(TILES, BACK_ROWS, 1, LANES), "grp", 0, 0)
    grad, log_intensity = collect(dealt, received.reshape(TILES * BACK_ROWS, LANES))
    return (grad, log_intensity)


def solution(mesh):
    return jax.shard_map(
        per_device,
        mesh=mesh,
        in_specs=(
            P(None, None, ("tm", "grp")),
            P(("tm", "grp")),
            P(("tm", "grp")),
            P(None, ("tm", "grp")),
            P(("tm", "grp")),
            P(("tm", "grp")),
        ),
        out_specs=(P(None, None, ("tm", "grp")), P(None, ("tm", "grp"))),
        check_vma=False,
    )
```

```python
import math

import jax
import jax.numpy as jnp
from jax import lax
from jax.experimental import pallas as pl
from jax.experimental.pallas import tpu as pltpu
from jax.sharding import PartitionSpec as P

offspring = 0.8
fast_rate = 0.125
slow_rate = 0.0009765625

CH = 16
LANES = 128
TILES = 32
BLK = 64
QUAD = 4
SLOTS = 32
DEAD = -1e30

HALF = TILES // 2

TIME_ROW, QUAD_ROW = 2 * CH, 2 * CH + 1
ROWS = 2 * CH + 2
META_LANE = (CH + 1) * QUAD
BACK_ROW, W_ROW = TIME_ROW + 1, 40
VALID, FIRST, LOW = range(3)
LOG_ROW = 2 * CH
BACK_ROWS = LOG_ROW + 1
PLACED = 24

SCALE = math.sqrt(0.5 / math.log(2.0))
UNSCALE = 1.0 / SCALE
LOG2E = 1.0 / math.log(2.0)
LOG2_SLOW = math.log2(offspring * 0.5 * slow_rate / (2.0 * math.pi))


def from_behind(value, axis, by):
    count = lax.axis_size(axis)
    pairs = [(i, i + by) for i in range(count) if 0 <= i + by < count]
    return lax.ppermute(value, axis, pairs)


def log2_time_kernel(delta):
    fast = (fast_rate / slow_rate) * jnp.exp2(delta * (-(fast_rate - slow_rate) * LOG2E))
    return (LOG2_SLOW - delta * (slow_rate * LOG2E)) + jnp.log(1.0 + fast) * LOG2E


def slot_lanes(lane, s):
    return (lane >= QUAD * s) & (lane < QUAD * (s + 1))


def lane_ids():
    return lax.broadcasted_iota(jnp.int32, (1, LANES), 1)


def spread_lanes(out, values):
    rows = values.shape[0]
    for child in range(LANES):
        out[child] = jnp.broadcast_to(values[:, child : child + 1], (rows, LANES))


def gather_lanes(sums):
    lane = lane_ids()
    collected = jnp.zeros(sums.shape[1:], jnp.float32)
    for child in range(LANES):
        collected = jnp.where(lane == child, jnp.sum(sums[child], axis=1, keepdims=True), collected)
    return [collected[j * CH : (j + 1) * CH] for j in range(3)]


def mirrored(tile):
    return ((tile & 1) << 4) | ((tile & 2) << 2) | (tile & 4) | ((tile & 8) >> 2) | ((tile & 16) >> 4)


def deal(live, first_window, second_window):
    quads = [jnp.clip((live - BLK * i + QUAD - 1) // QUAD, 0, BLK // QUAD) for i in range(2)]
    second = (first_window >= second_window).astype(jnp.int32)
    swap = second * (quads[1] - quads[0])
    return second, quads[0] + swap, quads[1] - swap


def quad_at(place, live, first_window, second_window):
    first, ahead, behind = deal(live, first_window, second_window)
    later = (place >= ahead).astype(jnp.int32)
    block = first + later * (1 - 2 * first)
    valid = place < ahead + behind
    return jnp.where(valid, block * (BLK // QUAD) + place - later * ahead, 0), valid


def unpack_tiles(flat, tiles, times_q):
    for q in range(TILES):
        tiles[q] = flat[ROWS * q : ROWS * q + 2 * CH]
        times_q[q : q + 1] = flat[ROWS * q + TIME_ROW : ROWS * q + TIME_ROW + 1]


def time_rows(info, s, log_t, child_t, times_q, own, first, last):
    pos = lax.broadcasted_iota(jnp.int32, (last - first, LANES), 0) * LANES + (first + (TILES if own else 0)) * LANES
    pos = pos + lax.broadcasted_iota(jnp.int32, (last - first, LANES), 1)
    ok = pos >= info[LOW, s]
    for i in range(QUAD):
        at = QUAD * s + i
        delta = jnp.maximum(child_t[pl.ds(at, 1)] - times_q[first:last], 0.0)
        allowed = ok & (pos < info[FIRST, s] + i) if own else ok
        log_t[at, first:last] = jnp.where(allowed, log2_time_kernel(delta), DEAD)


def kernel_of(tiles, q, child_b, log_t, at):
    dx = tiles[q, 0:CH] - child_b[at, 0:CH]
    dy = tiles[q, CH : 2 * CH] - child_b[at, CH : 2 * CH]
    lt = log_t[at, pl.ds(q, 1), :]
    return jnp.exp2((lt - dx * dx) - dy * dy), dx, dy


def short_steps(start, end, body):
    def once(step, carry):
        body([2 * step, 2 * step + 1])
        return carry

    lax.fori_loop(start, end, once, 0)


def steps(start, end, body):
    count = jnp.maximum(end - start, 0)

    def twice(i, carry):
        tile = 2 * start + 4 * i
        body([tile + u for u in range(4)])
        return carry

    lax.fori_loop(0, count // 2, twice, 0)

    @pl.when(count % 2 == 1)
    def _():
        body([2 * end - 2, 2 * end - 1])


def slot_sums(tiles, s, start, end, child_b, log_t, sums, steps, kern=None):
    def body(qs):
        for i in range(QUAD):
            at = QUAD * s + i
            acc = [sums[at, j * CH : (j + 1) * CH] for j in range(3)]
            for q in qs:
                k, dx, dy = kernel_of(tiles, q, child_b, log_t, at)
                if kern is not None:
                    kern[at, q] = k
                acc = [acc[0] + k, acc[1] + k * dx, acc[2] + k * dy]
            for j in range(3):
                sums[at, j * CH : (j + 1) * CH] = acc[j]

    steps(start, end, body)


def own_steps(info, s):
    return jnp.maximum(info[LOW, s] // (2 * LANES) - HALF, 0), info[FIRST, s] // (2 * LANES) - HALF + 1


def prev_start(info, s):
    return jnp.minimum(info[LOW, s] // (2 * LANES), HALF)


def exact_dot(a, b):
    return jnp.dot(a, b, precision=lax.Precision.HIGHEST, preferred_element_type=jnp.float32)


def square():
    return lax.broadcasted_iota(jnp.int32, (LANES, LANES), 0), lax.broadcasted_iota(jnp.int32, (LANES, LANES), 1)


def rows_of_quads(values):
    wide = jnp.concatenate([values, jnp.zeros((LANES - values.shape[0], LANES), jnp.float32)], axis=0)
    row, lane = square()
    by_lane = exact_dot(jnp.transpose(wide), (lane // QUAD == row).astype(jnp.float32))
    by_lane = jnp.where(lane % QUAD == row % QUAD, by_lane, 0.0)
    slot = lax.broadcasted_iota(jnp.int32, (SLOTS, LANES), 0)
    child = lax.broadcasted_iota(jnp.int32, (SLOTS, LANES), 1)
    return exact_dot((child // QUAD == slot).astype(jnp.float32), by_lane)


def place_quads(rows, source):
    row, lane = square()
    chosen = exact_dot(jnp.transpose(rows), (row == source).astype(jnp.float32))
    chosen = jnp.where(row % QUAD == lane % QUAD, chosen, 0.0)
    chain = lax.broadcasted_iota(jnp.int32, (PLACED, LANES), 0)
    place = lax.broadcasted_iota(jnp.int32, (PLACED, LANES), 1)
    return exact_dot((place // QUAD == chain).astype(jnp.float32), chosen)


def own_sums_kernel(info, flat, packed, sums, child_b, child_t, own, log_t, times_q, quad_rows):
    lane = lane_ids()
    unpack_tiles(flat, own, times_q)
    mine = jnp.zeros((2 * CH, LANES), jnp.float32)
    child_times = jnp.zeros((1, LANES), jnp.float32)
    quad_rows[...] = jnp.zeros((LANES, LANES), jnp.float32)
    for s in range(SLOTS):
        shift = lax.rem(QUAD * s + LANES - lax.rem(info[FIRST, s], LANES), LANES)
        mine = jnp.where(slot_lanes(lane, s), pltpu.roll(own[s], shift, 1), mine)
        child_times = jnp.where(slot_lanes(lane, s), pltpu.roll(times_q[s : s + 1], shift, 1), child_times)
        quad_rows[s : s + 1] = flat[ROWS * s + QUAD_ROW : ROWS * s + QUAD_ROW + 1]
    placed = place_quads(quad_rows[...], lane // QUAD)
    packed[0 : 2 * CH] = mine
    packed[TIME_ROW : TIME_ROW + 1] = child_times
    packed[BACK_ROW : BACK_ROW + 1] = placed[CH : CH + 1]
    packed[W_ROW:] = placed[0:CH]
    spread_lanes(child_b, mine)
    child_t[...] = jnp.transpose(jnp.broadcast_to(child_times, (LANES, LANES)))

    for begin, last in ((0, HALF), (HALF, TILES)):

        def times(s, carry, last=last):
            @pl.when(info[VALID, s] > 0)
            def _():
                time_rows(info, s, log_t, child_t, times_q, True, 0, last)

            return carry

        lax.fori_loop(begin, begin + HALF, times, 0)

    def clear(s, carry):
        for i in range(QUAD):
            sums[QUAD * s + i] = jnp.zeros((3 * CH, LANES), jnp.float32)
        return carry

    lax.fori_loop(0, SLOTS, clear, 0)

    def slot(s, carry):
        start, end = own_steps(info, s)
        slot_sums(own, s, start, end, child_b, log_t, sums, steps)
        return carry

    lax.fori_loop(0, SLOTS, slot, 0)


def prev_kernel(
    info, flat, packed, own_sums, child_b, child_t, part, result, ratio_out,
    log_t, kern, sums, total, times_q, prev
):
    unpack_tiles(flat, prev, times_q)

    for begin in (0, HALF):

        def times(s, carry, first=begin):
            @pl.when(info[LOW, s] < TILES * LANES)
            def _():
                time_rows(info, s, log_t, child_t, times_q, False, first, TILES)

            return carry

        lax.fori_loop(begin, begin + HALF, times, 0)

    def slot(s, carry):
        for i in range(QUAD):
            sums[QUAD * s + i] = own_sums[QUAD * s + i]
        slot_sums(prev, s, prev_start(info, s), HALF, child_b, log_t, sums, short_steps, kern)
        return carry

    lax.fori_loop(0, SLOTS, slot, 0)

    summed, pull_x, pull_y = gather_lanes(sums)
    xs, ys, weights = packed[0:CH], packed[CH : 2 * CH], packed[W_ROW : W_ROW + CH]
    intensity = packed[BACK_ROW : BACK_ROW + 1] + summed
    alive = packed[TIME_ROW : TIME_ROW + 1] >= 0.0
    ratio = weights / intensity
    ratio_out[...] = ratio
    result[0:CH] = ratio * pull_x * UNSCALE
    result[CH : 2 * CH] = ratio * pull_y * UNSCALE
    result[2 * CH :] = jnp.where(alive, jnp.log(intensity), 0.0)
    spread_lanes(sums, jnp.concatenate([ratio, ratio * xs, ratio * ys], axis=0))

    def clear(q, carry):
        total[q] = jnp.zeros((3 * CH, LANES), jnp.float32)
        return carry

    lax.fori_loop(0, TILES, clear, 0)

    def push(s, carry):
        def body(qs):
            for q in qs:
                ks = [kern[QUAD * s + i, q] for i in range(QUAD)]
                for j in range(3):
                    at = slice(j * CH, (j + 1) * CH)
                    add = [ks[i] * sums[QUAD * s + i, at] for i in range(QUAD)]
                    total[q, at] = total[q, at] + ((add[0] + add[1]) + (add[2] + add[3]))

        short_steps(prev_start(info, s), HALF, body)
        return carry

    lax.fori_loop(0, SLOTS, push, 0)

    for q in range(TILES):
        weight = total[q, 0:CH]
        for j in range(2):
            pulled = total[q, (j + 1) * CH : (j + 2) * CH] - prev[q, j * CH : (j + 1) * CH] * weight
            part[BACK_ROWS * q + j * CH : BACK_ROWS * q + (j + 1) * CH] = pulled * UNSCALE
        part[BACK_ROWS * q + LOG_ROW : BACK_ROWS * (q + 1)] = jnp.zeros((1, LANES), jnp.float32)


def own_push_kernel(info, own, log_t, result, ratio, child_b, flat, ratio_b, part, slot_logs):
    lane = lane_ids()
    spread_lanes(ratio_b, ratio[...] * -UNSCALE)

    def clear(q, carry):
        part[q] = jnp.zeros((2 * CH, LANES), jnp.float32)
        return carry

    lax.fori_loop(0, TILES, clear, 0)

    def slot(s, carry):
        start, end = own_steps(info, s)

        def body(qs):
            for q in qs:
                xs, ys = [], []
                for i in range(QUAD):
                    k, dx, dy = kernel_of(own, q, child_b, log_t, QUAD * s + i)
                    weighted = k * ratio_b[QUAD * s + i]
                    xs.append(weighted * dx)
                    ys.append(weighted * dy)
                part[q, 0:CH] = part[q, 0:CH] + ((xs[0] + xs[1]) + (xs[2] + xs[3]))
                part[q, CH : 2 * CH] = part[q, CH : 2 * CH] + ((ys[0] + ys[1]) + (ys[2] + ys[3]))

        steps(start, end, body)
        return carry

    lax.fori_loop(0, SLOTS, slot, 0)

    slot_logs[...] = rows_of_quads(result[2 * CH :])
    for s in range(SLOTS):
        at = lax.rem(info[FIRST, s], LANES)
        moved = pltpu.roll(result[0 : 2 * CH], lax.rem(at + LANES - QUAD * s, LANES), 1)
        here = (lane >= at) & (lane < at + QUAD)
        at = BACK_ROWS * s
        flat[at : at + 2 * CH] = part[s] + jnp.where(here, moved, 0.0)
        flat[at + LOG_ROW : at + BACK_ROWS] = jnp.where(info[VALID, s] > 0, slot_logs[s : s + 1], 0.0)


def call(kernel, out_rows, scratch, scalars, *operands, mib=8):
    vmem = pl.BlockSpec(memory_space=pltpu.VMEM)
    return pl.pallas_call(
        kernel,
        out_shape=[jax.ShapeDtypeStruct(shape, jnp.float32) for shape in out_rows],
        in_specs=[pl.BlockSpec(memory_space=pltpu.SMEM)] * len(scalars) + [vmem] * len(operands),
        out_specs=[vmem] * len(out_rows),
        scratch_shapes=[pltpu.VMEM(shape, jnp.float32) for shape in scratch],
        compiler_params=pltpu.CompilerParams(vmem_limit_bytes=mib * 2**20),
    )(*scalars, *operands)


TIMES = (TILES, LANES)
XY = (TILES, 2 * CH, LANES)
LOG_T = (LANES, TILES, LANES)
CHILD_B = (LANES, 2 * CH, LANES)
SUMS = (LANES, 3 * CH, LANES)


def pack_kernel(*refs):
    operands, out, source, scratch, arrived, quad_rows = refs[:6], refs[6], refs[7], refs[8:14], refs[14], refs[15]
    copies = [pltpu.make_async_copy(operands[i], scratch[i], arrived.at[i]) for i in range(6)]
    for copy in copies:
        copy.start()
    for copy in copies:
        copy.wait()
    window, live, locations, times, background, weights = scratch
    lane = lane_ids()
    alive = lane < live[0]
    meta = jnp.zeros((1, LANES), jnp.float32)
    for i, number in enumerate((live[0], window[0], window[1])):
        meta = jnp.where(lane == META_LANE + i, number.astype(jnp.float32), meta)
    quad_rows[0:SLOTS] = rows_of_quads(jnp.concatenate([jnp.where(alive, weights[...], 0.0), background[...]], axis=0))
    none = ((lane >= CH * QUAD) & (lane < META_LANE)).astype(jnp.float32)
    quad_rows[SLOTS:] = jnp.broadcast_to(none, (8, LANES))
    xs, ys = locations[:, 0, :] * SCALE, locations[:, 1, :] * SCALE
    time = jnp.where(alive, times[...], DEAD)
    turn = mirrored(lax.axis_index("grp"))
    for to in range(TILES):
        at = ROWS * to
        out[at : at + CH] = xs
        out[at + CH : at + 2 * CH] = ys
        out[at + TIME_ROW : at + TIME_ROW + 1] = time
        quad, valid = quad_at(to ^ turn, live[0], window[0], window[1])
        out[at + QUAD_ROW : at + ROWS] = quad_rows[pl.ds(jnp.where(valid, quad, SLOTS), 1)] + meta
    first, ahead, behind = deal(live[0], window[0], window[1])
    quad = (lane % BLK) // QUAD
    sooner = lane // BLK == first
    valid = quad < jnp.where(sooner, ahead, behind)
    dealt = jnp.where(valid, jnp.where(sooner, quad, quad + ahead) ^ turn, -1)
    source[...] = jnp.broadcast_to(dealt, (8, LANES))


def pack(*operands):
    spaces = [pltpu.SMEM] * 2 + [pltpu.VMEM] * 4
    return pl.pallas_call(
        pack_kernel,
        out_shape=[
            jax.ShapeDtypeStruct((TILES * ROWS, LANES), jnp.float32),
            jax.ShapeDtypeStruct((8, LANES), jnp.int32),
        ],
        in_specs=[pl.BlockSpec(memory_space=pltpu.HBM)] * 6,
        out_specs=[pl.BlockSpec(memory_space=pltpu.VMEM)] * 2,
        scratch_shapes=[space(x.shape, x.dtype) for space, x in zip(spaces, operands)]
        + [pltpu.SemaphoreType.DMA((6,)), pltpu.VMEM((SLOTS + 8, LANES), jnp.float32)],
        compiler_params=pltpu.CompilerParams(vmem_limit_bytes=60 * 2**20),
    )(*operands)


def collect_kernel(dealt, received, grad, logs, log_rows):
    log_rows[...] = jnp.zeros((LANES, LANES), jnp.float32)
    total = jnp.zeros((2 * CH, LANES), jnp.float32)
    for source in range(TILES):
        at = BACK_ROWS * source
        total = total + received[at : at + 2 * CH]
        log_rows[source : source + 1] = received[at + LOG_ROW : at + BACK_ROWS]
    grad[:, 0, :] = total[0:CH]
    grad[:, 1, :] = total[CH:]
    logs[...] = place_quads(log_rows[...], dealt[0:1])[0:CH]


def collect(dealt, received):
    vmem = pl.BlockSpec(memory_space=pltpu.VMEM)
    return pl.pallas_call(
        collect_kernel,
        out_shape=[
            jax.ShapeDtypeStruct((CH, 2, LANES), jnp.float32),
            jax.ShapeDtypeStruct((CH, LANES), jnp.float32),
        ],
        in_specs=[vmem] * 2,
        out_specs=[vmem] * 2,
        scratch_shapes=[pltpu.VMEM((LANES, LANES), jnp.float32)],
        compiler_params=pltpu.CompilerParams(vmem_limit_bytes=24 * 2**20),
    )(dealt, received)


def own_sums(info, flat):
    return call(
        own_sums_kernel,
        [(W_ROW + CH, LANES), SUMS, CHILD_B, (LANES, LANES), XY, LOG_T],
        [TIMES, (LANES, LANES)],
        (info,), flat,
    )


def prev_pairs(info, *operands):
    return call(
        prev_kernel,
        [(TILES * BACK_ROWS, LANES), (3 * CH, LANES), (CH, LANES)],
        [LOG_T, (LANES, TILES, CH, LANES), SUMS, (TILES, 3 * CH, LANES), TIMES, XY],
        (info,), *operands, mib=42,
    )


def own_push(info, *operands):
    return call(
        own_push_kernel,
        [(TILES * BACK_ROWS, LANES)],
        [(LANES, CH, LANES), XY, (SLOTS, LANES)],
        (info,), *operands,
    )[0]


def plan(meta, me, no_prev):
    live, first_window, second_window = [meta[:, i].astype(jnp.int32) for i in range(3)]
    tile = jnp.arange(TILES, dtype=jnp.int32)
    quad, valid = quad_at(me ^ mirrored(tile), live, first_window, second_window)
    window = jnp.where(quad < BLK // QUAD, first_window, second_window)
    low = jnp.maximum(window * BLK, jnp.where(no_prev, TILES * LANES, 0))
    first = (TILES + tile) * LANES + QUAD * quad
    return jnp.stack([valid.astype(jnp.int32), first, jnp.where(valid, low, 2 * TILES * LANES)])


def per_device(locations, times, background, weights, window_start, live):
    sent, dealt = pack(window_start, live, locations, times[None], background[None], weights)
    own = lax.all_to_all(sent.reshape(TILES, ROWS // 2, 2, LANES), "grp", 0, 0)
    flat = own.reshape(TILES * ROWS, LANES)
    prev = from_behind(flat, "tm", 1)
    meta = own[:, QUAD_ROW // 2, QUAD_ROW % 2, META_LANE : META_LANE + 3]
    info = plan(meta, lax.axis_index("grp").astype(jnp.int32), lax.axis_index("tm") == 0)
    packed, sums, child_b, child_t, tiles, log_t = own_sums(info, flat)
    part_prev, result, ratio = prev_pairs(info, prev, packed, sums, child_b, child_t)
    back = from_behind(part_prev, "tm", -1)
    part = own_push(info, tiles, log_t, result, ratio, child_b) + back
    received = lax.all_to_all(part.reshape(TILES, BACK_ROWS, 1, LANES), "grp", 0, 0)
    grad, log_intensity = collect(dealt, received.reshape(TILES * BACK_ROWS, LANES))
    return (grad, log_intensity)


def solution(mesh):
    return jax.shard_map(
        per_device,
        mesh=mesh,
        in_specs=(
            P(None, None, ("tm", "grp")),
            P(("tm", "grp")),
            P(("tm", "grp")),
            P(None, ("tm", "grp")),
            P(("tm", "grp")),
            P(("tm", "grp")),
        ),
        out_specs=(P(None, None, ("tm", "grp")), P(None, ("tm", "grp"))),
        check_vma=False,
    )
```
